32 devices in a mesh: layer: 4 (over z), row: 2 (over y), col: 4 (over x, core).
Axes of the slice: x: 2, y: 2, z: 4, core: 2. Of those that a mesh axis runs over, the one named last changes fastest.
Arguments:
- sources: bfloat16 [4, 64, 4, 16, 128], P('layer', None, 'row', 'col'), may hold values from -3 to 3
- adjoint_sources: bfloat16 [4, 64, 4, 16, 128], P('layer', None, 'row', 'col'), may hold values from -3 to 3
- blocks: bfloat16 [4, 4, 16, 9, 128, 128], P('layer', 'row', 'col'), may hold values from -0.2 to 1.4
- pattern: int32 [4, 4, 16, 9], P('layer', 'row', 'col'), may hold values 0 or 1
- coupling: float32 [4], replicated, may hold values from 0.7 to 0.9
- layer_group: int32 [4], replicated, may hold values from 0 to 3
- port_cells: int32 [64], replicated, may hold values from 0 to 8191
Outputs:
- forward_field: bfloat16 [4, 64, 4, 16, 128], P('layer', None, 'row', 'col')
- adjoint_field: bfloat16 [4, 64, 4, 16, 128], P('layer', None, 'row', 'col')
- gradient: float32 [4, 4, 16, 128], P(None, 'row', 'col')
The draws below stay inside these ranges and needn't reach their ends.
All inputs are finite; a program needn't handle non-finite values. No bound on the sum of `pattern` on one device may be relied on, other than what follows from the above.
Results may differ from the reference program's by a relative error of at most 0.01.
Values may be sent and summed in bfloat16 or wider, within the bound.
No kernel may reach another device: no remote copies, remote signals or barrier semaphores. Data moves between devices by JAX's collectives and lax.ppermute only.
A program may use at most 64 MiB of HBM per device.

```python
import math
import jax
import jax.numpy as jnp
from jax import lax

TILE = 128
PORTS = 64
NG = 4
L = 4
NTX = 4
NTY = 16
F = 8192


def draw_blocks(key, part):
    full_shape = (L, NTX, NTY, 9, TILE, TILE)
    spread = 0.3 / math.sqrt(6.0 * TILE)
    random_part = jax.random.normal(key, full_shape, jnp.float32) * spread
    center = (jnp.arange(9) == 4).astype(jnp.float32)[:, None, None] * jnp.eye(TILE, dtype=jnp.float32)[None] * 1.25
    return (random_part + center[None, None, None]).astype(jnp.bfloat16)


def touch_ends(entries, key, least, top_value):
    longest = entries.shape.index(max(entries.shape))
    spots = []
    for shift in (0, 1):
        where = [jax.random.randint(jax.random.fold_in(key, axis), (), 0, length) for axis, length in enumerate(entries.shape)]
        where[longest] = (where[longest] + shift) % entries.shape[longest]
        spots.append(tuple(where))
    return entries.at[spots[0]].set(least).at[spots[1]].set(top_value)


def block_levels(stream_key, shape, split, least, largest):
    loudness, own = 1.0, jax.random.fold_in(stream_key, 6)
    for dim, shards_of in split:
        heights = jnp.exp(jax.random.uniform(jax.random.fold_in(own, dim), (shards_of,), jnp.float32, least / len(split), largest / len(split)))
        loudness = loudness * jnp.repeat(heights, shape[dim] // shards_of).reshape([-1 if axis == dim else 1 for axis in range(len(shape))])
    return loudness


def normal_values(own_key, shape, deviation, most, split=(), kind=jnp.bfloat16):
    entries = jax.random.normal(own_key, shape, jnp.float32) * deviation
    if len(split) > 0:
        entries = block_levels(own_key, shape, split, -0.22, 0.18) * entries
    return jnp.clip(entries, min=-most, max=most).astype(kind)


def setup_inputs(seed: int = 0) -> dict:
    seeds = jax.random.split(jax.random.key(seed), 8)
    sources = normal_values(seeds[0], (L, PORTS, NTX, NTY, TILE), 0.5, 3.0, ((0, 4), (2, 2), (3, 4)))
    adjoint_sources = normal_values(seeds[1], (L, PORTS, NTX, NTY, TILE), 0.5, 3.0, ((0, 4), (2, 2), (3, 4)))
    blocks = draw_blocks(jax.random.fold_in(seeds[7], 71), 0)
    pattern = touch_ends((jax.random.randint(seeds[3], (L, NTX, NTY, 9), 0, 3) < 2).astype(jnp.int32), jax.random.fold_in(seeds[3], 1), 0, 1)
    coupling = jnp.clip(jax.random.uniform(seeds[4], (NG,), jnp.float32, 0.7, 0.9), 0.7, 0.9)
    layer_group = touch_ends(jax.random.randint(seeds[5], (L,), 0, NG), jax.random.fold_in(seeds[5], 1), 0, NG - 1).astype(jnp.int32)
    port_cells = touch_ends(jax.random.randint(seeds[6], (PORTS,), 0, F), jax.random.fold_in(seeds[6], 1), 0, F - 1).astype(jnp.int32)
    return {"sources": sources, "adjoint_sources": adjoint_sources, "blocks": blocks, "pattern": pattern, "coupling": coupling, "layer_group": layer_group, "port_cells": port_cells}


port_strength = 4.0
intersection_scale = 0.125


def apply_front(wave, front_blocks, front_mask):
    padded = jnp.pad(wave.astype(jnp.float32), ((0, 0), (1, 1), (1, 1), (0, 0)))
    summed = jnp.zeros(wave.shape, jnp.float32)
    for offset in range(9):
        step_x = offset // 3 - 1
        step_y = offset % 3 - 1
        beside = padded[:, 1 + step_x:1 + step_x + NTX, 1 + step_y:1 + step_y + NTY, :]
        product_term = jnp.einsum("pijc,ijcd->pijd", beside, front_blocks[:, :, offset].astype(jnp.float32), precision=lax.Precision.HIGHEST)
        summed = summed + front_mask[None, :, :, offset, None].astype(jnp.float32) * product_term
    return summed


def reference(sources, adjoint_sources, blocks, pattern, coupling, layer_group, port_cells):
    member = (layer_group[:, None] == jnp.arange(NG, dtype=jnp.int32)[None, :]).astype(jnp.float32)
    kappa = jnp.dot(member, coupling, precision=lax.Precision.HIGHEST)
    kappa_next = jnp.concatenate([kappa[1:], jnp.zeros((1,), jnp.float32)])
    cell_ids = jnp.arange(NTX * NTY * TILE, dtype=jnp.int32).reshape(NTX, NTY, TILE)
    port_map = (cell_ids[None] == port_cells[:, None, None, None]).astype(jnp.float32) * port_strength
    layer_ids = jnp.arange(L, dtype=jnp.int32)
    first_flag = (layer_ids == 0).astype(jnp.float32)
    last_flag = (layer_ids == L - 1).astype(jnp.float32)

    def sweep_step(previous, inputs):
        source_layer, front_blocks, front_mask, strength, flag_value = inputs
        wave = (source_layer.astype(jnp.float32) + flag_value * port_map + strength * previous.astype(jnp.float32)).astype(jnp.bfloat16)
        result = apply_front(wave, front_blocks, front_mask).astype(jnp.bfloat16)
        return result, result

    empty = jnp.zeros((PORTS, NTX, NTY, TILE), jnp.bfloat16)
    _, forward_field = lax.scan(sweep_step, empty, (sources, blocks, pattern, kappa, first_flag))
    _, adjoint_field = lax.scan(sweep_step, empty, (adjoint_sources, blocks, pattern, kappa_next, last_flag), reverse=True)
    intersection = jnp.sum(forward_field.astype(jnp.float32) * adjoint_field.astype(jnp.float32), axis=1) * intersection_scale
    gradient = jnp.einsum("lg,lxyc->gxyc", member, intersection, precision=lax.Precision.HIGHEST)
    return forward_field, adjoint_field, gradient
```

```python
import functools

import jax
import jax.numpy as jnp
from jax import lax
from jax.experimental import pallas as pl
from jax.experimental.pallas import tpu as pltpu
from jax.sharding import PartitionSpec as P

port_strength = 4.0
intersection_scale = 0.125
AXES = ("layer", "row", "col")
OFFSETS = 9
VMEM_BYTES = 24 * 1024 * 1024

VM = pl.BlockSpec(memory_space=pltpu.VMEM)
SM = pl.BlockSpec(memory_space=pltpu.SMEM)


def call(kernel, outs, *args, smem=0, scratch=(), aliases=None):
    return pl.pallas_call(
        kernel,
        out_shape=[jax.ShapeDtypeStruct(shape, dtype) for shape, dtype in outs],
        in_specs=[SM] * smem + [VM] * (len(args) - smem),
        out_specs=[VM] * len(outs),
        scratch_shapes=list(scratch),
        input_output_aliases=aliases or {},
        compiler_params=pltpu.CompilerParams(vmem_limit_bytes=VMEM_BYTES),
    )(*args)


def near(i, n):
    return i ^ 1


def far(i, n):
    return (((i + 1) ^ 1) - 1) % n


def pairings(n):
    return [near] if n == 2 else [near, far]


class Side:
    def __init__(self, pairing, axis, tiles):
        pos, count = lax.axis_index(axis), lax.axis_size(axis)
        even = lax.rem(pos, 2) == 0
        after = even if pairing is near else jnp.logical_not(even)
        self.step = jnp.where(after, 1, -1)
        self.edge = jnp.where(after, tiles - 1, 0)
        self.real = None
        if pairing is far:
            self.real = jnp.logical_not(
                jnp.logical_or(jnp.logical_and(after, pos == count - 1), jnp.logical_and(jnp.logical_not(after), pos == 0))
            )

    def when(self, body):
        if self.real is None:
            body()
        else:
            pl.when(self.real)(body)


def local(sources, adjoint_sources, blocks, pattern, coupling, layer_group, port_cells):
    ports, tiles_x, tiles_y, cells = sources.shape[1:]
    tiles = tiles_x * tiles_y
    groups = coupling.shape[0]
    layers, rows, cols = (lax.axis_size(axis) for axis in AXES)
    row_pairs, col_pairs = pairings(rows), pairings(cols)
    ext = tiles_x + len(row_pairs)
    bf16, f32 = jnp.bfloat16, jnp.float32

    def route(of_layer=None, of_row=None, of_col=None):
        pairs = []
        for l in range(layers):
            for r in range(rows):
                for c in range(cols):
                    a = of_layer(l) if of_layer else l
                    b = of_row(r, rows) if of_row else r
                    d = of_col(c, cols) if of_col else c
                    pairs.append(((l * rows + r) * cols + c, (a * rows + b) * cols + d))
        return pairs

    def swapped(array, **where):
        return lax.ppermute(array, AXES, route(**where))

    def is_active(step):
        pos = lax.axis_index("layer")
        return jnp.logical_or(pos == step, pos == layers - 1 - step)

    def sweep_of(step):
        return jnp.where(lax.axis_index("layer") == step, 0, 1)

    def port_map(cells_ref, x, y):
        x_pos = lax.axis_index("row") * tiles_x + x
        y_pos = lax.axis_index("col") * tiles_y + y
        first = (x_pos * (tiles_y * cols) + y_pos) * cells
        row = jnp.broadcast_to(cells_ref[...], (ports, ports))
        diagonal = lax.broadcasted_iota(jnp.int32, (ports, ports), 0) == lax.broadcasted_iota(
            jnp.int32, (ports, ports), 1
        )
        column = jnp.sum(jnp.where(diagonal, row, 0), axis=1, keepdims=True)
        lane = lax.broadcasted_iota(jnp.int32, (ports, cells), 1)
        return jnp.where(column - first == lane, port_strength, 0.0).astype(f32)

    def source_tile(flat_ref, cells_ref, sweep, x, y):
        tile = flat_ref[sweep, pl.ds(x * tiles_y + y, ports, stride=tiles), :]
        pos = lax.axis_index("layer")
        end = pos == (0 if sweep == 0 else layers - 1)
        return (tile + jnp.where(end, port_map(cells_ref, x, y), 0.0)).astype(bf16)

    def rims_kernel(forward_ref, adjoint_ref, cells_ref, flat_ref, *rim_refs):
        flat_ref[0] = forward_ref[...].astype(f32).reshape(ports * tiles, cells)
        flat_ref[1] = adjoint_ref[...].astype(f32).reshape(ports * tiles, cells)
        for pairing, rim_ref in zip(row_pairs, rim_refs):
            side = Side(pairing, "row", tiles_x)
            for sweep in range(2):
                for y in range(tiles_y):
                    rim_ref[sweep, y] = source_tile(flat_ref, cells_ref, sweep, side.edge, y)

    port_row = port_cells.reshape(1, ports)
    flat, *rims = call(
        rims_kernel,
        [((2, ports * tiles, cells), f32)] + [((2, tiles_y, ports, cells), bf16)] * len(row_pairs),
        sources.reshape(ports, tiles, cells),
        adjoint_sources.reshape(ports, tiles, cells),
        port_row,
    )
    source_rims = [swapped(rim, of_row=pairing) for rim, pairing in zip(rims, row_pairs)]

    def setup_kernel(pattern_ref, coupling_ref, group_ref, flat_ref, cells_ref, blocks_ref, source_ref, front_ref, kappa_ref, member_ref):
        for sweep in range(2):
            for x in range(tiles_x):
                for y in range(tiles_y):
                    source_ref[sweep, x * tiles_y + y] = source_tile(flat_ref, cells_ref, sweep, x, y)

        def mask_block(index, carry):
            for offset in range(OFFSETS):
                present = pattern_ref[index, offset] > 0
                front_ref[index, offset] = jnp.where(present, blocks_ref[index, offset], jnp.zeros((cells, cells), bf16))
            return carry

        lax.fori_loop(0, tiles, mask_block, 0)
        pos = lax.axis_index("layer")
        own = coupling_ref[group_ref[pos]]
        following = coupling_ref[group_ref[jnp.minimum(pos + 1, layers - 1)]]
        kappa_ref[0] = jnp.full((8, cells), own, f32)
        kappa_ref[1] = jnp.full((8, cells), following, f32)
        for g in range(groups):
            for l in range(layers):
                member_ref[g, l] = jnp.full((tiles, cells), jnp.where(group_ref[l] == g, 1.0, 0.0), f32)

    source, front, kappa, member = call(
        setup_kernel,
        [
            ((2, tiles, ports, cells), bf16),
            ((tiles, OFFSETS, cells, cells), bf16),
            ((2, 8, cells), f32),
            ((groups, layers, tiles, cells), f32),
        ],
        pattern.reshape(tiles, OFFSETS),
        coupling,
        layer_group,
        flat,
        port_row,
        blocks.reshape(tiles, OFFSETS, cells, cells),
        smem=3,
    )

    def wave_kernel(step, *refs):
        source_ref, kappa_ref = refs[:2]
        refs = refs[2:]
        halo_refs, refs = refs[: len(row_pairs)], refs[len(row_pairs) :]
        if step > 0:
            field_ref, refs = refs[0], refs[1:]
            field_rims, refs = refs[: len(row_pairs)], refs[len(row_pairs) :]
        wave_ref, rim_refs = refs[0], refs[1:]

        @pl.when(is_active(step))
        def _():
            sweep = sweep_of(step)

            def wave(base, field):
                if step == 0:
                    return base
                factor = kappa_ref[sweep, 0:1, :]
                return (base.astype(f32) + factor * field.astype(f32)).astype(bf16)

            for x in range(tiles_x):
                for y in range(tiles_y):
                    t = x * tiles_y + y
                    wave_ref[x, y] = wave(source_ref[sweep, t], field_ref[t] if step > 0 else None)
            for h, pairing in enumerate(row_pairs):
                side = Side(pairing, "row", tiles_x)
                for y in range(tiles_y):
                    value = wave(halo_refs[h][sweep, y], field_rims[h][y] if step > 0 else None)
                    if side.real is not None:
                        value = jnp.where(side.real, value, jnp.zeros_like(value))
                    wave_ref[tiles_x + h, y] = value
            for pairing, rim_ref in zip(col_pairs, rim_refs):
                edge = Side(pairing, "col", tiles_y).edge
                for x in range(ext):
                    rim_ref[x] = wave_ref[x, edge]

    def product(lhs, rhs):
        return jnp.dot(lhs, rhs, preferred_element_type=f32)

    def inner_kernel(step, wave_ref, front_ref, sum_ref):
        @pl.when(is_active(step))
        def _():
            for y in range(tiles_y):
                low, high = max(y - 1, 0), min(y + 1, tiles_y - 1)
                width = high - low + 1
                first = low - y + 1
                beside = [
                    jnp.concatenate([wave_ref[x, j] for j in range(low, high + 1)], axis=1) for x in range(ext)
                ]
                for x in range(tiles_x):
                    reach = [a for a in (-1, 0, 1) if 0 <= x + a < tiles_x]
                    lhs = jnp.concatenate([beside[x + a] for a in reach], axis=1)
                    rhs = jnp.concatenate(
                        [
                            front_ref[x * tiles_y + y, 3 * (a + 1) + first : 3 * (a + 1) + first + width].reshape(
                                width * cells, cells
                            )
                            for a in reach
                        ],
                        axis=0,
                    )
                    sum_ref[x * tiles_y + y] = product(lhs, rhs)
                for h, pairing in enumerate(row_pairs):
                    side = Side(pairing, "row", tiles_x)
                    t = side.edge * tiles_y + y
                    rhs = front_ref[t, pl.ds(3 * (side.step + 1) + first, width)].reshape(width * cells, cells)
                    sum_ref[t] += product(beside[tiles_x + h], rhs)

    def outer_kernel(step, *refs):
        front_ref = refs[1]
        halo_refs, refs = refs[2 : 2 + len(col_pairs)], refs[2 + len(col_pairs) :]
        if step == layers - 1:
            earlier, refs = refs[: layers - 1], refs[layers - 1 :]
        sum_ref, field_ref, refs = refs[0], refs[1], refs[2:]

        @pl.when(is_active(step))
        def _():
            for pairing, halo_ref in zip(col_pairs, halo_refs):
                across = Side(pairing, "col", tiles_y)

                def add(across=across, halo_ref=halo_ref):
                    for x in range(tiles_x):
                        t = x * tiles_y + across.edge
                        reach = [a for a in (-1, 0, 1) if 0 <= x + a < tiles_x]
                        lhs = jnp.concatenate([halo_ref[x + a] for a in reach], axis=1)
                        rhs = jnp.concatenate([front_ref[t, 3 * (a + 1) + 1 + across.step] for a in reach], axis=0)
                        sum_ref[t] += product(lhs, rhs)
                    for h, row_pairing in enumerate(row_pairs):
                        side = Side(row_pairing, "row", tiles_x)
                        t = side.edge * tiles_y + across.edge
                        sum_ref[t] += product(halo_ref[tiles_x + h], front_ref[t, 3 * (side.step + 1) + 1 + across.step])

                across.when(add)
            for t in range(tiles):
                field_ref[t] = sum_ref[t].astype(bf16)
            if step < layers - 1:
                for pairing, rim_ref in zip(row_pairs, refs):
                    edge = Side(pairing, "row", tiles_x).edge
                    rim_ref[...] = field_ref[pl.ds(edge * tiles_y, tiles_y)]

        if step == layers - 1:
            pos = lax.axis_index("layer")
            first = jnp.minimum(pos, layers - 1 - pos)
            for k in range(layers // 2):

                @pl.when(first == k)
                def _(k=k):
                    one, other = earlier[k], field_ref if k == 0 else earlier[layers - 1 - k]
                    for t in range(tiles):
                        both = one[t].astype(f32) * other[t].astype(f32)
                        refs[0][t : t + 1, :] = jnp.sum(both, axis=0, keepdims=True) * intersection_scale

    fields, received, received_rims = [], None, []
    for step in range(layers):
        wave, *rims = call(
            functools.partial(wave_kernel, step),
            [((ext, tiles_y, ports, cells), bf16)] + [((ext, ports, cells), bf16)] * len(col_pairs),
            source,
            kappa,
            *source_rims,
            *([received, *received_rims] if step > 0 else []),
        )
        halos = [swapped(rim, of_col=pairing) for rim, pairing in zip(rims, col_pairs)]
        (summed,) = call(
            functools.partial(inner_kernel, step), [((tiles, ports, cells), f32)], wave, front
        )
        last = step == layers - 1
        _, field, *extra = call(
            functools.partial(outer_kernel, step),
            [((tiles, ports, cells), f32), ((tiles, ports, cells), bf16)]
            + ([((tiles, cells), f32)] if last else [((tiles_y, ports, cells), bf16)] * len(row_pairs)),
            summed,
            front,
            *halos,
            *(fields if last else []),
            aliases={0: 0},
        )
        fields.append(field)
        if not last:
            partner = lambda l: l ^ 1 if step % 2 == 0 else (((l + 1) ^ 1) - 1) % layers
            received = swapped(field, of_layer=partner)
            received_rims = [
                swapped(rim, of_layer=partner, of_row=pairing) for rim, pairing in zip(extra, row_pairs)
            ]
    intersection = extra[0]

    def fields_kernel(*refs):
        field_refs, (forward_ref, adjoint_ref, flat_ref) = refs[:layers], refs[layers:]
        pos = lax.axis_index("layer")
        for out_ref, active in ((forward_ref, lambda s: s), (adjoint_ref, lambda s: layers - 1 - s)):
            for step in range(layers):

                @pl.when(pos == active(step))
                def _(step=step):
                    for t in range(tiles):
                        flat_ref[pl.ds(t, ports, stride=tiles), :] = field_refs[step][t].astype(f32)

            out_ref[...] = flat_ref[...].reshape(ports, tiles, cells).astype(bf16)

    forward, adjoint = call(
        fields_kernel,
        [((ports, tiles, cells), bf16)] * 2,
        *fields,
        scratch=[pltpu.VMEM((ports * tiles, cells), f32)],
    )

    if layers == 4:
        parts = [intersection] + [swapped(intersection, of_layer=lambda l, m=m: l ^ m) for m in range(1, layers)]

        def gradient_kernel(*refs):
            part_refs, member_ref, out_ref = refs[:layers], refs[layers], refs[layers + 1]
            pos = lax.axis_index("layer")
            for g in range(groups):
                total = jnp.zeros((tiles, cells), f32)
                for m in range(layers):
                    total = total + member_ref[g, pos ^ m] * part_refs[m][...]
                for x in range(tiles_x):
                    out_ref[g, x] = total[x * tiles_y : (x + 1) * tiles_y]

        (gradient,) = call(
            gradient_kernel, [((groups, tiles_x, tiles_y, cells), f32)], *parts, member
        )
    else:
        selected = lax.dynamic_index_in_dim(member, lax.axis_index("layer"), 1, keepdims=False)
        gradient = lax.psum(selected * intersection[None], "layer").reshape(groups, tiles_x, tiles_y, cells)
    shape = (1, ports, tiles_x, tiles_y, cells)
    return (forward.reshape(shape), adjoint.reshape(shape), gradient)


def solution(mesh):
    placed = (
        P("layer", None, "row", "col", None),
        P("layer", None, "row", "col", None),
        P("layer", "row", "col", None, None, None),
        P("layer", "row", "col", None),
        P(),
        P(),
        P(),
    )
    return jax.shard_map(
        local,
        mesh=mesh,
        in_specs=placed,
        out_specs=(
            P("layer", None, "row", "col", None),
            P("layer", None, "row", "col", None),
            P(None, "row", "col", None),
        ),
        check_vma=False,
    )
```

```python
import functools

import jax
import jax.numpy as jnp
from jax import lax
from jax.experimental import pallas as pl
from jax.experimental.pallas import tpu as pltpu
from jax.sharding import PartitionSpec as P

port_strength = 4.0
intersection_scale = 0.125
AXES = ("layer", "row", "col")
OFFSETS = 9
VMEM_BYTES = 24 * 1024 * 1024

VM = pl.BlockSpec(memory_space=pltpu.VMEM)


def call(kernel, outs, *args, far_args=0, scratch=(), aliases=None):
    args = [pltpu.with_memory_space_constraint(a, pltpu.HBM) for a in args[:far_args]] + list(args[far_args:])
    return pl.pallas_call(
        kernel,
        out_shape=[jax.ShapeDtypeStruct(shape, dtype) for shape, dtype in outs],
        in_specs=[pl.BlockSpec(memory_space=pltpu.HBM)] * far_args + [VM] * (len(args) - far_args),
        out_specs=[VM] * len(outs),
        scratch_shapes=list(scratch),
        input_output_aliases=aliases or {},
        compiler_params=pltpu.CompilerParams(vmem_limit_bytes=VMEM_BYTES),
    )(*args)


def near(i, n):
    return i ^ 1


def far(i, n):
    return (((i + 1) ^ 1) - 1) % n


def pairings(n):
    return [near] if n == 2 else [near, far]


class Side:
    def __init__(self, pairing, axis, tiles):
        pos, count = lax.axis_index(axis), lax.axis_size(axis)
        even = lax.rem(pos, 2) == 0
        after = even if pairing is near else jnp.logical_not(even)
        self.step = jnp.where(after, 1, -1)
        self.edge = jnp.where(after, tiles - 1, 0)
        self.real = None
        if pairing is far:
            self.real = jnp.logical_not(
                jnp.logical_or(jnp.logical_and(after, pos == count - 1), jnp.logical_and(jnp.logical_not(after), pos == 0))
            )

    def when(self, body):
        if self.real is None:
            body()
        else:
            pl.when(self.real)(body)


def local(sources, adjoint_sources, blocks, pattern, coupling, layer_group, port_cells):
    ports, tiles_x, tiles_y, cells = sources.shape[1:]
    tiles = tiles_x * tiles_y
    groups = coupling.shape[0]
    layers, rows, cols = (lax.axis_size(axis) for axis in AXES)
    row_pairs, col_pairs = pairings(rows), pairings(cols)
    ext = tiles_x + len(row_pairs)
    bf16, f32 = jnp.bfloat16, jnp.float32

    def route(of_layer=None, of_row=None, of_col=None):
        pairs = []
        for l in range(layers):
            for r in range(rows):
                for c in range(cols):
                    a = of_layer(l) if of_layer else l
                    b = of_row(r, rows) if of_row else r
                    d = of_col(c, cols) if of_col else c
                    pairs.append(((l * rows + r) * cols + c, (a * rows + b) * cols + d))
        return pairs

    def swapped(array, **where):
        return lax.ppermute(array, AXES, route(**where))

    def to_next(step, array, of_row=None):
        pairs = []
        for l in range(layers):
            a = (near if step % 2 == 0 else far)(l, layers)
            for r in range(rows):
                for c in range(cols):
                    if abs(a - l) == 1:
                        target = (a, of_row(r, rows) if of_row else r, c)
                    else:
                        target = (l, r, near(c, cols))
                    pairs.append(((l * rows + r) * cols + c, (target[0] * rows + target[1]) * cols + target[2]))
        return lax.ppermute(array, AXES, pairs)

    def is_active(step):
        pos = lax.axis_index("layer")
        return jnp.logical_or(pos == step, pos == layers - 1 - step)

    def sweep_of(step):
        return jnp.where(lax.axis_index("layer") == step, 0, 1)

    def port_map(cells_ref, x, y):
        x_pos = lax.axis_index("row") * tiles_x + x
        y_pos = lax.axis_index("col") * tiles_y + y
        first = (x_pos * (tiles_y * cols) + y_pos) * cells
        row = jnp.broadcast_to(cells_ref[...], (ports, ports))
        diagonal = lax.broadcasted_iota(jnp.int32, (ports, ports), 0) == lax.broadcasted_iota(
            jnp.int32, (ports, ports), 1
        )
        column = jnp.sum(jnp.where(diagonal, row, 0), axis=1, keepdims=True)
        lane = lax.broadcasted_iota(jnp.int32, (ports, cells), 1)
        return jnp.where(column - first == lane, port_strength, 0.0).astype(f32)

    def source_tile(flat_ref, cells_ref, sweep, x, y):
        tile = flat_ref[sweep, pl.ds(x * tiles_y + y, ports, stride=tiles), :]
        pos = lax.axis_index("layer")
        end = pos == (0 if sweep == 0 else layers - 1)
        return (tile + jnp.where(end, port_map(cells_ref, x, y), 0.0)).astype(bf16)

    def rims_kernel(forward_hbm, adjoint_hbm, cells_hbm, flat_ref, cells_ref, *refs):
        rim_refs, (forward_ref, adjoint_ref, sems) = refs[: len(row_pairs)], refs[len(row_pairs) :]
        copies = [
            pltpu.make_async_copy(src, dst, sems.at[i])
            for i, (src, dst) in enumerate(
                ((forward_hbm, forward_ref), (adjoint_hbm, adjoint_ref), (cells_hbm, cells_ref))
            )
        ]
        for copy in copies:
            copy.start()
        for copy in copies:
            copy.wait()
        flat_ref[0] = forward_ref[...].astype(f32).reshape(ports * tiles, cells)
        flat_ref[1] = adjoint_ref[...].astype(f32).reshape(ports * tiles, cells)
        for pairing, rim_ref in zip(row_pairs, rim_refs):
            side = Side(pairing, "row", tiles_x)
            for sweep in range(2):
                for y in range(tiles_y):
                    rim_ref[sweep, y] = source_tile(flat_ref, cells_ref, sweep, side.edge, y)

    port_row = port_cells.reshape(1, ports)
    raw = (ports, tiles, cells)
    flat, port_row, *rims = call(
        rims_kernel,
        [((2, ports * tiles, cells), f32), ((1, ports), jnp.int32)]
        + [((2, tiles_y, ports, cells), bf16)] * len(row_pairs),
        sources.reshape(raw),
        adjoint_sources.reshape(raw),
        port_row,
        far_args=3,
        scratch=[pltpu.VMEM(raw, bf16), pltpu.VMEM(raw, bf16), pltpu.SemaphoreType.DMA((3,))],
    )
    source_rims = [swapped(rim, of_row=pairing) for rim, pairing in zip(rims, row_pairs)]

    def setup_kernel(
        pattern_hbm,
        coupling_hbm,
        group_hbm,
        blocks_hbm,
        flat_ref,
        cells_ref,
        source_ref,
        front_ref,
        kappa_ref,
        member_ref,
        pattern_ref,
        coupling_ref,
        group_ref,
        blocks_ref,
        sems,
        block_sems,
    ):
        scalars = [
            pltpu.make_async_copy(src, dst, sems.at[i])
            for i, (src, dst) in enumerate(
                ((pattern_hbm, pattern_ref), (coupling_hbm, coupling_ref), (group_hbm, group_ref))
            )
        ]
        loads = [
            pltpu.make_async_copy(blocks_hbm.at[t], blocks_ref.at[t], block_sems.at[t]) for t in range(tiles)
        ]
        for copy in scalars + loads:
            copy.start()
        for sweep in range(2):
            for x in range(tiles_x):
                for y in range(tiles_y):
                    source_ref[sweep, x * tiles_y + y] = source_tile(flat_ref, cells_ref, sweep, x, y)

        for copy in scalars:
            copy.wait()
        for t in range(tiles):
            loads[t].wait()
            for offset in range(OFFSETS):
                present = pattern_ref[t // tiles_y, t % tiles_y, offset] > 0
                front_ref[t, offset] = jnp.where(present, blocks_ref[t, offset], jnp.zeros((cells, cells), bf16))
        pos = lax.axis_index("layer")
        own = coupling_ref[group_ref[pos]]
        following = coupling_ref[group_ref[jnp.minimum(pos + 1, layers - 1)]]
        kappa_ref[0] = jnp.full((8, cells), own, f32)
        kappa_ref[1] = jnp.full((8, cells), following, f32)
        for g in range(groups):
            for l in range(layers):
                member_ref[g, l] = jnp.full((tiles, cells), jnp.where(group_ref[l] == g, 1.0, 0.0), f32)

    source, front, kappa, member = call(
        setup_kernel,
        [
            ((2, tiles, ports, cells), bf16),
            ((tiles, OFFSETS, cells, cells), bf16),
            ((2, 8, cells), f32),
            ((groups, layers, tiles, cells), f32),
        ],
        pattern[0],
        coupling,
        layer_group,
        blocks.reshape(tiles, OFFSETS, cells, cells),
        flat,
        port_row,
        far_args=4,
        scratch=[
            pltpu.SMEM(pattern.shape[1:], jnp.int32),
            pltpu.SMEM(coupling.shape, f32),
            pltpu.SMEM(layer_group.shape, jnp.int32),
            pltpu.VMEM((tiles, OFFSETS, cells, cells), bf16),
            pltpu.SemaphoreType.DMA((3,)),
            pltpu.SemaphoreType.DMA((tiles,)),
        ],
    )

    def wave_kernel(step, *refs):
        source_ref, kappa_ref = refs[:2]
        refs = refs[2:]
        halo_refs, refs = refs[: len(row_pairs)], refs[len(row_pairs) :]
        if step > 0:
            field_ref, refs = refs[0], refs[1:]
            field_rims, refs = refs[: len(row_pairs)], refs[len(row_pairs) :]
        wave_ref, rim_refs = refs[0], refs[1:]

        @pl.when(is_active(step))
        def _():
            sweep = sweep_of(step)

            def wave(base, field):
                if step == 0:
                    return base
                factor = kappa_ref[sweep, 0:1, :]
                return (base.astype(f32) + factor * field.astype(f32)).astype(bf16)

            for x in range(tiles_x):
                for y in range(tiles_y):
                    t = x * tiles_y + y
                    wave_ref[x, y] = wave(source_ref[sweep, t], field_ref[t] if step > 0 else None)
            for h, pairing in enumerate(row_pairs):
                side = Side(pairing, "row", tiles_x)
                for y in range(tiles_y):
                    value = wave(halo_refs[h][sweep, y], field_rims[h][y] if step > 0 else None)
                    if side.real is not None:
                        value = jnp.where(side.real, value, jnp.zeros_like(value))
                    wave_ref[tiles_x + h, y] = value
            for pairing, rim_ref in zip(col_pairs, rim_refs):
                edge = Side(pairing, "col", tiles_y).edge
                for x in range(ext):
                    rim_ref[x] = wave_ref[x, edge]

    def product(lhs, rhs):
        return jnp.dot(lhs, rhs, preferred_element_type=f32)

    def inner_kernel(step, wave_ref, front_ref, sum_ref):
        @pl.when(is_active(step))
        def _():
            for y in range(tiles_y):
                low, high = max(y - 1, 0), min(y + 1, tiles_y - 1)
                width = high - low + 1
                first = low - y + 1
                beside = [
                    jnp.concatenate([wave_ref[x, j] for j in range(low, high + 1)], axis=1) for x in range(ext)
                ]
                for x in range(tiles_x):
                    reach = [a for a in (-1, 0, 1) if 0 <= x + a < tiles_x]
                    lhs = jnp.concatenate([beside[x + a] for a in reach], axis=1)
                    rhs = jnp.concatenate(
                        [
                            front_ref[x * tiles_y + y, 3 * (a + 1) + first : 3 * (a + 1) + first + width].reshape(
                                width * cells, cells
                            )
                            for a in reach
                        ],
                        axis=0,
                    )
                    sum_ref[x * tiles_y + y] = product(lhs, rhs)
                for h, pairing in enumerate(row_pairs):
                    side = Side(pairing, "row", tiles_x)
                    t = side.edge * tiles_y + y
                    rhs = front_ref[t, pl.ds(3 * (side.step + 1) + first, width)].reshape(width * cells, cells)
                    sum_ref[t] += product(beside[tiles_x + h], rhs)

    def outer_kernel(step, *refs):
        front_ref = refs[1]
        halo_refs, refs = refs[2 : 2 + len(col_pairs)], refs[2 + len(col_pairs) :]
        if step == layers - 1:
            earlier, refs = refs[: layers - 1], refs[layers - 1 :]
        sum_ref, field_ref, refs = refs[0], refs[1], refs[2:]

        @pl.when(is_active(step))
        def _():
            for pairing, halo_ref in zip(col_pairs, halo_refs):
                across = Side(pairing, "col", tiles_y)

                def add(across=across, halo_ref=halo_ref):
                    for x in range(tiles_x):
                        t = x * tiles_y + across.edge
                        reach = [a for a in (-1, 0, 1) if 0 <= x + a < tiles_x]
                        lhs = jnp.concatenate([halo_ref[x + a] for a in reach], axis=1)
                        rhs = jnp.concatenate([front_ref[t, 3 * (a + 1) + 1 + across.step] for a in reach], axis=0)
                        sum_ref[t] += product(lhs, rhs)
                    for h, row_pairing in enumerate(row_pairs):
                        side = Side(row_pairing, "row", tiles_x)
                        t = side.edge * tiles_y + across.edge
                        sum_ref[t] += product(halo_ref[tiles_x + h], front_ref[t, 3 * (side.step + 1) + 1 + across.step])

                across.when(add)
            for t in range(tiles):
                field_ref[t] = sum_ref[t].astype(bf16)
            if step < layers - 1:
                for pairing, rim_ref in zip(row_pairs, refs):
                    edge = Side(pairing, "row", tiles_x).edge
                    rim_ref[...] = field_ref[pl.ds(edge * tiles_y, tiles_y)]

        if step == layers - 1:
            pos = lax.axis_index("layer")
            first = jnp.minimum(pos, layers - 1 - pos)
            for k in range(layers // 2):

                @pl.when(first == k)
                def _(k=k):
                    one, other = earlier[k], field_ref if k == 0 else earlier[layers - 1 - k]
                    for t in range(tiles):
                        both = one[t].astype(f32) * other[t].astype(f32)
                        refs[0][t : t + 1, :] = jnp.sum(both, axis=0, keepdims=True) * intersection_scale

    fields, received, received_rims = [], None, []
    for step in range(layers):
        wave, *rims = call(
            functools.partial(wave_kernel, step),
            [((ext, tiles_y, ports, cells), bf16)] + [((ext, ports, cells), bf16)] * len(col_pairs),
            source,
            kappa,
            *source_rims,
            *([received, *received_rims] if step > 0 else []),
        )
        halos = [swapped(rim, of_col=pairing) for rim, pairing in zip(rims, col_pairs)]
        (summed,) = call(
            functools.partial(inner_kernel, step), [((tiles, ports, cells), f32)], wave, front
        )
        last = step == layers - 1
        _, field, *extra = call(
            functools.partial(outer_kernel, step),
            [((tiles, ports, cells), f32), ((tiles, ports, cells), bf16)]
            + ([((tiles, cells), f32)] if last else [((tiles_y, ports, cells), bf16)] * len(row_pairs)),
            summed,
            front,
            *halos,
            *(fields if last else []),
            aliases={0: 0},
        )
        fields.append(field)
        if not last:
            received = to_next(step, field)
            received_rims = [to_next(step, rim, pairing) for rim, pairing in zip(extra, row_pairs)]
    intersection = extra[0]

    def fields_kernel(*refs):
        field_refs, (forward_ref, adjoint_ref, flat_ref) = refs[:layers], refs[layers:]
        pos = lax.axis_index("layer")
        for out_ref, active in ((forward_ref, lambda s: s), (adjoint_ref, lambda s: layers - 1 - s)):
            for step in range(layers):

                @pl.when(pos == active(step))
                def _(step=step):
                    for t in range(tiles):
                        flat_ref[pl.ds(t, ports, stride=tiles), :] = field_refs[step][t].astype(f32)

            out_ref[...] = flat_ref[...].reshape(ports, tiles, cells).astype(bf16)

    forward, adjoint = call(
        fields_kernel,
        [((ports, tiles, cells), bf16)] * 2,
        *fields,
        scratch=[pltpu.VMEM((ports * tiles, cells), f32)],
    )

    if layers == 4:
        parts = [intersection] + [swapped(intersection, of_layer=lambda l, m=m: l ^ m) for m in range(1, layers)]

        def gradient_kernel(*refs):
            part_refs, member_ref, out_ref = refs[:layers], refs[layers], refs[layers + 1]
            pos = lax.axis_index("layer")
            for g in range(groups):
                total = jnp.zeros((tiles, cells), f32)
                for m in range(layers):
                    total = total + member_ref[g, pos ^ m] * part_refs[m][...]
                for x in range(tiles_x):
                    out_ref[g, x] = total[x * tiles_y : (x + 1) * tiles_y]

        (gradient,) = call(
            gradient_kernel, [((groups, tiles_x, tiles_y, cells), f32)], *parts, member
        )
    else:
        selected = lax.dynamic_index_in_dim(member, lax.axis_index("layer"), 1, keepdims=False)
        gradient = lax.psum(selected * intersection[None], "layer").reshape(groups, tiles_x, tiles_y, cells)
    shape = (1, ports, tiles_x, tiles_y, cells)
    return (forward.reshape(shape), adjoint.reshape(shape), gradient)


def solution(mesh):
    placed = (
        P("layer", None, "row", "col", None),
        P("layer", None, "row", "col", None),
        P("layer", "row", "col", None, None, None),
        P("layer", "row", "col", None),
        P(),
        P(),
        P(),
    )
    return jax.shard_map(
        local,
        mesh=mesh,
        in_specs=placed,
        out_specs=(
            P("layer", None, "row", "col", None),
            P("layer", None, "row", "col", None),
            P(None, "row", "col", None),
        ),
        check_vma=False,
    )
```

```python
import functools

import jax
import jax.numpy as jnp
from jax import lax
from jax.experimental import pallas as pl
from jax.experimental.pallas import tpu as pltpu
from jax.sharding import PartitionSpec as P

port_strength = 4.0
intersection_scale = 0.125
AXES = ("layer", "row", "col")
OFFSETS = 9
VMEM_BYTES = 24 * 1024 * 1024
SPARE = 2

VM = pl.BlockSpec(memory_space=pltpu.VMEM)


def call(kernel, outs, *args, far_args=0, scratch=(), aliases=None):
    args = [pltpu.with_memory_space_constraint(a, pltpu.HBM) for a in args[:far_args]] + list(args[far_args:])
    return pl.pallas_call(
        kernel,
        out_shape=[jax.ShapeDtypeStruct(shape, dtype) for shape, dtype in outs],
        in_specs=[pl.BlockSpec(memory_space=pltpu.HBM)] * far_args + [VM] * (len(args) - far_args),
        out_specs=[VM] * len(outs),
        scratch_shapes=list(scratch),
        input_output_aliases=aliases or {},
        compiler_params=pltpu.CompilerParams(vmem_limit_bytes=VMEM_BYTES),
    )(*args)


def near(i, n):
    return i ^ 1


def far(i, n):
    return (((i + 1) ^ 1) - 1) % n


def pairings(n):
    return [near] if n == 2 else [near, far]


class Side:
    def __init__(self, pairing, axis, tiles):
        pos, count = lax.axis_index(axis), lax.axis_size(axis)
        even = lax.rem(pos, 2) == 0
        after = even if pairing is near else jnp.logical_not(even)
        self.step = jnp.where(after, 1, -1)
        self.edge = jnp.where(after, tiles - 1, 0)
        self.real = None
        if pairing is far:
            self.real = jnp.logical_not(
                jnp.logical_or(jnp.logical_and(after, pos == count - 1), jnp.logical_and(jnp.logical_not(after), pos == 0))
            )

    def when(self, body):
        if self.real is None:
            body()
        else:
            pl.when(self.real)(body)


def local(sources, adjoint_sources, blocks, pattern, coupling, layer_group, port_cells):
    ports, tiles_x, tiles_y, cells = sources.shape[1:]
    tiles = tiles_x * tiles_y
    groups = coupling.shape[0]
    layers, rows, cols = (lax.axis_size(axis) for axis in AXES)
    if cols != 4 or layers % 2 or rows % 2:
        raise ValueError("unsupported mesh")
    row_pairs = pairings(rows)
    halos = len(row_pairs)
    ext = tiles_x + halos
    bf16, f32 = jnp.bfloat16, jnp.float32
    tile = (ports, cells)

    def permuted(array, target):
        pairs = []
        for l in range(layers):
            for r in range(rows):
                for c in range(cols):
                    a, b, d = target(l, r, c)
                    pairs.append(((l * rows + r) * cols + c, (a * rows + b) * cols + d))
        return lax.ppermute(array, AXES, pairs)

    def to_core(array):
        return permuted(array, lambda l, r, c: (l, r, near(c, cols)))

    def to_layer(step, beside):
        def target(l, r, c):
            if step is None:
                return l, *beside(r, c)
            a = (near if step % 2 == 0 else far)(l, layers)
            return (a, *beside(r, c)) if abs(a - l) == 1 else (l, r, near(c, cols))

        return lambda array: permuted(array, target)

    def same(r, c):
        return r, c

    def other_row(pairing):
        return lambda r, c: (pairing(r, rows), c)

    def other_chip(pairing):
        def beside(r, c):
            d = far(c, cols)
            return (r if abs(d - c) == 1 else pairing(r, rows)), d

        return beside

    def is_active(step):
        pos = lax.axis_index("layer")
        return jnp.logical_or(pos == step, pos == layers - 1 - step)

    def taker(refs):
        refs = list(refs)

        def take(count=None):
            taken = refs[: 1 if count is None else count]
            del refs[: len(taken)]
            return taken[0] if count is None else taken

        return take

    def first_sweep():
        return jnp.where(lax.axis_index("layer") < layers // 2, 0, 1)

    def port_map(cells_ref, x, y):
        x_pos = lax.axis_index("row") * tiles_x + x
        y_pos = lax.axis_index("col") * tiles_y + y
        first = (x_pos * (tiles_y * cols) + y_pos) * cells
        row = jnp.broadcast_to(cells_ref[...], (ports, ports))
        diagonal = lax.broadcasted_iota(jnp.int32, (ports, ports), 0) == lax.broadcasted_iota(
            jnp.int32, (ports, ports), 1
        )
        column = jnp.sum(jnp.where(diagonal, row, 0), axis=1, keepdims=True)
        lane = lax.broadcasted_iota(jnp.int32, tile, 1)
        return jnp.where(column - first == lane, port_strength, 0.0).astype(f32)

    def source_tile(flat_ref, cells_ref, phase, x, y):
        value = flat_ref[phase, pl.ds(x * tiles_y + y, ports, stride=tiles), :]
        if phase == 0:
            pos = lax.axis_index("layer")
            end = jnp.logical_or(pos == 0, pos == layers - 1)
            value = value + jnp.where(end, port_map(cells_ref, x, y), 0.0)
        return value.astype(bf16)

    def corner_kernel(forward_hbm, adjoint_hbm, cells_hbm, flat_ref, cells_ref, corner_ref, raw_ref, sems):
        copies = [
            pltpu.make_async_copy(src, dst, sems.at[i])
            for i, (src, dst) in enumerate(
                ((forward_hbm, raw_ref.at[0]), (adjoint_hbm, raw_ref.at[1]), (cells_hbm, cells_ref))
            )
        ]
        for copy in copies:
            copy.start()
        for copy in copies:
            copy.wait()
        edge = Side(far, "col", tiles_y).edge
        for phase in range(2):
            flat_ref[phase] = raw_ref[first_sweep() ^ phase].astype(f32).reshape(ports * tiles, cells)
            for h, pairing in enumerate(row_pairs):
                row = Side(pairing, "row", tiles_x).edge
                corner_ref[h, phase] = source_tile(flat_ref, cells_ref, phase, row, edge)

    def rims_kernel(flat_ref, cells_ref, *refs):
        take = taker(refs)
        rim_refs, column_ref = take(halos), take()
        edge = Side(far, "col", tiles_y).edge
        for phase in range(2):
            for x in range(tiles_x):
                column_ref[phase, x] = source_tile(flat_ref, cells_ref, phase, x, edge)
            for h, pairing in enumerate(row_pairs):
                row = Side(pairing, "row", tiles_x).edge
                for y in range(tiles_y):
                    rim_refs[h][phase, y] = source_tile(flat_ref, cells_ref, phase, row, y)

    raw_shape = (ports, tiles, cells)
    flat, port_row, corner = call(
        corner_kernel,
        [((2, ports * tiles, cells), f32), ((1, ports), jnp.int32), ((SPARE * halos, 2, *tile), bf16)],
        sources.reshape(raw_shape),
        adjoint_sources.reshape(raw_shape),
        port_cells.reshape(1, ports),
        far_args=3,
        scratch=[pltpu.VMEM((2, *raw_shape), bf16), pltpu.SemaphoreType.DMA((3,))],
    )
    corner = to_core(corner)
    outward = call(
        rims_kernel, [((2, tiles_y, *tile), bf16)] * halos + [((2, tiles_x, *tile), bf16)], flat, port_row
    )

    def relay_kernel(*refs):
        take = taker(refs)
        column_ref, corner_ref, out_refs = take(), take(), take(halos)
        inner = Side(far, "col", tiles_y).real

        @pl.when(inner)
        def _():
            for out_ref in out_refs:
                out_ref[...] = column_ref[...]

        @pl.when(jnp.logical_not(inner))
        def _():
            for h, out_ref in enumerate(out_refs):
                if len(out_ref.shape) == 4:
                    for phase in range(2):
                        out_ref[phase, 0] = corner_ref[h, phase]
                else:
                    out_ref[0] = corner_ref[h]

    def exchange(step, corner, outward, field=None):
        rims, column = outward[:halos], outward[halos]
        arrived = [] if field is None else [to_layer(step, same)(field)]
        arrived += [to_layer(step, other_row(pairing))(rim) for rim, pairing in zip(rims, row_pairs)]
        carried = call(relay_kernel, [(column.shape, bf16)] * halos, column, corner)
        return arrived + [to_layer(step, other_chip(pairing))(part) for part, pairing in zip(carried, row_pairs)]

    source_beside = exchange(None, corner, outward)

    def setup_kernel(pattern_hbm, coupling_hbm, group_hbm, blocks_hbm, *refs):
        take = taker(refs)
        flat_ref, cells_ref, source_ref, front_ref, kappa_ref, member_ref = (take() for _ in range(6))
        pattern_ref, coupling_ref, group_ref, blocks_ref, sems, block_sems = (take() for _ in range(6))
        scalars = [
            pltpu.make_async_copy(src, dst, sems.at[i])
            for i, (src, dst) in enumerate(
                ((pattern_hbm, pattern_ref), (coupling_hbm, coupling_ref), (group_hbm, group_ref))
            )
        ]
        loads = [
            pltpu.make_async_copy(blocks_hbm.at[t], blocks_ref.at[t], block_sems.at[t]) for t in range(tiles)
        ]
        for copy in scalars + loads:
            copy.start()
        for phase in range(2):
            for x in range(tiles_x):
                for y in range(tiles_y):
                    source_ref[phase, x * tiles_y + y] = source_tile(flat_ref, cells_ref, phase, x, y)
        for copy in scalars:
            copy.wait()
        for t in range(tiles):
            loads[t].wait()
            for offset in range(OFFSETS):
                present = pattern_ref[t // tiles_y, t % tiles_y, offset] > 0
                front_ref[t, offset] = jnp.where(present, blocks_ref[t, offset], jnp.zeros((cells, cells), bf16))
        pos = lax.axis_index("layer")
        own = coupling_ref[group_ref[pos]]
        following = coupling_ref[group_ref[jnp.minimum(pos + 1, layers - 1)]]
        early = first_sweep() == 0
        kappa_ref[0] = jnp.full((8, cells), jnp.where(early, own, following), f32)
        kappa_ref[1] = jnp.full((8, cells), jnp.where(early, following, own), f32)
        for g in range(groups):
            for l in range(layers):
                member_ref[g, l] = jnp.full((tiles, cells), jnp.where(group_ref[l] == g, 1.0, 0.0), f32)

    source, front, kappa, member = call(
        setup_kernel,
        [
            ((2, tiles, *tile), bf16),
            ((tiles, OFFSETS, cells, cells), bf16),
            ((2, 8, cells), f32),
            ((groups, layers, tiles, cells), f32),
        ],
        pattern[0],
        coupling,
        layer_group,
        blocks.reshape(tiles, OFFSETS, cells, cells),
        flat,
        port_row,
        far_args=4,
        scratch=[
            pltpu.SMEM(pattern.shape[1:], jnp.int32),
            pltpu.SMEM(coupling.shape, f32),
            pltpu.SMEM(layer_group.shape, jnp.int32),
            pltpu.VMEM((tiles, OFFSETS, cells, cells), bf16),
            pltpu.SemaphoreType.DMA((3,)),
            pltpu.SemaphoreType.DMA((tiles,)),
        ],
    )

    def waves(phase, kappa_ref):
        def wave(base, field=None, real=None):
            if field is not None:
                factor = kappa_ref[phase, 0:1, :]
                base = (base.astype(f32) + factor * field.astype(f32)).astype(bf16)
            return base if real is None else jnp.where(real, base, jnp.zeros_like(base))

        return wave

    def row_real():
        return [Side(pairing, "row", tiles_x).real for pairing in row_pairs]

    def wave_kernel(step, *refs):
        take = taker(refs)
        phase = int(step >= layers // 2)
        source_ref, kappa_ref, rim_refs, column_refs = take(), take(), take(halos), take(halos)
        field_ref, field_rims, carried = None, [None] * halos, column_refs
        if step > 0:
            field_ref, field_rims, carried = take(), take(halos), take(halos)
        wave_ref, core_ref, side_ref = take(), take(), take()
        if step > 0:
            for h in range(halos):
                core_ref[ext + h] = carried[h][0]
        else:
            for h in range(halos):
                for p in range(2):
                    core_ref[ext + p * halos + h] = column_refs[h][p, 0]

        @pl.when(is_active(step))
        def _():
            wave = waves(phase, kappa_ref)
            real = row_real()
            for x in range(tiles_x):
                for y in range(tiles_y):
                    t = x * tiles_y + y
                    wave_ref[x, y] = wave(source_ref[phase, t], None if step == 0 else field_ref[t])
                side_ref[x] = wave(column_refs[0][phase, x], None if step == 0 else carried[0][x])
            for h in range(halos):
                for y in range(tiles_y):
                    wave_ref[tiles_x + h, y] = wave(
                        rim_refs[h][phase, y], None if step == 0 else field_rims[h][y], real[h]
                    )
            edge = Side(near, "col", tiles_y).edge
            for x in range(ext):
                core_ref[x] = wave_ref[x, edge]

    def product(lhs, rhs):
        return jnp.dot(lhs, rhs, preferred_element_type=f32)

    def add_column(across, sum_ref, front_ref, halo_ref):
        for x in range(tiles_x):
            t = x * tiles_y + across.edge
            reach = [a for a in (-1, 0, 1) if 0 <= x + a < tiles_x]
            lhs = jnp.concatenate([halo_ref[x + a] for a in reach], axis=1)
            rhs = jnp.concatenate([front_ref[t, 3 * (a + 1) + 1 + across.step] for a in reach], axis=0)
            sum_ref[t] += product(lhs, rhs)

    def add_corner(across, pairing, sum_ref, front_ref, corner):
        side = Side(pairing, "row", tiles_x)
        t = side.edge * tiles_y + across.edge
        sum_ref[t] += product(corner, front_ref[t, 3 * (side.step + 1) + 1 + across.step])

    def inner_kernel(step, wave_ref, side_ref, front_ref, sum_ref):
        @pl.when(is_active(step))
        def _():
            for y in range(tiles_y):
                low, high = max(y - 1, 0), min(y + 1, tiles_y - 1)
                width = high - low + 1
                first = low - y + 1
                beside = [
                    jnp.concatenate([wave_ref[x, j] for j in range(low, high + 1)], axis=1) for x in range(ext)
                ]
                for x in range(tiles_x):
                    reach = [a for a in (-1, 0, 1) if 0 <= x + a < tiles_x]
                    lhs = jnp.concatenate([beside[x + a] for a in reach], axis=1)
                    rhs = jnp.concatenate(
                        [
                            front_ref[x * tiles_y + y, 3 * (a + 1) + first : 3 * (a + 1) + first + width].reshape(
                                width * cells, cells
                            )
                            for a in reach
                        ],
                        axis=0,
                    )
                    sum_ref[x * tiles_y + y] = product(lhs, rhs)
                for h, pairing in enumerate(row_pairs):
                    side = Side(pairing, "row", tiles_x)
                    t = side.edge * tiles_y + y
                    rhs = front_ref[t, pl.ds(3 * (side.step + 1) + first, width)].reshape(width * cells, cells)
                    sum_ref[t] += product(beside[tiles_x + h], rhs)
            across = Side(far, "col", tiles_y)
            across.when(lambda: add_column(across, sum_ref, front_ref, side_ref))

    def add_far_corners(step, sum_ref, front_ref, kappa_ref, core_ref, base_ref):
        phase = int(step >= layers // 2)
        wave = waves(phase, kappa_ref)
        real = row_real()
        beyond = Side(far, "col", tiles_y)

        def corners():
            for h, pairing in enumerate(row_pairs):
                base = base_ref[ext + phase * halos + h]
                corner = wave(base, None if step == 0 else core_ref[ext + h], real[h])
                add_corner(beyond, pairing, sum_ref, front_ref, corner)

        beyond.when(corners)

    def corner_front_kernel(step, *refs):
        take = taker(refs)
        take()
        front_ref, kappa_ref, core_ref, base_ref, sum_ref, corner_ref = (take() for _ in range(6))

        @pl.when(is_active(step))
        def _():
            add_far_corners(step, sum_ref, front_ref, kappa_ref, core_ref, base_ref)
            edge = Side(far, "col", tiles_y).edge
            for h, pairing in enumerate(row_pairs):
                row = Side(pairing, "row", tiles_x).edge
                corner_ref[h] = sum_ref[row * tiles_y + edge].astype(bf16)

    def outer_kernel(step, *refs):
        take = taker(refs)
        take()
        front_ref, core_ref = take(), take()
        last = step == layers - 1
        kappa_ref, base_ref = (take(), take()) if last else (None, None)
        earlier = take(layers - 1) if last else []
        sum_ref, field_ref, rest = take(), take(), take(halos + 1)

        @pl.when(is_active(step))
        def _():
            if last:
                add_far_corners(step, sum_ref, front_ref, kappa_ref, core_ref, base_ref)
            across = Side(near, "col", tiles_y)
            add_column(across, sum_ref, front_ref, core_ref)
            for h, pairing in enumerate(row_pairs):
                add_corner(across, pairing, sum_ref, front_ref, core_ref[tiles_x + h])
            for t in range(tiles):
                field_ref[t] = sum_ref[t].astype(bf16)
            if not last:
                edge = Side(far, "col", tiles_y).edge
                for x in range(tiles_x):
                    rest[halos][x] = field_ref[x * tiles_y + edge]
                for h, pairing in enumerate(row_pairs):
                    row = Side(pairing, "row", tiles_x).edge
                    rest[h][...] = field_ref[pl.ds(row * tiles_y, tiles_y)]

        if step == layers - 1:
            pos = lax.axis_index("layer")
            first = jnp.minimum(pos, layers - 1 - pos)
            for k in range(layers // 2):

                @pl.when(first == k)
                def _(k=k):
                    one, other = earlier[k], field_ref if k == 0 else earlier[layers - 1 - k]
                    for t in range(tiles):
                        both = one[t].astype(f32) * other[t].astype(f32)
                        rest[0][t : t + 1, :] = jnp.sum(both, axis=0, keepdims=True) * intersection_scale

    fields, field_arrived, first_core = [], [], None
    for step in range(layers):
        last = step == layers - 1
        wave, core, side = call(
            functools.partial(wave_kernel, step),
            [
                ((ext, tiles_y, *tile), bf16),
                ((ext + halos * (2 if step == 0 else 1), *tile), bf16),
                ((tiles_x, *tile), bf16),
            ],
            source,
            kappa,
            *source_beside,
            *field_arrived,
        )
        core = to_core(core)
        if step == 0:
            first_core = core
        (summed,) = call(
            functools.partial(inner_kernel, step), [((tiles, *tile), f32)], wave, side, front
        )
        base = core if step == 0 else first_core
        if not last:
            summed, corner = call(
                functools.partial(corner_front_kernel, step),
                [((tiles, *tile), f32), ((SPARE * halos, *tile), bf16)],
                summed,
                front,
                kappa,
                core,
                base,
                aliases={0: 0},
            )
            corner = to_core(corner)
        _, field, *extra = call(
            functools.partial(outer_kernel, step),
            [((tiles, *tile), f32), ((tiles, *tile), bf16)]
            + (
                [((tiles, cells), f32)]
                if last
                else [((tiles_y, *tile), bf16)] * halos + [((tiles_x, *tile), bf16)]
            ),
            summed,
            front,
            core,
            *([kappa, base, *fields] if last else []),
            aliases={0: 0},
        )
        fields.append(field)
        if not last:
            field_arrived = exchange(step, corner, extra, field)
    intersection = extra[0]

    def fields_kernel(*refs):
        field_refs, (forward_ref, adjoint_ref, flat_ref) = refs[:layers], refs[layers:]
        pos = lax.axis_index("layer")
        for out_ref, active in ((forward_ref, lambda s: s), (adjoint_ref, lambda s: layers - 1 - s)):
            for step in range(layers):

                @pl.when(pos == active(step))
                def _(step=step):
                    for t in range(tiles):
                        flat_ref[pl.ds(t, ports, stride=tiles), :] = field_refs[step][t].astype(f32)

            out_ref[...] = flat_ref[...].reshape(ports, tiles, cells).astype(bf16)

    forward, adjoint = call(
        fields_kernel,
        [((ports, tiles, cells), bf16)] * 2,
        *fields,
        scratch=[pltpu.VMEM((ports * tiles, cells), f32)],
    )

    if layers == 4:
        parts = [intersection] + [
            permuted(intersection, lambda l, r, c, m=m: (l ^ m, r, c)) for m in range(1, layers)
        ]

        def gradient_kernel(*refs):
            part_refs, member_ref, out_ref = refs[:layers], refs[layers], refs[layers + 1]
            pos = lax.axis_index("layer")
            for g in range(groups):
                total = jnp.zeros((tiles, cells), f32)
                for m in range(layers):
                    total = total + member_ref[g, pos ^ m] * part_refs[m][...]
                for x in range(tiles_x):
                    out_ref[g, x] = total[x * tiles_y : (x + 1) * tiles_y]

        (gradient,) = call(
            gradient_kernel, [((groups, tiles_x, tiles_y, cells), f32)], *parts, member
        )
    else:
        selected = lax.dynamic_index_in_dim(member, lax.axis_index("layer"), 1, keepdims=False)
        gradient = lax.psum(selected * intersection[None], "layer").reshape(groups, tiles_x, tiles_y, cells)
    shape = (1, ports, tiles_x, tiles_y, cells)
    return (forward.reshape(shape), adjoint.reshape(shape), gradient)


def solution(mesh):
    placed = (
        P("layer", None, "row", "col", None),
        P("layer", None, "row", "col", None),
        P("layer", "row", "col", None, None, None),
        P("layer", "row", "col", None),
        P(),
        P(),
        P(),
    )
    return jax.shard_map(
        local,
        mesh=mesh,
        in_specs=placed,
        out_specs=(
            P("layer", None, "row", "col", None),
            P("layer", None, "row", "col", None),
            P(None, "row", "col", None),
        ),
        check_vma=False,
    )
```

```python
import functools

import jax
import jax.numpy as jnp
from jax import lax
from jax.experimental import pallas as pl
from jax.experimental.pallas import tpu as pltpu
from jax.sharding import PartitionSpec as P

port_strength = 4.0
intersection_scale = 0.125
AXES = ("layer", "row", "col")
OFFSETS = 9
VMEM_BYTES = 24 * 1024 * 1024
SPARE = 2

VM = pl.BlockSpec(memory_space=pltpu.VMEM)


def call(kernel, outs, *args, far_args=0, scratch=(), aliases=None):
    args = [pltpu.with_memory_space_constraint(a, pltpu.HBM) for a in args[:far_args]] + list(args[far_args:])
    return pl.pallas_call(
        kernel,
        out_shape=[jax.ShapeDtypeStruct(shape, dtype) for shape, dtype in outs],
        in_specs=[pl.BlockSpec(memory_space=pltpu.HBM)] * far_args + [VM] * (len(args) - far_args),
        out_specs=[VM] * len(outs),
        scratch_shapes=list(scratch),
        input_output_aliases=aliases or {},
        compiler_params=pltpu.CompilerParams(vmem_limit_bytes=VMEM_BYTES),
    )(*args)


def near(i, n):
    return i ^ 1


def far(i, n):
    return (((i + 1) ^ 1) - 1) % n


def pairings(n):
    return [near] if n == 2 else [near, far]


class Side:
    def __init__(self, pairing, axis, tiles):
        pos, count = lax.axis_index(axis), lax.axis_size(axis)
        even = lax.rem(pos, 2) == 0
        after = even if pairing is near else jnp.logical_not(even)
        self.step = jnp.where(after, 1, -1)
        self.edge = jnp.where(after, tiles - 1, 0)
        self.real = None
        if pairing is far:
            self.real = jnp.logical_not(
                jnp.logical_or(jnp.logical_and(after, pos == count - 1), jnp.logical_and(jnp.logical_not(after), pos == 0))
            )

    def when(self, body):
        if self.real is None:
            body()
        else:
            pl.when(self.real)(body)


def local(sources, adjoint_sources, blocks, pattern, coupling, layer_group, port_cells):
    ports, tiles_x, tiles_y, cells = sources.shape[1:]
    tiles = tiles_x * tiles_y
    groups = coupling.shape[0]
    layers, rows, cols = (lax.axis_size(axis) for axis in AXES)
    if cols != 4 or layers % 2 or rows % 2:
        raise ValueError("unsupported mesh")
    row_pairs = pairings(rows)
    halos = len(row_pairs)
    ext = tiles_x + halos
    bf16, f32 = jnp.bfloat16, jnp.float32
    tile = (ports, cells)

    def permuted(array, target):
        pairs = []
        for l in range(layers):
            for r in range(rows):
                for c in range(cols):
                    a, b, d = target(l, r, c)
                    pairs.append(((l * rows + r) * cols + c, (a * rows + b) * cols + d))
        return lax.ppermute(array, AXES, pairs)

    def to_core(array):
        return permuted(array, lambda l, r, c: (l, r, near(c, cols)))

    def to_layer(step, beside):
        def target(l, r, c):
            if step is None:
                return l, *beside(r, c)
            a = (near if step % 2 == 0 else far)(l, layers)
            return (a, *beside(r, c)) if abs(a - l) == 1 else (l, r, near(c, cols))

        return lambda array: permuted(array, target)

    def same(r, c):
        return r, c

    def other_row(pairing):
        return lambda r, c: (pairing(r, rows), c)

    def other_chip(pairing):
        def beside(r, c):
            d = far(c, cols)
            return (r if abs(d - c) == 1 else pairing(r, rows)), d

        return beside

    def is_active(step):
        pos = lax.axis_index("layer")
        return jnp.logical_or(pos == step, pos == layers - 1 - step)

    def taker(refs):
        refs = list(refs)

        def take(count=None):
            taken = refs[: 1 if count is None else count]
            del refs[: len(taken)]
            return taken[0] if count is None else taken

        return take

    def first_sweep():
        return jnp.where(lax.axis_index("layer") < layers // 2, 0, 1)

    def port_map(cells_ref, x, y):
        x_pos = lax.axis_index("row") * tiles_x + x
        y_pos = lax.axis_index("col") * tiles_y + y
        first = (x_pos * (tiles_y * cols) + y_pos) * cells
        row = jnp.broadcast_to(cells_ref[...], (ports, ports))
        diagonal = lax.broadcasted_iota(jnp.int32, (ports, ports), 0) == lax.broadcasted_iota(
            jnp.int32, (ports, ports), 1
        )
        column = jnp.sum(jnp.where(diagonal, row, 0), axis=1, keepdims=True)
        lane = lax.broadcasted_iota(jnp.int32, tile, 1)
        return jnp.where(column - first == lane, port_strength, 0.0).astype(f32)

    def source_tile(flat_ref, cells_ref, phase, x, y):
        value = flat_ref[phase, pl.ds(x * tiles_y + y, ports, stride=tiles), :]
        if phase == 0:
            pos = lax.axis_index("layer")
            end = jnp.logical_or(pos == 0, pos == layers - 1)
            value = value + jnp.where(end, port_map(cells_ref, x, y), 0.0)
        return value.astype(bf16)

    def corner_kernel(forward_hbm, adjoint_hbm, cells_hbm, flat_ref, cells_ref, corner_ref, raw_ref, sems):
        copies = [
            pltpu.make_async_copy(src, dst, sems.at[i])
            for i, (src, dst) in enumerate(
                ((forward_hbm, raw_ref.at[0]), (adjoint_hbm, raw_ref.at[1]), (cells_hbm, cells_ref))
            )
        ]
        for copy in copies:
            copy.start()
        for copy in copies:
            copy.wait()
        edge = Side(far, "col", tiles_y).edge
        for phase in range(2):
            flat_ref[phase] = raw_ref[first_sweep() ^ phase].astype(f32).reshape(ports * tiles, cells)
            for h, pairing in enumerate(row_pairs):
                row = Side(pairing, "row", tiles_x).edge
                corner_ref[h, phase] = source_tile(flat_ref, cells_ref, phase, row, edge)

    def rims_kernel(flat_ref, cells_ref, *refs):
        take = taker(refs)
        rim_refs, column_ref = take(halos), take()
        edge = Side(far, "col", tiles_y).edge
        for x in range(tiles_x):
            column_ref[x] = source_tile(flat_ref, cells_ref, 0, x, edge)
        for h, pairing in enumerate(row_pairs):
            row = Side(pairing, "row", tiles_x).edge
            for y in range(tiles_y):
                rim_refs[h][y] = source_tile(flat_ref, cells_ref, 0, row, y)

    raw_shape = (ports, tiles, cells)
    flat, port_row, corner = call(
        corner_kernel,
        [((2, ports * tiles, cells), f32), ((1, ports), jnp.int32), ((SPARE * halos, 2, *tile), bf16)],
        sources.reshape(raw_shape),
        adjoint_sources.reshape(raw_shape),
        port_cells.reshape(1, ports),
        far_args=3,
        scratch=[pltpu.VMEM((2, *raw_shape), bf16), pltpu.SemaphoreType.DMA((3,))],
    )
    corner = to_core(corner)
    outward = call(rims_kernel, [((tiles_y, *tile), bf16)] * halos + [((tiles_x, *tile), bf16)], flat, port_row)

    def relay_kernel(phase, *refs):
        take = taker(refs)
        column_ref, corner_ref, out_refs = take(), take(), take(halos)
        inner = Side(far, "col", tiles_y).real

        @pl.when(inner)
        def _():
            for out_ref in out_refs:
                out_ref[:tiles_x] = column_ref[...]

        @pl.when(jnp.logical_not(inner))
        def _():
            for h, out_ref in enumerate(out_refs):
                out_ref[0] = corner_ref[h] if phase is None else corner_ref[h, phase]

    def exchange(step, corner, outward, field=None):
        rims, column = outward[:halos], outward[halos]
        arrived = [] if field is None else [to_layer(step, same)(field)]
        arrived += [to_layer(step, other_row(pairing))(rim) for rim, pairing in zip(rims, row_pairs)]
        kernel = functools.partial(relay_kernel, 0 if step is None else None)
        carried = call(kernel, [(column.shape, bf16)] * halos, column, corner)
        return arrived + [to_layer(step, other_chip(pairing))(part) for part, pairing in zip(carried, row_pairs)]

    source_beside = exchange(None, corner, outward)

    def setup_kernel(pattern_hbm, coupling_hbm, group_hbm, blocks_hbm, *refs):
        take = taker(refs)
        flat_ref, cells_ref, corner_ref, source_ref, front_ref, kappa_ref, member_ref = (take() for _ in range(7))
        late_refs, carried_refs = take(halos), take(halos)
        pattern_ref, coupling_ref, group_ref, blocks_ref, sems, block_sems = (take() for _ in range(6))
        scalars = [
            pltpu.make_async_copy(src, dst, sems.at[i])
            for i, (src, dst) in enumerate(
                ((pattern_hbm, pattern_ref), (coupling_hbm, coupling_ref), (group_hbm, group_ref))
            )
        ]
        loads = [
            pltpu.make_async_copy(blocks_hbm.at[t], blocks_ref.at[t], block_sems.at[t]) for t in range(tiles)
        ]
        for copy in scalars + loads:
            copy.start()
        for phase in range(2):
            for x in range(tiles_x):
                for y in range(tiles_y):
                    source_ref[phase, x * tiles_y + y] = source_tile(flat_ref, cells_ref, phase, x, y)
        for pairing, rim_ref in zip(row_pairs, late_refs):
            row = Side(pairing, "row", tiles_x).edge
            rim_ref[...] = source_ref[1, pl.ds(row * tiles_y, tiles_y)]
        beyond = Side(far, "col", tiles_y)
        for h, carried_ref in enumerate(carried_refs):
            for x in range(tiles_x):
                carried_ref[x] = source_ref[1, x * tiles_y + beyond.edge]

            @pl.when(jnp.logical_not(beyond.real))
            def _(h=h, carried_ref=carried_ref):
                carried_ref[0] = corner_ref[h, 1]

        for copy in scalars:
            copy.wait()
        for t in range(tiles):
            loads[t].wait()
            for offset in range(OFFSETS):
                present = pattern_ref[t // tiles_y, t % tiles_y, offset] > 0
                front_ref[t, offset] = jnp.where(present, blocks_ref[t, offset], jnp.zeros((cells, cells), bf16))
        pos = lax.axis_index("layer")
        own = coupling_ref[group_ref[pos]]
        following = coupling_ref[group_ref[jnp.minimum(pos + 1, layers - 1)]]
        early = first_sweep() == 0
        kappa_ref[0] = jnp.full((8, cells), jnp.where(early, own, following), f32)
        kappa_ref[1] = jnp.full((8, cells), jnp.where(early, following, own), f32)
        for g in range(groups):
            for l in range(layers):
                member_ref[g, l] = jnp.full((tiles, cells), jnp.where(group_ref[l] == g, 1.0, 0.0), f32)

    source, front, kappa, member, *late = call(
        setup_kernel,
        [
            ((2, tiles, *tile), bf16),
            ((tiles, OFFSETS, cells, cells), bf16),
            ((2, 8, cells), f32),
            ((groups, layers, tiles, cells), f32),
        ]
        + [((tiles_y, *tile), bf16)] * halos
        + [((max(tiles_x, tiles_y), *tile), bf16)] * halos,
        pattern[0],
        coupling,
        layer_group,
        blocks.reshape(tiles, OFFSETS, cells, cells),
        flat,
        port_row,
        corner,
        far_args=4,
        scratch=[
            pltpu.SMEM(pattern.shape[1:], jnp.int32),
            pltpu.SMEM(coupling.shape, f32),
            pltpu.SMEM(layer_group.shape, jnp.int32),
            pltpu.VMEM((tiles, OFFSETS, cells, cells), bf16),
            pltpu.SemaphoreType.DMA((3,)),
            pltpu.SemaphoreType.DMA((tiles,)),
        ],
    )

    late = [
        to_layer(None, beside(pairing))(part)
        for part, (beside, pairing) in zip(late, [(b, p) for b in (other_row, other_chip) for p in row_pairs])
    ]

    def waves(phase, kappa_ref):
        def wave(base, field=None, real=None):
            if field is not None:
                factor = kappa_ref[phase, 0:1, :]
                base = (base.astype(f32) + factor * field.astype(f32)).astype(bf16)
            return base if real is None else jnp.where(real, base, jnp.zeros_like(base))

        return wave

    def row_real():
        return [Side(pairing, "row", tiles_x).real for pairing in row_pairs]

    def wave_kernel(step, *refs):
        take = taker(refs)
        phase = int(step >= layers // 2)
        source_ref, kappa_ref, rim_refs, column_refs = take(), take(), take(halos), take(halos)
        field_ref, field_rims, carried = None, [None] * halos, column_refs
        if step > 0:
            field_ref, field_rims, carried = take(), take(halos), take(halos)
        wave_ref, core_ref, side_ref = take(), take(), take()
        for h in range(halos):
            core_ref[ext + h] = carried[h][0]
            if step == layers // 2:
                core_ref[ext + halos + h] = column_refs[h][0]

        @pl.when(is_active(step))
        def _():
            wave = waves(phase, kappa_ref)
            real = row_real()
            for x in range(tiles_x):
                for y in range(tiles_y):
                    t = x * tiles_y + y
                    wave_ref[x, y] = wave(source_ref[phase, t], None if step == 0 else field_ref[t])
                side_ref[x] = wave(column_refs[0][x], None if step == 0 else carried[0][x])
            for h in range(halos):
                for y in range(tiles_y):
                    wave_ref[tiles_x + h, y] = wave(
                        rim_refs[h][y], None if step == 0 else field_rims[h][y], real[h]
                    )
            edge = Side(near, "col", tiles_y).edge
            for x in range(ext):
                core_ref[x] = wave_ref[x, edge]

    def product(lhs, rhs):
        return jnp.dot(lhs, rhs, preferred_element_type=f32)

    def add_column(across, sum_ref, front_ref, halo_ref):
        for x in range(tiles_x):
            t = x * tiles_y + across.edge
            reach = [a for a in (-1, 0, 1) if 0 <= x + a < tiles_x]
            lhs = jnp.concatenate([halo_ref[x + a] for a in reach], axis=1)
            rhs = jnp.concatenate([front_ref[t, 3 * (a + 1) + 1 + across.step] for a in reach], axis=0)
            sum_ref[t] += product(lhs, rhs)

    def add_corner(across, pairing, sum_ref, front_ref, corner):
        side = Side(pairing, "row", tiles_x)
        t = side.edge * tiles_y + across.edge
        sum_ref[t] += product(corner, front_ref[t, 3 * (side.step + 1) + 1 + across.step])

    def inner_kernel(step, wave_ref, side_ref, front_ref, sum_ref):
        @pl.when(is_active(step))
        def _():
            for y in range(tiles_y):
                low, high = max(y - 1, 0), min(y + 1, tiles_y - 1)
                width = high - low + 1
                first = low - y + 1
                beside = [
                    jnp.concatenate([wave_ref[x, j] for j in range(low, high + 1)], axis=1) for x in range(ext)
                ]
                for x in range(tiles_x):
                    reach = [a for a in (-1, 0, 1) if 0 <= x + a < tiles_x]
                    lhs = jnp.concatenate([beside[x + a] for a in reach], axis=1)
                    rhs = jnp.concatenate(
                        [
                            front_ref[x * tiles_y + y, 3 * (a + 1) + first : 3 * (a + 1) + first + width].reshape(
                                width * cells, cells
                            )
                            for a in reach
                        ],
                        axis=0,
                    )
                    sum_ref[x * tiles_y + y] = product(lhs, rhs)
                for h, pairing in enumerate(row_pairs):
                    side = Side(pairing, "row", tiles_x)
                    t = side.edge * tiles_y + y
                    rhs = front_ref[t, pl.ds(3 * (side.step + 1) + first, width)].reshape(width * cells, cells)
                    sum_ref[t] += product(beside[tiles_x + h], rhs)
            across = Side(far, "col", tiles_y)
            across.when(lambda: add_column(across, sum_ref, front_ref, side_ref))

    def add_far_corners(step, sum_ref, front_ref, kappa_ref, core_ref, base_ref):
        phase = int(step >= layers // 2)
        wave = waves(phase, kappa_ref)
        real = row_real()
        beyond = Side(far, "col", tiles_y)

        def corners():
            for h, pairing in enumerate(row_pairs):
                base = base_ref[ext + phase * halos + h]
                corner = wave(base, None if step == 0 else core_ref[ext + h], real[h])
                add_corner(beyond, pairing, sum_ref, front_ref, corner)

        beyond.when(corners)

    def corner_front_kernel(step, *refs):
        take = taker(refs)
        take()
        front_ref, kappa_ref, core_ref, base_ref = (take() for _ in range(4))
        if step == 1:
            take(2 * halos)
        sum_ref, corner_ref = take(), take()

        @pl.when(is_active(step))
        def _():
            add_far_corners(step, sum_ref, front_ref, kappa_ref, core_ref, base_ref)
            edge = Side(far, "col", tiles_y).edge
            for h, pairing in enumerate(row_pairs):
                row = Side(pairing, "row", tiles_x).edge
                corner_ref[h] = sum_ref[row * tiles_y + edge].astype(bf16)

    def outer_kernel(step, *refs):
        take = taker(refs)
        take()
        front_ref, core_ref = take(), take()
        last = step == layers - 1
        kappa_ref, base_ref = (take(), take()) if last else (None, None)
        earlier = take(layers - 1) if last else []
        sum_ref, field_ref, rest = take(), take(), take(halos + 1)

        @pl.when(is_active(step))
        def _():
            if last:
                add_far_corners(step, sum_ref, front_ref, kappa_ref, core_ref, base_ref)
            across = Side(near, "col", tiles_y)
            add_column(across, sum_ref, front_ref, core_ref)
            for h, pairing in enumerate(row_pairs):
                add_corner(across, pairing, sum_ref, front_ref, core_ref[tiles_x + h])
            for t in range(tiles):
                field_ref[t] = sum_ref[t].astype(bf16)
            if not last:
                edge = Side(far, "col", tiles_y).edge
                for x in range(tiles_x):
                    rest[halos][x] = field_ref[x * tiles_y + edge]
                for h, pairing in enumerate(row_pairs):
                    row = Side(pairing, "row", tiles_x).edge
                    rest[h][...] = field_ref[pl.ds(row * tiles_y, tiles_y)]

        if step == layers - 1:
            pos = lax.axis_index("layer")
            first = jnp.minimum(pos, layers - 1 - pos)
            for k in range(layers // 2):

                @pl.when(first == k)
                def _(k=k):
                    one, other = earlier[k], field_ref if k == 0 else earlier[layers - 1 - k]
                    for t in range(tiles):
                        both = one[t].astype(f32) * other[t].astype(f32)
                        rest[0][t : t + 1, :] = jnp.sum(both, axis=0, keepdims=True) * intersection_scale

    fields, field_arrived = [], []
    for step in range(layers):
        last = step == layers - 1
        wave, core, side = call(
            functools.partial(wave_kernel, step),
            [
                ((ext, tiles_y, *tile), bf16),
                ((ext + halos * (2 if step == layers // 2 else 1), *tile), bf16),
                ((tiles_x, *tile), bf16),
            ],
            source,
            kappa,
            *(source_beside if step < layers // 2 else late),
            *field_arrived,
        )
        core = to_core(core)
        (summed,) = call(
            functools.partial(inner_kernel, step), [((tiles, *tile), f32)], wave, side, front
        )
        if step in (0, layers // 2):
            base = core
        if not last:
            summed, corner = call(
                functools.partial(corner_front_kernel, step),
                [((tiles, *tile), f32), ((SPARE * halos, *tile), bf16)],
                summed,
                front,
                kappa,
                core,
                base,
                *(late if step == 1 else []),
                aliases={0: 0},
            )
            corner = to_core(corner)
        _, field, *extra = call(
            functools.partial(outer_kernel, step),
            [((tiles, *tile), f32), ((tiles, *tile), bf16)]
            + (
                [((tiles, cells), f32)]
                if last
                else [((tiles_y, *tile), bf16)] * halos + [((tiles_x, *tile), bf16)]
            ),
            summed,
            front,
            core,
            *([kappa, base, *fields] if last else []),
            aliases={0: 0},
        )
        fields.append(field)
        if not last:
            field_arrived = exchange(step, corner, extra, field)
    intersection = extra[0]

    def fields_kernel(*refs):
        field_refs, (forward_ref, adjoint_ref, flat_ref) = refs[:layers], refs[layers:]
        pos = lax.axis_index("layer")
        for out_ref, active in ((forward_ref, lambda s: s), (adjoint_ref, lambda s: layers - 1 - s)):
            for step in range(layers):

                @pl.when(pos == active(step))
                def _(step=step):
                    for t in range(tiles):
                        flat_ref[pl.ds(t, ports, stride=tiles), :] = field_refs[step][t].astype(f32)

            out_ref[...] = flat_ref[...].reshape(ports, tiles, cells).astype(bf16)

    forward, adjoint = call(
        fields_kernel,
        [((ports, tiles, cells), bf16)] * 2,
        *fields,
        scratch=[pltpu.VMEM((ports * tiles, cells), f32)],
    )

    if layers == 4:
        parts = [intersection] + [
            permuted(intersection, lambda l, r, c, m=m: (l ^ m, r, c)) for m in range(1, layers)
        ]

        def gradient_kernel(*refs):
            part_refs, member_ref, out_ref = refs[:layers], refs[layers], refs[layers + 1]
            pos = lax.axis_index("layer")
            for g in range(groups):
                total = jnp.zeros((tiles, cells), f32)
                for m in range(layers):
                    total = total + member_ref[g, pos ^ m] * part_refs[m][...]
                for x in range(tiles_x):
                    out_ref[g, x] = total[x * tiles_y : (x + 1) * tiles_y]

        (gradient,) = call(
            gradient_kernel, [((groups, tiles_x, tiles_y, cells), f32)], *parts, member
        )
    else:
        selected = lax.dynamic_index_in_dim(member, lax.axis_index("layer"), 1, keepdims=False)
        gradient = lax.psum(selected * intersection[None], "layer").reshape(groups, tiles_x, tiles_y, cells)
    shape = (1, ports, tiles_x, tiles_y, cells)
    return (forward.reshape(shape), adjoint.reshape(shape), gradient)


def solution(mesh):
    placed = (
        P("layer", None, "row", "col", None),
        P("layer", None, "row", "col", None),
        P("layer", "row", "col", None, None, None),
        P("layer", "row", "col", None),
        P(),
        P(),
        P(),
    )
    return jax.shard_map(
        local,
        mesh=mesh,
        in_specs=placed,
        out_specs=(
            P("layer", None, "row", "col", None),
            P("layer", None, "row", "col", None),
            P(None, "row", "col", None),
        ),
        check_vma=False,
    )
```

```python
import functools

import jax
import jax.numpy as jnp
from jax import lax
from jax.experimental import pallas as pl
from jax.experimental.pallas import tpu as pltpu
from jax.sharding import PartitionSpec as P

port_strength = 4.0
intersection_scale = 0.125
AXES = ("layer", "row", "col")
OFFSETS = 9
VMEM_BYTES = 24 * 1024 * 1024
SPARE = 2

VM = pl.BlockSpec(memory_space=pltpu.VMEM)


def call(kernel, outs, *args, far_args=0, scratch=(), aliases=None):
    args = [pltpu.with_memory_space_constraint(a, pltpu.HBM) for a in args[:far_args]] + list(args[far_args:])
    return pl.pallas_call(
        kernel,
        out_shape=[jax.ShapeDtypeStruct(shape, dtype) for shape, dtype in outs],
        in_specs=[pl.BlockSpec(memory_space=pltpu.HBM)] * far_args + [VM] * (len(args) - far_args),
        out_specs=[VM] * len(outs),
        scratch_shapes=list(scratch),
        input_output_aliases=aliases or {},
        compiler_params=pltpu.CompilerParams(vmem_limit_bytes=VMEM_BYTES),
    )(*args)


def near(i, n):
    return i ^ 1


def far(i, n):
    return (((i + 1) ^ 1) - 1) % n


def pairings(n):
    return [near] if n == 2 else [near, far]


class Side:
    def __init__(self, pairing, axis, tiles):
        pos, count = lax.axis_index(axis), lax.axis_size(axis)
        even = lax.rem(pos, 2) == 0
        after = even if pairing is near else jnp.logical_not(even)
        self.step = jnp.where(after, 1, -1)
        self.edge = jnp.where(after, tiles - 1, 0)
        self.real = None
        if pairing is far:
            self.real = jnp.logical_not(
                jnp.logical_or(jnp.logical_and(after, pos == count - 1), jnp.logical_and(jnp.logical_not(after), pos == 0))
            )

    def when(self, body):
        if self.real is None:
            body()
        else:
            pl.when(self.real)(body)


def local(sources, adjoint_sources, blocks, pattern, coupling, layer_group, port_cells):
    ports, tiles_x, tiles_y, cells = sources.shape[1:]
    tiles = tiles_x * tiles_y
    groups = coupling.shape[0]
    layers, rows, cols = (lax.axis_size(axis) for axis in AXES)
    if cols != 4 or layers % 2 or rows % 2:
        raise ValueError("unsupported mesh")
    row_pairs = pairings(rows)
    halos = len(row_pairs)
    ext = tiles_x + halos
    bf16, f32 = jnp.bfloat16, jnp.float32
    tile = (ports, cells)

    def permuted(array, target):
        pairs = []
        for l in range(layers):
            for r in range(rows):
                for c in range(cols):
                    a, b, d = target(l, r, c)
                    pairs.append(((l * rows + r) * cols + c, (a * rows + b) * cols + d))
        return lax.ppermute(array, AXES, pairs)

    def to_core(array):
        return permuted(array, lambda l, r, c: (l, r, near(c, cols)))

    def to_layer(step, beside):
        def target(l, r, c):
            if step is None:
                return l, *beside(r, c)
            a = (near if step % 2 == 0 else far)(l, layers)
            return (a, *beside(r, c)) if abs(a - l) == 1 else (l, r, near(c, cols))

        return lambda array: permuted(array, target)

    def same(r, c):
        return r, c

    def other_row(pairing):
        return lambda r, c: (pairing(r, rows), c)

    def other_chip(pairing):
        def beside(r, c):
            d = far(c, cols)
            return (r if abs(d - c) == 1 else pairing(r, rows)), d

        return beside

    def is_active(step):
        pos = lax.axis_index("layer")
        return jnp.logical_or(pos == step, pos == layers - 1 - step)

    def taker(refs):
        refs = list(refs)

        def take(count=None):
            taken = refs[: 1 if count is None else count]
            del refs[: len(taken)]
            return taken[0] if count is None else taken

        return take

    def first_sweep():
        return jnp.where(lax.axis_index("layer") < layers // 2, 0, 1)

    def port_map(cells_ref, x, y):
        x_pos = lax.axis_index("row") * tiles_x + x
        y_pos = lax.axis_index("col") * tiles_y + y
        first = (x_pos * (tiles_y * cols) + y_pos) * cells
        row = jnp.broadcast_to(cells_ref[...], (ports, ports))
        diagonal = lax.broadcasted_iota(jnp.int32, (ports, ports), 0) == lax.broadcasted_iota(
            jnp.int32, (ports, ports), 1
        )
        column = jnp.sum(jnp.where(diagonal, row, 0), axis=1, keepdims=True)
        lane = lax.broadcasted_iota(jnp.int32, tile, 1)
        return jnp.where(column - first == lane, port_strength, 0.0).astype(f32)

    def source_tile(flat_ref, cells_ref, phase, x, y):
        value = flat_ref[phase, pl.ds(x * tiles_y + y, ports, stride=tiles), :]
        if phase == 0:
            pos = lax.axis_index("layer")
            end = jnp.logical_or(pos == 0, pos == layers - 1)
            value = value + jnp.where(end, port_map(cells_ref, x, y), 0.0)
        return value.astype(bf16)

    def corner_kernel(forward_hbm, adjoint_hbm, cells_hbm, flat_ref, cells_ref, corner_ref, raw_ref, sems):
        copies = [
            pltpu.make_async_copy(src, dst, sems.at[i])
            for i, (src, dst) in enumerate(
                ((forward_hbm, raw_ref.at[0]), (adjoint_hbm, raw_ref.at[1]), (cells_hbm, cells_ref))
            )
        ]
        for copy in copies:
            copy.start()
        for copy in copies:
            copy.wait()
        edge = Side(far, "col", tiles_y).edge
        for phase in range(2):
            flat_ref[phase] = raw_ref[first_sweep() ^ phase].astype(f32).reshape(ports * tiles, cells)
            for h, pairing in enumerate(row_pairs):
                row = Side(pairing, "row", tiles_x).edge
                corner_ref[h, phase] = source_tile(flat_ref, cells_ref, phase, row, edge)

    def rims_kernel(flat_ref, cells_ref, *refs):
        take = taker(refs)
        rim_refs, column_ref = take(halos), take()
        edge = Side(far, "col", tiles_y).edge
        for x in range(tiles_x):
            column_ref[x] = source_tile(flat_ref, cells_ref, 0, x, edge)
        for h, pairing in enumerate(row_pairs):
            row = Side(pairing, "row", tiles_x).edge
            for y in range(tiles_y):
                rim_refs[h][y] = source_tile(flat_ref, cells_ref, 0, row, y)

    raw_shape = (ports, tiles, cells)
    flat, port_row, corner = call(
        corner_kernel,
        [((2, ports * tiles, cells), f32), ((1, ports), jnp.int32), ((SPARE * halos, 2, *tile), bf16)],
        sources.reshape(raw_shape),
        adjoint_sources.reshape(raw_shape),
        port_cells.reshape(1, ports),
        far_args=3,
        scratch=[pltpu.VMEM((2, *raw_shape), bf16), pltpu.SemaphoreType.DMA((3,))],
    )
    corner = to_core(corner)
    outward = call(rims_kernel, [((tiles_y, *tile), bf16)] * halos + [((tiles_x, *tile), bf16)], flat, port_row)

    def relay_kernel(phase, *refs):
        take = taker(refs)
        column_ref, corner_ref, out_refs = take(), take(), take(halos)
        inner = Side(far, "col", tiles_y).real

        @pl.when(inner)
        def _():
            for out_ref in out_refs:
                out_ref[:tiles_x] = column_ref[...]

        @pl.when(jnp.logical_not(inner))
        def _():
            for h, out_ref in enumerate(out_refs):
                out_ref[0] = corner_ref[h] if phase is None else corner_ref[h, phase]

    def exchange(step, corner, outward, field=None):
        rims, column = outward[:halos], outward[halos]
        arrived = [] if field is None else [to_layer(step, same)(field)]
        arrived += [to_layer(step, other_row(pairing))(rim) for rim, pairing in zip(rims, row_pairs)]
        kernel = functools.partial(relay_kernel, 0 if step is None else None)
        carried = call(kernel, [(column.shape, bf16)] * halos, column, corner)
        return arrived + [to_layer(step, other_chip(pairing))(part) for part, pairing in zip(carried, row_pairs)]

    source_beside = exchange(None, corner, outward)

    def setup_kernel(pattern_hbm, coupling_hbm, group_hbm, blocks_hbm, *refs):
        take = taker(refs)
        flat_ref, cells_ref, corner_ref, source_ref, front_ref, kappa_ref, member_ref = (take() for _ in range(7))
        late_refs, carried_refs = take(halos), take(halos)
        pattern_ref, coupling_ref, group_ref, blocks_ref, sems, block_sems = (take() for _ in range(6))
        scalars = [
            pltpu.make_async_copy(src, dst, sems.at[i])
            for i, (src, dst) in enumerate(
                ((pattern_hbm, pattern_ref), (coupling_hbm, coupling_ref), (group_hbm, group_ref))
            )
        ]
        loads = [
            pltpu.make_async_copy(blocks_hbm.at[t], blocks_ref.at[t], block_sems.at[t]) for t in range(tiles)
        ]
        for copy in scalars + loads:
            copy.start()
        for phase in range(2):
            for x in range(tiles_x):
                for y in range(tiles_y):
                    source_ref[phase, x * tiles_y + y] = source_tile(flat_ref, cells_ref, phase, x, y)
        for pairing, rim_ref in zip(row_pairs, late_refs):
            row = Side(pairing, "row", tiles_x).edge
            rim_ref[...] = source_ref[1, pl.ds(row * tiles_y, tiles_y)]
        beyond = Side(far, "col", tiles_y)
        for h, carried_ref in enumerate(carried_refs):
            for x in range(tiles_x):
                carried_ref[x] = source_ref[1, x * tiles_y + beyond.edge]

            @pl.when(jnp.logical_not(beyond.real))
            def _(h=h, carried_ref=carried_ref):
                carried_ref[0] = corner_ref[h, 1]

        for copy in scalars:
            copy.wait()
        for t in range(tiles):
            loads[t].wait()
            for offset in range(OFFSETS):
                present = pattern_ref[t // tiles_y, t % tiles_y, offset] > 0
                front_ref[t, offset] = jnp.where(present, blocks_ref[t, offset], jnp.zeros((cells, cells), bf16))
        pos = lax.axis_index("layer")
        own = coupling_ref[group_ref[pos]]
        following = coupling_ref[group_ref[jnp.minimum(pos + 1, layers - 1)]]
        early = first_sweep() == 0
        kappa_ref[0] = jnp.full((8, cells), jnp.where(early, own, following), f32)
        kappa_ref[1] = jnp.full((8, cells), jnp.where(early, following, own), f32)
        for g in range(groups):
            for l in range(layers):
                member_ref[g, l] = jnp.full((tiles, cells), jnp.where(group_ref[l] == g, 1.0, 0.0), f32)

    source, front, kappa, member, *late = call(
        setup_kernel,
        [
            ((2, tiles, *tile), bf16),
            ((tiles, OFFSETS, cells, cells), bf16),
            ((2, 8, cells), f32),
            ((groups, layers, tiles, cells), f32),
        ]
        + [((tiles_y, *tile), bf16)] * halos
        + [((max(tiles_x, tiles_y), *tile), bf16)] * halos,
        pattern[0],
        coupling,
        layer_group,
        blocks.reshape(tiles, OFFSETS, cells, cells),
        flat,
        port_row,
        corner,
        far_args=4,
        scratch=[
            pltpu.SMEM(pattern.shape[1:], jnp.int32),
            pltpu.SMEM(coupling.shape, f32),
            pltpu.SMEM(layer_group.shape, jnp.int32),
            pltpu.VMEM((tiles, OFFSETS, cells, cells), bf16),
            pltpu.SemaphoreType.DMA((3,)),
            pltpu.SemaphoreType.DMA((tiles,)),
        ],
    )

    late = [
        to_layer(None, beside(pairing))(part)
        for part, (beside, pairing) in zip(late, [(b, p) for b in (other_row, other_chip) for p in row_pairs])
    ]

    def waves(phase, kappa_ref):
        def wave(base, field=None, real=None):
            if field is not None:
                factor = kappa_ref[phase, 0:1, :]
                base = (base.astype(f32) + factor * field.astype(f32)).astype(bf16)
            return base if real is None else jnp.where(real, base, jnp.zeros_like(base))

        return wave

    def row_real():
        return [Side(pairing, "row", tiles_x).real for pairing in row_pairs]

    def step_inputs(step, take):
        source_ref, kappa_ref, rim_refs, column_refs = take(), take(), take(halos), take(halos)
        if step == 0:
            return source_ref, kappa_ref, rim_refs, column_refs, None, [None] * halos, column_refs
        return source_ref, kappa_ref, rim_refs, column_refs, take(), take(halos), take(halos)

    def core_kernel(step, *refs):
        take = taker(refs)
        phase = int(step >= layers // 2)
        source_ref, kappa_ref, rim_refs, column_refs, field_ref, field_rims, carried = step_inputs(step, take)
        core_ref = take()
        for h in range(halos):
            core_ref[ext + h] = carried[h][0]
            if step == layers // 2:
                core_ref[ext + halos + h] = column_refs[h][0]

        @pl.when(is_active(step))
        def _():
            wave = waves(phase, kappa_ref)
            real = row_real()
            edge = Side(near, "col", tiles_y).edge
            for x in range(tiles_x):
                t = x * tiles_y + edge
                core_ref[x] = wave(source_ref[phase, t], None if step == 0 else field_ref[t])
            for h in range(halos):
                core_ref[tiles_x + h] = wave(
                    rim_refs[h][edge], None if step == 0 else field_rims[h][edge], real[h]
                )

    def product(lhs, rhs):
        return jnp.dot(lhs, rhs, preferred_element_type=f32)

    def column_products(across, front_ref, halo_ref):
        totals = []
        for x in range(tiles_x):
            t = x * tiles_y + across.edge
            reach = [a for a in (-1, 0, 1) if 0 <= x + a < tiles_x]
            lhs = jnp.concatenate([halo_ref[x + a] for a in reach], axis=1)
            rhs = jnp.concatenate([front_ref[t, 3 * (a + 1) + 1 + across.step] for a in reach], axis=0)
            totals.append(product(lhs, rhs))
        return totals

    def corner_product(across, pairing, front_ref, corner):
        side = Side(pairing, "row", tiles_x)
        t = side.edge * tiles_y + across.edge
        return t, product(corner, front_ref[t, 3 * (side.step + 1) + 1 + across.step])

    def early_tiles():
        edge = Side(far, "col", tiles_y).edge
        inside = [(x, y) for x in range(tiles_x) for y in range(1, tiles_y - 1)]
        if halos > 1:
            return inside + [(x, edge) for x in range(1, tiles_x - 1)]
        low = jnp.where(Side(near, "row", tiles_x).edge == 0, 1, 0)
        return inside + [(low + i, edge) for i in range(tiles_x - 1)]

    def late_tiles():
        beside, beyond = (Side(pairing, "col", tiles_y).edge for pairing in (near, far))
        corners = [(Side(pairing, "row", tiles_x).edge, beyond) for pairing in row_pairs]
        return [(x, beside) for x in range(tiles_x)] + corners

    def add_parts(some, one_ref, other_ref, part_ref):
        for x, y in some:
            t = x * tiles_y + y
            both = one_ref[t].astype(f32) * other_ref[t].astype(f32)
            part_ref[pl.ds(t, 1), :] = jnp.sum(both, axis=0, keepdims=True) * intersection_scale

    def inner_kernel(step, *refs):
        take = taker(refs)
        phase, last = int(step >= layers // 2), step == layers - 1
        source_ref, kappa_ref, rim_refs, column_refs, field_ref, field_rims, carried = step_inputs(step, take)
        take()
        front_ref, earlier = take(), take(layers - 1 if last else 0)
        sum_ref, out_ref, rest, wave_ref, side_ref = take(), take(), take(1 if last else halos + 1), take(), take()

        @pl.when(is_active(step))
        def _():
            wave = waves(phase, kappa_ref)
            real = row_real()
            for x in range(tiles_x):
                for y in range(tiles_y):
                    t = x * tiles_y + y
                    wave_ref[x, y] = wave(source_ref[phase, t], None if step == 0 else field_ref[t])
                side_ref[x] = wave(column_refs[0][x], None if step == 0 else carried[0][x])
            for h in range(halos):
                for y in range(tiles_y):
                    wave_ref[tiles_x + h, y] = wave(
                        rim_refs[h][y], None if step == 0 else field_rims[h][y], real[h]
                    )
            for y in range(tiles_y):
                low, high = max(y - 1, 0), min(y + 1, tiles_y - 1)
                width = high - low + 1
                first = low - y + 1
                beside = [
                    jnp.concatenate([wave_ref[x, j] for j in range(low, high + 1)], axis=1) for x in range(ext)
                ]
                for x in range(tiles_x):
                    reach = [a for a in (-1, 0, 1) if 0 <= x + a < tiles_x]
                    lhs = jnp.concatenate([beside[x + a] for a in reach], axis=1)
                    rhs = jnp.concatenate(
                        [
                            front_ref[x * tiles_y + y, 3 * (a + 1) + first : 3 * (a + 1) + first + width].reshape(
                                width * cells, cells
                            )
                            for a in reach
                        ],
                        axis=0,
                    )
                    sum_ref[x * tiles_y + y] = product(lhs, rhs)
                for h, pairing in enumerate(row_pairs):
                    side = Side(pairing, "row", tiles_x)
                    t = side.edge * tiles_y + y
                    rhs = front_ref[t, pl.ds(3 * (side.step + 1) + first, width)].reshape(width * cells, cells)
                    sum_ref[t] += product(beside[tiles_x + h], rhs)
            across = Side(far, "col", tiles_y)

            def beyond():
                for x, total in enumerate(column_products(across, front_ref, side_ref)):
                    sum_ref[x * tiles_y + across.edge] += total

            across.when(beyond)
            some = early_tiles()
            for x, y in some:
                out_ref[x * tiles_y + y] = sum_ref[x * tiles_y + y].astype(bf16)
            if last:
                add_parts(some, earlier[0], out_ref, rest[0])
            else:
                for x in range(tiles_x):
                    rest[halos][x] = out_ref[x * tiles_y + across.edge]
                for h, pairing in enumerate(row_pairs):
                    row = Side(pairing, "row", tiles_x).edge
                    rest[h][1 : tiles_y - 1] = out_ref[pl.ds(row * tiles_y + 1, tiles_y - 2)]

        if last:
            pos = lax.axis_index("layer")
            first = jnp.minimum(pos, layers - 1 - pos)
            whole = [(x, y) for x in range(tiles_x) for y in range(tiles_y)]
            for k in range(1, layers // 2):

                @pl.when(first == k)
                def _(k=k):
                    add_parts(whole, earlier[k], earlier[layers - 1 - k], rest[0])

    def add_far_corners(step, sum_ref, front_ref, kappa_ref, core_ref, base_ref):
        phase = int(step >= layers // 2)
        wave = waves(phase, kappa_ref)
        real = row_real()
        beyond = Side(far, "col", tiles_y)

        def corners():
            for h, pairing in enumerate(row_pairs):
                base = base_ref[ext + phase * halos + h]
                corner = wave(base, None if step == 0 else core_ref[ext + h], real[h])
                t, total = corner_product(beyond, pairing, front_ref, corner)
                sum_ref[t] += total

        beyond.when(corners)

    def corner_front_kernel(step, *refs):
        take = taker(refs)
        take()
        front_ref, kappa_ref, core_ref, base_ref = (take() for _ in range(4))
        if step == 1:
            take(2 * halos)
        sum_ref, corner_ref = take(), take()

        @pl.when(is_active(step))
        def _():
            add_far_corners(step, sum_ref, front_ref, kappa_ref, core_ref, base_ref)
            edge = Side(far, "col", tiles_y).edge
            for h, pairing in enumerate(row_pairs):
                row = Side(pairing, "row", tiles_x).edge
                corner_ref[h] = sum_ref[row * tiles_y + edge].astype(bf16)

    def outer_kernel(step, *refs):
        take = taker(refs)
        last = step == layers - 1
        take(2 + (1 if last else halos + 1))
        front_ref, core_ref = take(), take()
        kappa_ref, base_ref, first_ref = (take(), take(), take()) if last else (None, None, None)
        sum_ref, field_ref, rest = take(), take(), take(1 if last else halos + 1)

        @pl.when(is_active(step))
        def _():
            if last:
                add_far_corners(step, sum_ref, front_ref, kappa_ref, core_ref, base_ref)
            across, beyond = Side(near, "col", tiles_y), Side(far, "col", tiles_y)
            totals = column_products(across, front_ref, core_ref)
            corners = [
                corner_product(across, pairing, front_ref, core_ref[tiles_x + h])[1]
                for h, pairing in enumerate(row_pairs)
            ]
            edges = [Side(pairing, "row", tiles_x).edge for pairing in row_pairs]
            for x, total in enumerate(totals):
                t = x * tiles_y + across.edge
                total = sum_ref[t] + total
                for edge, corner in zip(edges, corners):
                    total = total + jnp.where(edge == x, corner, 0.0)
                field_ref[t] = total.astype(bf16)
            for edge in edges:
                t = edge * tiles_y + beyond.edge
                field_ref[t] = sum_ref[t].astype(bf16)
            some = late_tiles()
            if last:
                add_parts(some, first_ref, field_ref, rest[0])
            else:
                for h, pairing in enumerate(row_pairs):
                    row = Side(pairing, "row", tiles_x).edge
                    rest[halos][row] = field_ref[row * tiles_y + beyond.edge]
                    for edge in (across.edge, beyond.edge):
                        rest[h][edge] = field_ref[row * tiles_y + edge]

    fields, field_arrived = [], []
    for step in range(layers):
        last = step == layers - 1
        inputs = [source, kappa, *(source_beside if step < layers // 2 else late), *field_arrived]
        (core_out,) = call(
            functools.partial(core_kernel, step),
            [((ext + halos * (2 if step == layers // 2 else 1), *tile), bf16)],
            *inputs,
        )
        core = to_core(core_out)
        summed, *partial_out = call(
            functools.partial(inner_kernel, step),
            [((tiles, *tile), f32), ((tiles, *tile), bf16)]
            + ([((tiles, cells), f32)] if last else [((tiles_y, *tile), bf16)] * halos + [((tiles_x, *tile), bf16)]),
            *inputs,
            core_out,
            front,
            *(fields if last else []),
            scratch=[pltpu.VMEM((ext, tiles_y, *tile), bf16), pltpu.VMEM((tiles_x, *tile), bf16)],
        )
        if step in (0, layers // 2):
            base = core
        if not last:
            summed, corner = call(
                functools.partial(corner_front_kernel, step),
                [((tiles, *tile), f32), ((SPARE * halos, *tile), bf16)],
                summed,
                front,
                kappa,
                core,
                base,
                *(late if step == 1 else []),
                aliases={0: 0},
            )
            corner = to_core(corner)
        _, field, *extra = call(
            functools.partial(outer_kernel, step),
            [(part.shape, part.dtype) for part in (summed, *partial_out)],
            summed,
            *partial_out,
            front,
            core,
            *([kappa, base, fields[0]] if last else []),
            aliases={i: i for i in range(1 + len(partial_out))},
        )
        fields.append(field)
        if not last:
            field_arrived = exchange(step, corner, extra, field)
    intersection = extra[0]

    def fields_kernel(*refs):
        field_refs, (forward_ref, adjoint_ref, flat_ref) = refs[:layers], refs[layers:]
        pos = lax.axis_index("layer")
        for out_ref, active in ((forward_ref, lambda s: s), (adjoint_ref, lambda s: layers - 1 - s)):
            for step in range(layers):

                @pl.when(pos == active(step))
                def _(step=step):
                    for t in range(tiles):
                        flat_ref[pl.ds(t, ports, stride=tiles), :] = field_refs[step][t].astype(f32)

            out_ref[...] = flat_ref[...].reshape(ports, tiles, cells).astype(bf16)

    forward, adjoint = call(
        fields_kernel,
        [((ports, tiles, cells), bf16)] * 2,
        *fields,
        scratch=[pltpu.VMEM((ports * tiles, cells), f32)],
    )

    if layers == 4:
        parts = [intersection] + [
            permuted(intersection, lambda l, r, c, m=m: (l ^ m, r, c)) for m in range(1, layers)
        ]

        def gradient_kernel(*refs):
            part_refs, member_ref, out_ref = refs[:layers], refs[layers], refs[layers + 1]
            pos = lax.axis_index("layer")
            for g in range(groups):
                total = jnp.zeros((tiles, cells), f32)
                for m in range(layers):
                    total = total + member_ref[g, pos ^ m] * part_refs[m][...]
                for x in range(tiles_x):
                    out_ref[g, x] = total[x * tiles_y : (x + 1) * tiles_y]

        (gradient,) = call(
            gradient_kernel, [((groups, tiles_x, tiles_y, cells), f32)], *parts, member
        )
    else:
        selected = lax.dynamic_index_in_dim(member, lax.axis_index("layer"), 1, keepdims=False)
        gradient = lax.psum(selected * intersection[None], "layer").reshape(groups, tiles_x, tiles_y, cells)
    shape = (1, ports, tiles_x, tiles_y, cells)
    return (forward.reshape(shape), adjoint.reshape(shape), gradient)


def solution(mesh):
    placed = (
        P("layer", None, "row", "col", None),
        P("layer", None, "row", "col", None),
        P("layer", "row", "col", None, None, None),
        P("layer", "row", "col", None),
        P(),
        P(),
        P(),
    )
    return jax.shard_map(
        local,
        mesh=mesh,
        in_specs=placed,
        out_specs=(
            P("layer", None, "row", "col", None),
            P("layer", None, "row", "col", None),
            P(None, "row", "col", None),
        ),
        check_vma=False,
    )
```

```python
import functools

import jax
import jax.numpy as jnp
from jax import lax
from jax.experimental import pallas as pl
from jax.experimental.pallas import tpu as pltpu
from jax.sharding import PartitionSpec as P

port_strength = 4.0
intersection_scale = 0.125
AXES = ("layer", "row", "col")
OFFSETS = 9
VMEM_BYTES = 24 * 1024 * 1024
BESIDE = 16
SPARE = 2

VM = pl.BlockSpec(memory_space=pltpu.VMEM)


def call(kernel, outs, *args, far_args=0, scratch=(), aliases=None):
    args = [pltpu.with_memory_space_constraint(a, pltpu.HBM) for a in args[:far_args]] + list(args[far_args:])
    return pl.pallas_call(
        kernel,
        out_shape=[jax.ShapeDtypeStruct(shape, dtype) for shape, dtype in outs],
        in_specs=[pl.BlockSpec(memory_space=pltpu.HBM)] * far_args + [VM] * (len(args) - far_args),
        out_specs=[VM] * len(outs),
        scratch_shapes=list(scratch),
        input_output_aliases=aliases or {},
        compiler_params=pltpu.CompilerParams(vmem_limit_bytes=VMEM_BYTES),
    )(*args)


def near(i, n):
    return i ^ 1


def far(i, n):
    return (((i + 1) ^ 1) - 1) % n


def pairings(n):
    return [near] if n == 2 else [near, far]


class Side:
    def __init__(self, pairing, axis, tiles):
        pos, count = lax.axis_index(axis), lax.axis_size(axis)
        even = lax.rem(pos, 2) == 0
        after = even if pairing is near else jnp.logical_not(even)
        self.step = jnp.where(after, 1, -1)
        self.edge = jnp.where(after, tiles - 1, 0)
        self.real = None
        if pairing is far:
            self.real = jnp.logical_not(
                jnp.logical_or(jnp.logical_and(after, pos == count - 1), jnp.logical_and(jnp.logical_not(after), pos == 0))
            )

    def when(self, body):
        if self.real is None:
            body()
        else:
            pl.when(self.real)(body)


def local(sources, adjoint_sources, blocks, pattern, coupling, layer_group, port_cells):
    ports, tiles_x, tiles_y, cells = sources.shape[1:]
    tiles = tiles_x * tiles_y
    groups = coupling.shape[0]
    layers, rows, cols = (lax.axis_size(axis) for axis in AXES)
    if cols != 4 or layers % 2 or rows % 2:
        raise ValueError("unsupported mesh")
    row_pairs = pairings(rows)
    halos = len(row_pairs)
    ext = tiles_x + halos
    bf16, f32 = jnp.bfloat16, jnp.float32
    tile = (ports, cells)

    def permuted(array, target):
        pairs = []
        for l in range(layers):
            for r in range(rows):
                for c in range(cols):
                    a, b, d = target(l, r, c)
                    pairs.append(((l * rows + r) * cols + c, (a * rows + b) * cols + d))
        return lax.ppermute(array, AXES, pairs)

    def to_core(array):
        return permuted(array, lambda l, r, c: (l, r, near(c, cols)))

    def to_layer(step, beside):
        def target(l, r, c):
            if step is None:
                return l, *beside(r, c)
            a = (near if step % 2 == 0 else far)(l, layers)
            return (a, *beside(r, c)) if abs(a - l) == 1 else (l, r, near(c, cols))

        return lambda array: permuted(array, target)

    def same(r, c):
        return r, c

    def other_row(pairing):
        return lambda r, c: (pairing(r, rows), c)

    def other_chip(pairing):
        def beside(r, c):
            d = far(c, cols)
            return (r if abs(d - c) == 1 else pairing(r, rows)), d

        return beside

    def is_active(step):
        pos = lax.axis_index("layer")
        return jnp.logical_or(pos == step, pos == layers - 1 - step)

    def taker(refs):
        refs = list(refs)

        def take(count=None):
            taken = refs[: 1 if count is None else count]
            del refs[: len(taken)]
            return taken[0] if count is None else taken

        return take

    def first_sweep():
        return jnp.where(lax.axis_index("layer") < layers // 2, 0, 1)

    def port_map(cells_ref, x, y):
        x_pos = lax.axis_index("row") * tiles_x + x
        y_pos = lax.axis_index("col") * tiles_y + y
        first = (x_pos * (tiles_y * cols) + y_pos) * cells
        row = jnp.broadcast_to(cells_ref[...], (ports, ports))
        diagonal = lax.broadcasted_iota(jnp.int32, (ports, ports), 0) == lax.broadcasted_iota(
            jnp.int32, (ports, ports), 1
        )
        column = jnp.sum(jnp.where(diagonal, row, 0), axis=1, keepdims=True)
        lane = lax.broadcasted_iota(jnp.int32, tile, 1)
        return jnp.where(column - first == lane, port_strength, 0.0).astype(f32)

    def source_tile(flat_ref, cells_ref, phase, x, y):
        value = flat_ref[phase, pl.ds(x * tiles_y + y, ports, stride=tiles), :]
        if phase == 0:
            pos = lax.axis_index("layer")
            end = jnp.logical_or(pos == 0, pos == layers - 1)
            value = value + jnp.where(end, port_map(cells_ref, x, y), 0.0)
        return value.astype(bf16)

    def corner_kernel(forward_hbm, adjoint_hbm, cells_hbm, flat_ref, cells_ref, corner_ref, raw_ref, sems):
        copies = [
            pltpu.make_async_copy(src, dst, sems.at[i])
            for i, (src, dst) in enumerate(
                ((forward_hbm, raw_ref.at[0]), (adjoint_hbm, raw_ref.at[1]), (cells_hbm, cells_ref))
            )
        ]
        for copy in copies:
            copy.start()
        for copy in copies:
            copy.wait()
        edge = Side(far, "col", tiles_y).edge
        for phase in range(2):
            flat_ref[phase] = raw_ref[first_sweep() ^ phase].astype(f32).reshape(ports * tiles, cells)
            for h, pairing in enumerate(row_pairs):
                row = Side(pairing, "row", tiles_x).edge
                corner_ref[h, phase] = source_tile(flat_ref, cells_ref, phase, row, edge)

    def rims_kernel(flat_ref, cells_ref, *refs):
        take = taker(refs)
        rim_refs, column_ref = take(halos), take()
        edge = Side(far, "col", tiles_y).edge
        for x in range(tiles_x):
            column_ref[x] = source_tile(flat_ref, cells_ref, 0, x, edge)
        for h, pairing in enumerate(row_pairs):
            row = Side(pairing, "row", tiles_x).edge
            for y in range(tiles_y):
                rim_refs[h][y] = source_tile(flat_ref, cells_ref, 0, row, y)

    raw_shape = (ports, tiles, cells)
    flat, port_row, corner = call(
        corner_kernel,
        [((2, ports * tiles, cells), f32), ((1, ports), jnp.int32), ((SPARE * halos, 2, *tile), bf16)],
        sources.reshape(raw_shape),
        adjoint_sources.reshape(raw_shape),
        port_cells.reshape(1, ports),
        far_args=3,
        scratch=[pltpu.VMEM((2, *raw_shape), bf16), pltpu.SemaphoreType.DMA((3,))],
    )
    corner = to_core(corner)
    outward = call(rims_kernel, [((tiles_y, *tile), bf16)] * halos + [((tiles_x, *tile), bf16)], flat, port_row)

    def relay_kernel(phase, *refs):
        take = taker(refs)
        column_ref, corner_ref, out_refs = take(), take(), take(halos)
        inner = Side(far, "col", tiles_y).real

        @pl.when(inner)
        def _():
            for out_ref in out_refs:
                out_ref[:tiles_x] = column_ref[...]

        @pl.when(jnp.logical_not(inner))
        def _():
            for h, out_ref in enumerate(out_refs):
                out_ref[0] = corner_ref[h] if phase is None else corner_ref[h, phase]

    def exchange(step, corner, outward, field=None):
        rims, column = outward[:halos], outward[halos]
        arrived = [] if field is None else [to_layer(step, same)(field)]
        arrived += [to_layer(step, other_row(pairing))(rim) for rim, pairing in zip(rims, row_pairs)]
        kernel = functools.partial(relay_kernel, 0 if step is None else None)
        carried = call(kernel, [(column.shape, bf16)] * halos, column, corner)
        return arrived + [to_layer(step, other_chip(pairing))(part) for part, pairing in zip(carried, row_pairs)]

    source_beside = exchange(None, corner, outward)

    def setup_kernel(pattern_hbm, coupling_hbm, group_hbm, blocks_hbm, *refs):
        take = taker(refs)
        flat_ref, cells_ref, corner_ref, source_ref, front_ref, kappa_ref, member_ref = (take() for _ in range(7))
        late_refs, carried_refs = take(halos), take(halos)
        pattern_ref, coupling_ref, group_ref, blocks_ref, sems, block_sems = (take() for _ in range(6))
        scalars = [
            pltpu.make_async_copy(src, dst, sems.at[i])
            for i, (src, dst) in enumerate(
                ((pattern_hbm, pattern_ref), (coupling_hbm, coupling_ref), (group_hbm, group_ref))
            )
        ]
        loads = [
            pltpu.make_async_copy(blocks_hbm.at[t], blocks_ref.at[t], block_sems.at[t]) for t in range(tiles)
        ]
        for copy in scalars + loads:
            copy.start()
        for phase in range(2):
            for x in range(tiles_x):
                for y in range(tiles_y):
                    source_ref[phase, x * tiles_y + y] = source_tile(flat_ref, cells_ref, phase, x, y)
        for pairing, rim_ref in zip(row_pairs, late_refs):
            row = Side(pairing, "row", tiles_x).edge
            rim_ref[...] = source_ref[1, pl.ds(row * tiles_y, tiles_y)]
        beyond = Side(far, "col", tiles_y)
        for h, carried_ref in enumerate(carried_refs):
            for x in range(tiles_x):
                carried_ref[x] = source_ref[1, x * tiles_y + beyond.edge]

            @pl.when(jnp.logical_not(beyond.real))
            def _(h=h, carried_ref=carried_ref):
                carried_ref[0] = corner_ref[h, 1]

        for copy in scalars:
            copy.wait()
        for t in range(tiles):
            loads[t].wait()
            for offset in range(OFFSETS):
                present = pattern_ref[t // tiles_y, t % tiles_y, offset] > 0
                front_ref[t, offset] = jnp.where(present, blocks_ref[t, offset], jnp.zeros((cells, cells), bf16))
        pos = lax.axis_index("layer")
        own = coupling_ref[group_ref[pos]]
        following = coupling_ref[group_ref[jnp.minimum(pos + 1, layers - 1)]]
        early = first_sweep() == 0
        kappa_ref[0] = jnp.full((8, cells), jnp.where(early, own, following), f32)
        kappa_ref[1] = jnp.full((8, cells), jnp.where(early, following, own), f32)
        for g in range(groups):
            for l in range(layers):
                member_ref[g, l] = jnp.full((tiles, cells), jnp.where(group_ref[l] == g, 1.0, 0.0), f32)

    source, front, kappa, member, *late = call(
        setup_kernel,
        [
            ((2, tiles, *tile), bf16),
            ((tiles, OFFSETS, cells, cells), bf16),
            ((2, 8, cells), f32),
            ((groups, layers, tiles, cells), f32),
        ]
        + [((tiles_y, *tile), bf16)] * halos
        + [((max(tiles_x, tiles_y), *tile), bf16)] * halos,
        pattern[0],
        coupling,
        layer_group,
        blocks.reshape(tiles, OFFSETS, cells, cells),
        flat,
        port_row,
        corner,
        far_args=4,
        scratch=[
            pltpu.SMEM(pattern.shape[1:], jnp.int32),
            pltpu.SMEM(coupling.shape, f32),
            pltpu.SMEM(layer_group.shape, jnp.int32),
            pltpu.VMEM((tiles, OFFSETS, cells, cells), bf16),
            pltpu.SemaphoreType.DMA((3,)),
            pltpu.SemaphoreType.DMA((tiles,)),
        ],
    )

    late = [
        to_layer(None, beside(pairing))(part)
        for part, (beside, pairing) in zip(late, [(b, p) for b in (other_row, other_chip) for p in row_pairs])
    ]

    def waves(phase, kappa_ref):
        def wave(base, field=None, real=None):
            if field is not None:
                factor = kappa_ref[phase, 0:1, :]
                base = (base.astype(f32) + factor * field.astype(f32)).astype(bf16)
            return base if real is None else jnp.where(real, base, jnp.zeros_like(base))

        return wave

    def row_real():
        return [Side(pairing, "row", tiles_x).real for pairing in row_pairs]

    def step_inputs(step, take):
        source_ref, kappa_ref, rim_refs, column_refs = take(), take(), take(halos), take(halos)
        if step == 0:
            return source_ref, kappa_ref, rim_refs, column_refs, None, [None] * halos, column_refs
        return source_ref, kappa_ref, rim_refs, column_refs, take(), take(halos), take(halos)

    def core_kernel(step, *refs):
        take = taker(refs)
        phase = int(step >= layers // 2)
        source_ref, kappa_ref, rim_refs, column_refs, field_ref, field_rims, carried = step_inputs(step, take)
        core_ref = take()
        for h in range(halos):
            core_ref[ext + h] = carried[h][0]
            if step == layers // 2:
                core_ref[ext + halos + h] = column_refs[h][0]

        @pl.when(is_active(step))
        def _():
            wave = waves(phase, kappa_ref)
            real = row_real()
            edge = Side(near, "col", tiles_y).edge
            for x in range(tiles_x):
                t = x * tiles_y + edge
                core_ref[x] = wave(source_ref[phase, t], None if step == 0 else field_ref[t])
            for h in range(halos):
                core_ref[tiles_x + h] = wave(
                    rim_refs[h][edge], None if step == 0 else field_rims[h][edge], real[h]
                )

    def product(lhs, rhs):
        return jnp.dot(lhs, rhs, preferred_element_type=f32)

    def column_products(across, front_ref, halo_ref):
        totals = []
        for x in range(tiles_x):
            t = x * tiles_y + across.edge
            reach = [a for a in (-1, 0, 1) if 0 <= x + a < tiles_x]
            lhs = jnp.concatenate([halo_ref[x + a] for a in reach], axis=1)
            rhs = jnp.concatenate([front_ref[t, 3 * (a + 1) + 1 + across.step] for a in reach], axis=0)
            totals.append(product(lhs, rhs))
        return totals

    def corner_product(across, pairing, front_ref, corner):
        side = Side(pairing, "row", tiles_x)
        t = side.edge * tiles_y + across.edge
        return t, product(corner, front_ref[t, 3 * (side.step + 1) + 1 + across.step])

    def early_tiles():
        edge = Side(far, "col", tiles_y).edge
        inside = [(x, y) for x in range(tiles_x) for y in range(1, tiles_y - 1)]
        if halos > 1:
            return inside + [(x, edge) for x in range(1, tiles_x - 1)]
        low = jnp.where(Side(near, "row", tiles_x).edge == 0, 1, 0)
        return inside + [(low + i, edge) for i in range(tiles_x - 1)]

    def late_tiles():
        beside, beyond = (Side(pairing, "col", tiles_y).edge for pairing in (near, far))
        corners = [(Side(pairing, "row", tiles_x).edge, beyond) for pairing in row_pairs]
        return [(x, beside) for x in range(tiles_x)] + corners

    def add_parts(some, one_ref, other_ref, part_ref):
        for x, y in some:
            t = x * tiles_y + y
            both = one_ref[t].astype(f32) * other_ref[t].astype(f32)
            part_ref[pl.ds(t, 1), :] = jnp.sum(both, axis=0, keepdims=True) * intersection_scale

    def inner_kernel(step, *refs):
        take = taker(refs)
        phase, last = int(step >= layers // 2), step == layers - 1
        source_ref, kappa_ref, rim_refs, column_refs, field_ref, field_rims, carried = step_inputs(step, take)
        take()
        front_ref, earlier = take(), take(layers - 1 if last else 0)
        sum_ref, out_ref, rest, wave_ref, side_ref = take(), take(), take(1 if last else halos + 1), take(), take()

        @pl.when(is_active(step))
        def _():
            wave = waves(phase, kappa_ref)
            real = row_real()
            for x in range(tiles_x):
                for y in range(tiles_y):
                    t = x * tiles_y + y
                    wave_ref[x, y] = wave(source_ref[phase, t], None if step == 0 else field_ref[t])
                side_ref[x] = wave(column_refs[0][x], None if step == 0 else carried[0][x])
            for h in range(halos):
                for y in range(tiles_y):
                    wave_ref[tiles_x + h, y] = wave(
                        rim_refs[h][y], None if step == 0 else field_rims[h][y], real[h]
                    )
            for y in range(tiles_y):
                low, high = max(y - 1, 0), min(y + 1, tiles_y - 1)
                width = high - low + 1
                first = low - y + 1
                beside = [
                    jnp.concatenate([wave_ref[x, j] for j in range(low, high + 1)], axis=1) for x in range(ext)
                ]
                for x in range(tiles_x):
                    reach = [a for a in (-1, 0, 1) if 0 <= x + a < tiles_x]
                    lhs = jnp.concatenate([beside[x + a] for a in reach], axis=1)
                    rhs = jnp.concatenate(
                        [
                            front_ref[x * tiles_y + y, 3 * (a + 1) + first : 3 * (a + 1) + first + width].reshape(
                                width * cells, cells
                            )
                            for a in reach
                        ],
                        axis=0,
                    )
                    sum_ref[x * tiles_y + y] = product(lhs, rhs)
                for h, pairing in enumerate(row_pairs):
                    side = Side(pairing, "row", tiles_x)
                    t = side.edge * tiles_y + y
                    rhs = front_ref[t, pl.ds(3 * (side.step + 1) + first, width)].reshape(width * cells, cells)
                    sum_ref[t] += product(beside[tiles_x + h], rhs)
            across = Side(far, "col", tiles_y)

            def beyond():
                for x, total in enumerate(column_products(across, front_ref, side_ref)):
                    sum_ref[x * tiles_y + across.edge] += total

            across.when(beyond)
            some = early_tiles()
            for x, y in some:
                out_ref[x * tiles_y + y] = sum_ref[x * tiles_y + y].astype(bf16)
            if last:
                add_parts(some, earlier[0], out_ref, rest[0])
            else:
                for x in range(tiles_x):
                    rest[halos][x] = out_ref[x * tiles_y + across.edge]
                for h, pairing in enumerate(row_pairs):
                    row = Side(pairing, "row", tiles_x).edge
                    rest[h][1 : tiles_y - 1] = out_ref[pl.ds(row * tiles_y + 1, tiles_y - 2)]

        if last:
            pos = lax.axis_index("layer")
            first = jnp.minimum(pos, layers - 1 - pos)
            whole = [(x, y) for x in range(tiles_x) for y in range(tiles_y)]
            for k in range(1, layers // 2):

                @pl.when(first == k)
                def _(k=k):
                    add_parts(whole, earlier[k], earlier[layers - 1 - k], rest[0])

    def add_far_corners(step, sum_ref, front_ref, kappa_ref, core_ref, base_ref):
        phase = int(step >= layers // 2)
        wave = waves(phase, kappa_ref)
        real = row_real()
        beyond = Side(far, "col", tiles_y)

        def corners():
            for h, pairing in enumerate(row_pairs):
                base = base_ref[ext + phase * halos + h]
                corner = wave(base, None if step == 0 else core_ref[ext + h], real[h])
                t, total = corner_product(beyond, pairing, front_ref, corner)
                sum_ref[t] += total

        beyond.when(corners)

    def corner_front_kernel(step, *refs):
        take = taker(refs)
        take()
        front_ref, kappa_ref, core_ref, base_ref = (take() for _ in range(4))
        if step == 1:
            take(2 * halos)
        sum_ref, corner_ref = take(), take()

        @pl.when(is_active(step))
        def _():
            add_far_corners(step, sum_ref, front_ref, kappa_ref, core_ref, base_ref)
            edge = Side(far, "col", tiles_y).edge
            for h, pairing in enumerate(row_pairs):
                row = Side(pairing, "row", tiles_x).edge
                corner_ref[h] = sum_ref[row * tiles_y + edge].astype(bf16)

    def outer_kernel(step, *refs):
        take = taker(refs)
        last = step == layers - 1
        take(2 + (1 if last else halos + 1))
        front_ref, core_ref = take(), take()
        if last and layers == 4:
            take()
        kappa_ref, base_ref, first_ref = (take(), take(), take()) if last else (None, None, None)
        sum_ref, field_ref, rest = take(), take(), take(1 if last else halos + 1)

        @pl.when(is_active(step))
        def _():
            if last:
                add_far_corners(step, sum_ref, front_ref, kappa_ref, core_ref, base_ref)
            across, beyond = Side(near, "col", tiles_y), Side(far, "col", tiles_y)
            totals = column_products(across, front_ref, core_ref)
            corners = [
                corner_product(across, pairing, front_ref, core_ref[tiles_x + h])[1]
                for h, pairing in enumerate(row_pairs)
            ]
            edges = [Side(pairing, "row", tiles_x).edge for pairing in row_pairs]
            for x, total in enumerate(totals):
                t = x * tiles_y + across.edge
                total = sum_ref[t] + total
                for edge, corner in zip(edges, corners):
                    total = total + jnp.where(edge == x, corner, 0.0)
                field_ref[t] = total.astype(bf16)
            for edge in edges:
                t = edge * tiles_y + beyond.edge
                field_ref[t] = sum_ref[t].astype(bf16)
            some = late_tiles()
            if last:
                add_parts(some, first_ref, field_ref, rest[0])
            else:
                for h, pairing in enumerate(row_pairs):
                    row = Side(pairing, "row", tiles_x).edge
                    rest[halos][row] = field_ref[row * tiles_y + beyond.edge]
                    for edge in (across.edge, beyond.edge):
                        rest[h][edge] = field_ref[row * tiles_y + edge]

    def middle_kernel(one_ref, other_ref, part_ref):
        pos = lax.axis_index("layer")

        @pl.when(jnp.logical_and(pos > 0, pos < layers - 1))
        def _():
            whole = [(x, y) for x in range(tiles_x) for y in range(tiles_y)]
            add_parts(whole, one_ref, other_ref, part_ref)

    fields, field_arrived = [], []
    for step in range(layers):
        last = step == layers - 1
        inputs = [source, kappa, *(source_beside if step < layers // 2 else late), *field_arrived]
        (core_out,) = call(
            functools.partial(core_kernel, step),
            [((ext + halos * (2 if step == layers // 2 else 1), *tile), bf16)],
            *inputs,
        )
        core = to_core(core_out)
        summed, *partial_out = call(
            functools.partial(inner_kernel, step),
            [((tiles, *tile), f32), ((tiles, *tile), bf16)]
            + ([((tiles, cells), f32)] if last else [((tiles_y, *tile), bf16)] * halos + [((tiles_x, *tile), bf16)]),
            *inputs,
            core_out,
            front,
            *(fields if last else []),
            scratch=[pltpu.VMEM((ext, tiles_y, *tile), bf16), pltpu.VMEM((tiles_x, *tile), bf16)],
        )
        if step in (0, layers // 2):
            base = core
        if not last:
            summed, corner = call(
                functools.partial(corner_front_kernel, step),
                [((tiles, *tile), f32), ((SPARE * halos, *tile), bf16)],
                summed,
                front,
                kappa,
                core,
                base,
                *(late if step == 1 else []),
                aliases={0: 0},
            )
            corner = to_core(corner)
        _, field, *extra = call(
            functools.partial(outer_kernel, step),
            [(part.shape, part.dtype) for part in (summed, *partial_out)],
            summed,
            *partial_out,
            front,
            core,
            *([beside] if last and layers == 4 else []),
            *([kappa, base, fields[0]] if last else []),
            aliases={i: i for i in range(1 + len(partial_out))},
        )
        fields.append(field)
        if not last:
            field_arrived = exchange(step, corner, extra, field)
        if layers == 4 and step == 2:
            (beside,) = call(middle_kernel, [((BESIDE * tiles, cells), f32)], fields[1], fields[2])
            beside = permuted(beside, lambda l, r, c: (l ^ 1, r, c))
    intersection = extra[0]

    def fields_kernel(*refs):
        field_refs, (forward_ref, adjoint_ref, flat_ref) = refs[:layers], refs[layers:]
        pos = lax.axis_index("layer")
        for out_ref, active in ((forward_ref, lambda s: s), (adjoint_ref, lambda s: layers - 1 - s)):
            for step in range(layers):

                @pl.when(pos == active(step))
                def _(step=step):
                    for t in range(tiles):
                        flat_ref[pl.ds(t, ports, stride=tiles), :] = field_refs[step][t].astype(f32)

            out_ref[...] = flat_ref[...].reshape(ports, tiles, cells).astype(bf16)

    forward, adjoint = call(
        fields_kernel,
        [((ports, tiles, cells), bf16)] * 2,
        *fields,
        scratch=[pltpu.VMEM((ports * tiles, cells), f32)],
    )

    if layers == 4:

        def pair_kernel(own_ref, beside_ref, out_ref):
            out_ref[0] = own_ref[...]
            out_ref[1] = beside_ref[:tiles]

        def gather(parts, member_ref, out_ref):
            for g in range(groups):
                total = jnp.zeros((tiles, cells), f32)
                for layer, part in parts:
                    total = total + member_ref[g, layer] * part
                for x in range(tiles_x):
                    out_ref[g, x] = total[x * tiles_y : (x + 1) * tiles_y]

        def ends_kernel(own_ref, beside_ref, across_ref, member_ref, out_ref):
            pos = lax.axis_index("layer")
            end = layers - 1 - pos
            parts = [(pos, own_ref[...]), (pos ^ 1, beside_ref[:tiles]), (end, across_ref[0]), (end ^ 1, across_ref[1])]
            gather(parts, member_ref, out_ref)

        def middle_layers_kernel(ends_ref, own_ref, across_ref, next_ref, other_ref, member_ref, out_ref, sum_ref, sem):
            pos = lax.axis_index("layer")

            @pl.when(jnp.logical_and(pos > 0, pos < layers - 1))
            def _():
                parts = [
                    (pos, own_ref[...]),
                    (layers - 1 - pos, across_ref[0]),
                    (pos ^ 1, next_ref[...]),
                    (pos ^ 2, other_ref[...]),
                ]
                gather(parts, member_ref, sum_ref)
                copy = pltpu.make_async_copy(sum_ref, out_ref, sem)
                copy.start()
                copy.wait()

        out_shape = (groups, tiles_x, tiles_y, cells)
        (both,) = call(pair_kernel, [((2, tiles, cells), f32)], intersection, beside)
        across = permuted(both, lambda l, r, c: (layers - 1 - l, r, c))
        following = permuted(intersection, lambda l, r, c: (l ^ 1, r, c))
        other = permuted(intersection, lambda l, r, c: (l ^ 2, r, c))
        (gradient,) = call(ends_kernel, [(out_shape, f32)], intersection, beside, across, member)
        hbm = pl.BlockSpec(memory_space=pltpu.HBM)
        gradient = pl.pallas_call(
            middle_layers_kernel,
            out_shape=jax.ShapeDtypeStruct(out_shape, f32),
            in_specs=[hbm] + [VM] * 5,
            out_specs=hbm,
            scratch_shapes=[pltpu.VMEM(out_shape, f32), pltpu.SemaphoreType.DMA],
            input_output_aliases={0: 0},
            compiler_params=pltpu.CompilerParams(vmem_limit_bytes=VMEM_BYTES),
        )(
            pltpu.with_memory_space_constraint(gradient, pltpu.HBM),
            intersection,
            across,
            following,
            other,
            member,
        )
    else:
        selected = lax.dynamic_index_in_dim(member, lax.axis_index("layer"), 1, keepdims=False)
        gradient = lax.psum(selected * intersection[None], "layer").reshape(groups, tiles_x, tiles_y, cells)
    shape = (1, ports, tiles_x, tiles_y, cells)
    return (forward.reshape(shape), adjoint.reshape(shape), gradient)


def solution(mesh):
    placed = (
        P("layer", None, "row", "col", None),
        P("layer", None, "row", "col", None),
        P("layer", "row", "col", None, None, None),
        P("layer", "row", "col", None),
        P(),
        P(),
        P(),
    )
    return jax.shard_map(
        local,
        mesh=mesh,
        in_specs=placed,
        out_specs=(
            P("layer", None, "row", "col", None),
            P("layer", None, "row", "col", None),
            P(None, "row", "col", None),
        ),
        check_vma=False,
    )
```

```python
import functools

import jax
import jax.numpy as jnp
from jax import lax
from jax.experimental import pallas as pl
from jax.experimental.pallas import tpu as pltpu
from jax.sharding import PartitionSpec as P

port_strength = 4.0
intersection_scale = 0.125
AXES = ("layer", "row", "col")
OFFSETS = 9
VMEM_BYTES = 24 * 1024 * 1024
BESIDE = 16
SPARE = 2

VM = pl.BlockSpec(memory_space=pltpu.VMEM)


def call(kernel, outs, *args, far_args=0, scratch=(), aliases=None):
    args = [pltpu.with_memory_space_constraint(a, pltpu.HBM) for a in args[:far_args]] + list(args[far_args:])
    return pl.pallas_call(
        kernel,
        out_shape=[jax.ShapeDtypeStruct(shape, dtype) for shape, dtype in outs],
        in_specs=[pl.BlockSpec(memory_space=pltpu.HBM)] * far_args + [VM] * (len(args) - far_args),
        out_specs=[VM] * len(outs),
        scratch_shapes=list(scratch),
        input_output_aliases=aliases or {},
        compiler_params=pltpu.CompilerParams(vmem_limit_bytes=VMEM_BYTES),
    )(*args)


def near(i, n):
    return i ^ 1


def far(i, n):
    return (((i + 1) ^ 1) - 1) % n


def pairings(n):
    return [near] if n == 2 else [near, far]


class Side:
    def __init__(self, pairing, axis, tiles):
        pos, count = lax.axis_index(axis), lax.axis_size(axis)
        even = lax.rem(pos, 2) == 0
        after = even if pairing is near else jnp.logical_not(even)
        self.step = jnp.where(after, 1, -1)
        self.edge = jnp.where(after, tiles - 1, 0)
        self.real = None
        if pairing is far:
            self.real = jnp.logical_not(
                jnp.logical_or(jnp.logical_and(after, pos == count - 1), jnp.logical_and(jnp.logical_not(after), pos == 0))
            )

    def when(self, body):
        if self.real is None:
            body()
        else:
            pl.when(self.real)(body)


def local(sources, adjoint_sources, blocks, pattern, coupling, layer_group, port_cells):
    ports, tiles_x, tiles_y, cells = sources.shape[1:]
    tiles = tiles_x * tiles_y
    groups = coupling.shape[0]
    layers, rows, cols = (lax.axis_size(axis) for axis in AXES)
    if cols != 4 or layers % 2 or layers < 4 or rows % 2:
        raise ValueError("unsupported mesh")
    row_pairs = pairings(rows)
    halos = len(row_pairs)
    ext = tiles_x + halos
    bf16, f32 = jnp.bfloat16, jnp.float32
    tile = (ports, cells)

    def permuted(array, target):
        pairs = []
        for l in range(layers):
            for r in range(rows):
                for c in range(cols):
                    a, b, d = target(l, r, c)
                    pairs.append(((l * rows + r) * cols + c, (a * rows + b) * cols + d))
        return lax.ppermute(array, AXES, pairs)

    def to_core(array):
        return permuted(array, lambda l, r, c: (l, r, near(c, cols)))

    def to_layer(step, beside):
        def target(l, r, c):
            if step is None:
                return l, *beside(r, c)
            a = (near if step % 2 == 0 else far)(l, layers)
            return (a, *beside(r, c)) if abs(a - l) == 1 else (l, r, near(c, cols))

        return lambda array: permuted(array, target)

    def same(r, c):
        return r, c

    def other_row(pairing):
        return lambda r, c: (pairing(r, rows), c)

    def other_chip(pairing):
        def beside(r, c):
            d = far(c, cols)
            return (r if abs(d - c) == 1 else pairing(r, rows)), d

        return beside

    def is_active(step):
        pos = lax.axis_index("layer")
        return jnp.logical_or(pos == step, pos == layers - 1 - step)

    def taker(refs):
        refs = list(refs)

        def take(count=None):
            taken = refs[: 1 if count is None else count]
            del refs[: len(taken)]
            return taken[0] if count is None else taken

        return take

    def first_sweep():
        return jnp.where(lax.axis_index("layer") < layers // 2, 0, 1)

    def port_map(cells_ref, x, y):
        x_pos = lax.axis_index("row") * tiles_x + x
        y_pos = lax.axis_index("col") * tiles_y + y
        first = (x_pos * (tiles_y * cols) + y_pos) * cells
        row = jnp.broadcast_to(cells_ref[...], (ports, ports))
        diagonal = lax.broadcasted_iota(jnp.int32, (ports, ports), 0) == lax.broadcasted_iota(
            jnp.int32, (ports, ports), 1
        )
        column = jnp.sum(jnp.where(diagonal, row, 0), axis=1, keepdims=True)
        lane = lax.broadcasted_iota(jnp.int32, tile, 1)
        return jnp.where(column - first == lane, port_strength, 0.0).astype(f32)

    def source_tile(flat_ref, cells_ref, phase, x, y):
        value = flat_ref[phase, pl.ds(x * tiles_y + y, ports, stride=tiles), :]
        if phase == 0:
            pos = lax.axis_index("layer")
            end = jnp.logical_or(pos == 0, pos == layers - 1)
            value = value + jnp.where(end, port_map(cells_ref, x, y), 0.0)
        return value.astype(bf16)

    def corner_kernel(forward_hbm, adjoint_hbm, cells_hbm, flat_ref, cells_ref, corner_ref, raw_ref, sems):
        copies = [
            pltpu.make_async_copy(src, dst, sems.at[i])
            for i, (src, dst) in enumerate(
                ((forward_hbm, raw_ref.at[0]), (adjoint_hbm, raw_ref.at[1]), (cells_hbm, cells_ref))
            )
        ]
        for copy in copies:
            copy.start()
        for copy in copies:
            copy.wait()
        edge = Side(far, "col", tiles_y).edge
        for phase in range(2):
            flat_ref[phase] = raw_ref[first_sweep() ^ phase].astype(f32).reshape(ports * tiles, cells)
            for h, pairing in enumerate(row_pairs):
                row = Side(pairing, "row", tiles_x).edge
                corner_ref[h, phase] = source_tile(flat_ref, cells_ref, phase, row, edge)

    def rims_kernel(flat_ref, cells_ref, *refs):
        take = taker(refs)
        rim_refs, column_ref = take(halos), take()
        edge = Side(far, "col", tiles_y).edge
        for x in range(tiles_x):
            column_ref[x] = source_tile(flat_ref, cells_ref, 0, x, edge)
        for h, pairing in enumerate(row_pairs):
            row = Side(pairing, "row", tiles_x).edge
            for y in range(tiles_y):
                rim_refs[h][y] = source_tile(flat_ref, cells_ref, 0, row, y)

    raw_shape = (ports, tiles, cells)
    flat, port_row, corner = call(
        corner_kernel,
        [((2, ports * tiles, cells), f32), ((1, ports), jnp.int32), ((SPARE * halos, 2, *tile), bf16)],
        sources.reshape(raw_shape),
        adjoint_sources.reshape(raw_shape),
        port_cells.reshape(1, ports),
        far_args=3,
        scratch=[pltpu.VMEM((2, *raw_shape), bf16), pltpu.SemaphoreType.DMA((3,))],
    )
    corner = to_core(corner)
    outward = call(rims_kernel, [((tiles_y, *tile), bf16)] * halos + [((tiles_x, *tile), bf16)], flat, port_row)

    def relay_kernel(phase, *refs):
        take = taker(refs)
        column_ref, corner_ref, out_refs = take(), take(), take(halos)
        inner = Side(far, "col", tiles_y).real

        @pl.when(inner)
        def _():
            for out_ref in out_refs:
                out_ref[:tiles_x] = column_ref[...]

        @pl.when(jnp.logical_not(inner))
        def _():
            for h, out_ref in enumerate(out_refs):
                out_ref[0] = corner_ref[h] if phase is None else corner_ref[h, phase]

    def exchange(step, corner, outward, field=None):
        rims, column = outward[:halos], outward[halos]
        arrived = [] if field is None else [to_layer(step, same)(field)]
        arrived += [to_layer(step, other_row(pairing))(rim) for rim, pairing in zip(rims, row_pairs)]
        kernel = functools.partial(relay_kernel, 0 if step is None else None)
        carried = call(kernel, [(column.shape, bf16)] * halos, column, corner)
        return arrived + [to_layer(step, other_chip(pairing))(part) for part, pairing in zip(carried, row_pairs)]

    source_beside = exchange(None, corner, outward)

    def setup_kernel(pattern_hbm, coupling_hbm, group_hbm, blocks_hbm, *refs):
        take = taker(refs)
        flat_ref, cells_ref, source_ref, front_ref, kappa_ref, member_ref = (take() for _ in range(6))
        late_refs, late_column_ref, late_corner_refs = take(halos), take(), take(halos)
        pattern_ref, coupling_ref, group_ref, blocks_ref, sems, block_sems = (take() for _ in range(6))
        scalars = [
            pltpu.make_async_copy(src, dst, sems.at[i])
            for i, (src, dst) in enumerate(
                ((pattern_hbm, pattern_ref), (coupling_hbm, coupling_ref), (group_hbm, group_ref))
            )
        ]
        loads = [
            pltpu.make_async_copy(blocks_hbm.at[t], blocks_ref.at[t], block_sems.at[t]) for t in range(tiles)
        ]
        for copy in scalars + loads:
            copy.start()
        for phase in range(2):
            for x in range(tiles_x):
                for y in range(tiles_y):
                    source_ref[phase, x * tiles_y + y] = source_tile(flat_ref, cells_ref, phase, x, y)
        for pairing, rim_ref in zip(row_pairs, late_refs):
            row = Side(pairing, "row", tiles_x).edge
            rim_ref[...] = source_ref[1, pl.ds(row * tiles_y, tiles_y)]
        edge = Side(far, "col", tiles_y).edge
        for x in range(tiles_x):
            late_column_ref[x] = source_ref[1, x * tiles_y + edge]
        for pairing, corner_ref in zip(row_pairs, late_corner_refs):
            corner_ref[0] = source_ref[1, Side(pairing, "row", tiles_x).edge * tiles_y + edge]
        for copy in scalars:
            copy.wait()
        for t in range(tiles):
            loads[t].wait()
            for offset in range(OFFSETS):
                present = pattern_ref[t // tiles_y, t % tiles_y, offset] > 0
                front_ref[t, offset] = jnp.where(present, blocks_ref[t, offset], jnp.zeros((cells, cells), bf16))
        pos = lax.axis_index("layer")
        own = coupling_ref[group_ref[pos]]
        following = coupling_ref[group_ref[jnp.minimum(pos + 1, layers - 1)]]
        early = first_sweep() == 0
        kappa_ref[0] = jnp.full((8, cells), jnp.where(early, own, following), f32)
        kappa_ref[1] = jnp.full((8, cells), jnp.where(early, following, own), f32)
        for g in range(groups):
            for l in range(layers):
                member_ref[g, l] = jnp.full((tiles, cells), jnp.where(group_ref[l] == g, 1.0, 0.0), f32)

    source, front, kappa, member, *late = call(
        setup_kernel,
        [
            ((2, tiles, *tile), bf16),
            ((tiles, OFFSETS, cells, cells), bf16),
            ((2, 8, cells), f32),
            ((groups, layers, tiles, cells), f32),
        ]
        + [((tiles_y, *tile), bf16)] * halos
        + [((max(tiles_x, tiles_y), *tile), bf16)] * (halos + 1),
        pattern[0],
        coupling,
        layer_group,
        blocks.reshape(tiles, OFFSETS, cells, cells),
        flat,
        port_row,
        far_args=4,
        scratch=[
            pltpu.SMEM(pattern.shape[1:], jnp.int32),
            pltpu.SMEM(coupling.shape, f32),
            pltpu.SMEM(layer_group.shape, jnp.int32),
            pltpu.VMEM((tiles, OFFSETS, cells, cells), bf16),
            pltpu.SemaphoreType.DMA((3,)),
            pltpu.SemaphoreType.DMA((tiles,)),
        ],
    )

    late_rims, late_sides = late[:halos], late[halos:]
    late_rims = [to_layer(None, other_row(pairing))(part) for part, pairing in zip(late_rims, row_pairs)]

    def inner_only(beside, pairing):
        def target(l, r, c):
            return (l, *beside(r, c)) if abs(far(c, cols) - c) == 1 else (l, pairing(r, rows), c)

        return target

    late_corners = [
        permuted(part, inner_only(lambda r, c, pairing=pairing: (pairing(r, rows), far(c, cols)), pairing))
        for part, pairing in zip(late_sides[1:], row_pairs)
    ]
    late_sides = [permuted(late_sides[0], inner_only(lambda r, c: (r, far(c, cols)), near))] + late_corners
    turn = layers // 2

    def waves(phase, kappa_ref):
        def wave(base, field=None, real=None):
            if field is not None:
                factor = kappa_ref[phase, 0:1, :]
                base = (base.astype(f32) + factor * field.astype(f32)).astype(bf16)
            return base if real is None else jnp.where(real, base, jnp.zeros_like(base))

        return wave

    def row_real():
        return [Side(pairing, "row", tiles_x).real for pairing in row_pairs]

    def step_inputs(step, take):
        source_ref, kappa_ref, rim_refs = take(), take(), take(halos)
        column_refs = take(halos if step < turn else 0 if step == turn else 1)
        if step == 0:
            return source_ref, kappa_ref, rim_refs, column_refs, None, [None] * halos, column_refs
        return source_ref, kappa_ref, rim_refs, column_refs, take(), take(halos), take(halos)

    def core_kernel(step, *refs):
        take = taker(refs)
        phase = int(step >= layers // 2)
        source_ref, kappa_ref, rim_refs, column_refs, field_ref, field_rims, carried = step_inputs(step, take)
        core_ref = take()
        for h in range(halos):
            core_ref[ext + h] = carried[h][0]

        @pl.when(is_active(step))
        def _():
            wave = waves(phase, kappa_ref)
            real = row_real()
            edge = Side(near, "col", tiles_y).edge
            for x in range(tiles_x):
                t = x * tiles_y + edge
                core_ref[x] = wave(source_ref[phase, t], None if step == 0 else field_ref[t])
            for h in range(halos):
                core_ref[tiles_x + h] = wave(
                    rim_refs[h][edge], None if step == 0 else field_rims[h][edge], real[h]
                )

    def product(lhs, rhs):
        return jnp.dot(lhs, rhs, preferred_element_type=f32)

    def column_products(across, front_ref, halo_ref):
        totals = []
        for x in range(tiles_x):
            t = x * tiles_y + across.edge
            reach = [a for a in (-1, 0, 1) if 0 <= x + a < tiles_x]
            lhs = jnp.concatenate([halo_ref[x + a] for a in reach], axis=1)
            rhs = jnp.concatenate([front_ref[t, 3 * (a + 1) + 1 + across.step] for a in reach], axis=0)
            totals.append(product(lhs, rhs))
        return totals

    def corner_product(across, pairing, front_ref, corner):
        side = Side(pairing, "row", tiles_x)
        t = side.edge * tiles_y + across.edge
        return t, product(corner, front_ref[t, 3 * (side.step + 1) + 1 + across.step])

    def early_tiles(step):
        edge = Side(far, "col", tiles_y).edge
        inside = [(x, y) for x in range(tiles_x) for y in range(1, tiles_y - 1)]
        if step == turn:
            return inside
        if halos > 1:
            return inside + [(x, edge) for x in range(1, tiles_x - 1)]
        low = jnp.where(Side(near, "row", tiles_x).edge == 0, 1, 0)
        return inside + [(low + i, edge) for i in range(tiles_x - 1)]

    def late_tiles(step):
        beside, beyond = (Side(pairing, "col", tiles_y).edge for pairing in (near, far))
        corners = [(Side(pairing, "row", tiles_x).edge, beyond) for pairing in row_pairs]
        if step == turn:
            corners = [(x, beyond) for x in range(tiles_x)]
        return [(x, beside) for x in range(tiles_x)] + corners

    def add_parts(some, one_ref, other_ref, part_ref):
        for x, y in some:
            t = x * tiles_y + y
            both = one_ref[t].astype(f32) * other_ref[t].astype(f32)
            part_ref[pl.ds(t, 1), :] = jnp.sum(both, axis=0, keepdims=True) * intersection_scale

    def inner_kernel(step, *refs):
        take = taker(refs)
        phase, last = int(step >= layers // 2), step == layers - 1
        source_ref, kappa_ref, rim_refs, column_refs, field_ref, field_rims, carried = step_inputs(step, take)
        take()
        front_ref, earlier = take(), take(layers - 1 if last else 0)
        sum_ref, out_ref, rest, wave_ref, side_ref = take(), take(), take(1 if last else halos + 1), take(), take()

        @pl.when(is_active(step))
        def _():
            wave = waves(phase, kappa_ref)
            real = row_real()
            for x in range(tiles_x):
                for y in range(tiles_y):
                    t = x * tiles_y + y
                    wave_ref[x, y] = wave(source_ref[phase, t], None if step == 0 else field_ref[t])
                if step != turn:
                    side_ref[x] = wave(column_refs[0][x], None if step == 0 else carried[0][x])
            for h in range(halos):
                for y in range(tiles_y):
                    wave_ref[tiles_x + h, y] = wave(
                        rim_refs[h][y], None if step == 0 else field_rims[h][y], real[h]
                    )
            for y in range(tiles_y):
                low, high = max(y - 1, 0), min(y + 1, tiles_y - 1)
                width = high - low + 1
                first = low - y + 1
                beside = [
                    jnp.concatenate([wave_ref[x, j] for j in range(low, high + 1)], axis=1) for x in range(ext)
                ]
                for x in range(tiles_x):
                    reach = [a for a in (-1, 0, 1) if 0 <= x + a < tiles_x]
                    lhs = jnp.concatenate([beside[x + a] for a in reach], axis=1)
                    rhs = jnp.concatenate(
                        [
                            front_ref[x * tiles_y + y, 3 * (a + 1) + first : 3 * (a + 1) + first + width].reshape(
                                width * cells, cells
                            )
                            for a in reach
                        ],
                        axis=0,
                    )
                    sum_ref[x * tiles_y + y] = product(lhs, rhs)
                for h, pairing in enumerate(row_pairs):
                    side = Side(pairing, "row", tiles_x)
                    t = side.edge * tiles_y + y
                    rhs = front_ref[t, pl.ds(3 * (side.step + 1) + first, width)].reshape(width * cells, cells)
                    sum_ref[t] += product(beside[tiles_x + h], rhs)
            across = Side(far, "col", tiles_y)

            def beyond():
                for x, total in enumerate(column_products(across, front_ref, side_ref)):
                    sum_ref[x * tiles_y + across.edge] += total

            if step != turn:
                across.when(beyond)
            some = early_tiles(step)
            for x, y in some:
                out_ref[x * tiles_y + y] = sum_ref[x * tiles_y + y].astype(bf16)
            if last:
                add_parts(some, earlier[0], out_ref, rest[0])
            else:
                for x in range(tiles_x):
                    rest[halos][x] = out_ref[x * tiles_y + across.edge]
                for h, pairing in enumerate(row_pairs):
                    row = Side(pairing, "row", tiles_x).edge
                    rest[h][1 : tiles_y - 1] = out_ref[pl.ds(row * tiles_y + 1, tiles_y - 2)]

        if last:
            pos = lax.axis_index("layer")
            first = jnp.minimum(pos, layers - 1 - pos)
            whole = [(x, y) for x in range(tiles_x) for y in range(tiles_y)]
            for k in range(1, layers // 2):

                @pl.when(first == k)
                def _(k=k):
                    add_parts(whole, earlier[k], earlier[layers - 1 - k], rest[0])

    def add_far_corners(step, sum_ref, front_ref, kappa_ref, core_ref, bases, column_ref=None, carried_ref=None):
        wave = waves(int(step >= turn), kappa_ref)
        real = row_real()
        beyond = Side(far, "col", tiles_y)

        def corners():
            if step == turn:
                side = [wave(column_ref[x], carried_ref[x]) for x in range(tiles_x)]
                for x, total in enumerate(column_products(beyond, front_ref, side)):
                    sum_ref[x * tiles_y + beyond.edge] += total
            for h, pairing in enumerate(row_pairs):
                corner = wave(bases[h], None if step == 0 else core_ref[ext + h], real[h])
                t, total = corner_product(beyond, pairing, front_ref, corner)
                sum_ref[t] += total

        beyond.when(corners)

    def corner_bases(step, refs):
        return [refs[0][ext + h] for h in range(halos)] if step < turn else [ref[0] for ref in refs]

    def corner_front_kernel(step, *refs):
        take = taker(refs)
        take()
        front_ref, kappa_ref, core_ref = take(), take(), take()
        bases = corner_bases(step, take(1 if step < turn else halos))
        extra = take(2 if step == turn else 0)
        if step == 1:
            take(halos)
        sum_ref, corner_ref = take(), take()

        @pl.when(is_active(step))
        def _():
            add_far_corners(step, sum_ref, front_ref, kappa_ref, core_ref, bases, *extra)
            edge = Side(far, "col", tiles_y).edge
            for h, pairing in enumerate(row_pairs):
                row = Side(pairing, "row", tiles_x).edge
                corner_ref[h] = sum_ref[row * tiles_y + edge].astype(bf16)

    def outer_kernel(step, *refs):
        take = taker(refs)
        last = step == layers - 1
        take(2 + (1 if last else halos + 1))
        front_ref, core_ref = take(), take()
        if last and layers == 4:
            take()
        kappa_ref, bases = (take(), corner_bases(step, take(halos))) if last else (None, None)
        first_ref = take() if last else None
        sum_ref, field_ref, rest = take(), take(), take(1 if last else halos + 1)

        @pl.when(is_active(step))
        def _():
            if last:
                add_far_corners(step, sum_ref, front_ref, kappa_ref, core_ref, bases)
            across, beyond = Side(near, "col", tiles_y), Side(far, "col", tiles_y)
            totals = column_products(across, front_ref, core_ref)
            corners = [
                corner_product(across, pairing, front_ref, core_ref[tiles_x + h])[1]
                for h, pairing in enumerate(row_pairs)
            ]
            edges = [Side(pairing, "row", tiles_x).edge for pairing in row_pairs]
            for x, total in enumerate(totals):
                t = x * tiles_y + across.edge
                total = sum_ref[t] + total
                for edge, corner in zip(edges, corners):
                    total = total + jnp.where(edge == x, corner, 0.0)
                field_ref[t] = total.astype(bf16)
            some = late_tiles(step)
            for x, y in some[tiles_x:]:
                field_ref[x * tiles_y + y] = sum_ref[x * tiles_y + y].astype(bf16)
            if last:
                add_parts(some, first_ref, field_ref, rest[0])
            else:
                for x, y in some[tiles_x:]:
                    rest[halos][x] = field_ref[x * tiles_y + y]
                for h, pairing in enumerate(row_pairs):
                    row = Side(pairing, "row", tiles_x).edge
                    for edge in (across.edge, beyond.edge):
                        rest[h][edge] = field_ref[row * tiles_y + edge]

    def middle_kernel(one_ref, other_ref, part_ref):
        pos = lax.axis_index("layer")

        @pl.when(jnp.logical_and(pos > 0, pos < layers - 1))
        def _():
            whole = [(x, y) for x in range(tiles_x) for y in range(tiles_y)]
            add_parts(whole, one_ref, other_ref, part_ref)

    fields, field_arrived = [], []
    for step in range(layers):
        last = step == layers - 1
        halo = source_beside if step < turn else [*late_rims, *(late_sides[:1] if step > turn else [])]
        inputs = [source, kappa, *halo, *field_arrived]
        (core_out,) = call(
            functools.partial(core_kernel, step),
            [((ext + halos, *tile), bf16)],
            *inputs,
        )
        core = to_core(core_out)
        summed, *partial_out = call(
            functools.partial(inner_kernel, step),
            [((tiles, *tile), f32), ((tiles, *tile), bf16)]
            + ([((tiles, cells), f32)] if last else [((tiles_y, *tile), bf16)] * halos + [((tiles_x, *tile), bf16)]),
            *inputs,
            core_out,
            front,
            *(fields if last else []),
            scratch=[pltpu.VMEM((ext, tiles_y, *tile), bf16), pltpu.VMEM((tiles_x, *tile), bf16)],
        )
        if step == 0:
            base = [core]
        elif step == turn:
            base = late_sides[1:]
        if not last:
            summed, corner = call(
                functools.partial(corner_front_kernel, step),
                [((tiles, *tile), f32), ((SPARE * halos, *tile), bf16)],
                summed,
                front,
                kappa,
                core,
                *base,
                *([late_sides[0], field_arrived[1 + halos]] if step == turn else []),
                *(late_rims if step == 1 else []),
                aliases={0: 0},
            )
            corner = to_core(corner)
        _, field, *extra = call(
            functools.partial(outer_kernel, step),
            [(part.shape, part.dtype) for part in (summed, *partial_out)],
            summed,
            *partial_out,
            front,
            core,
            *([beside] if last and layers == 4 else []),
            *([kappa, *base, fields[0]] if last else []),
            aliases={i: i for i in range(1 + len(partial_out))},
        )
        fields.append(field)
        if not last:
            field_arrived = exchange(step, corner, extra, field)
        if layers == 4 and step == 2:
            (beside,) = call(middle_kernel, [((BESIDE * tiles, cells), f32)], fields[1], fields[2])
            beside = permuted(beside, lambda l, r, c: (l ^ 1, r, c))
    intersection = extra[0]

    def fields_kernel(*refs):
        field_refs, (forward_ref, adjoint_ref, flat_ref) = refs[:layers], refs[layers:]
        pos = lax.axis_index("layer")
        for out_ref, active in ((forward_ref, lambda s: s), (adjoint_ref, lambda s: layers - 1 - s)):
            for step in range(layers):

                @pl.when(pos == active(step))
                def _(step=step):
                    for t in range(tiles):
                        flat_ref[pl.ds(t, ports, stride=tiles), :] = field_refs[step][t].astype(f32)

            out_ref[...] = flat_ref[...].reshape(ports, tiles, cells).astype(bf16)

    forward, adjoint = call(
        fields_kernel,
        [((ports, tiles, cells), bf16)] * 2,
        *fields,
        scratch=[pltpu.VMEM((ports * tiles, cells), f32)],
    )

    if layers == 4:

        def pair_kernel(own_ref, beside_ref, out_ref):
            out_ref[0] = own_ref[...]
            out_ref[1] = beside_ref[:tiles]

        def gather(parts, member_ref, out_ref):
            for g in range(groups):
                total = jnp.zeros((tiles, cells), f32)
                for layer, part in parts:
                    total = total + member_ref[g, layer] * part
                for x in range(tiles_x):
                    out_ref[g, x] = total[x * tiles_y : (x + 1) * tiles_y]

        def ends_kernel(own_ref, beside_ref, across_ref, member_ref, out_ref):
            pos = lax.axis_index("layer")
            end = layers - 1 - pos
            parts = [(pos, own_ref[...]), (pos ^ 1, beside_ref[:tiles]), (end, across_ref[0]), (end ^ 1, across_ref[1])]
            gather(parts, member_ref, out_ref)

        def middle_layers_kernel(ends_ref, own_ref, across_ref, next_ref, other_ref, member_ref, out_ref, sum_ref, sem):
            pos = lax.axis_index("layer")

            @pl.when(jnp.logical_and(pos > 0, pos < layers - 1))
            def _():
                parts = [
                    (pos, own_ref[...]),
                    (layers - 1 - pos, across_ref[0]),
                    (pos ^ 1, next_ref[...]),
                    (pos ^ 2, other_ref[...]),
                ]
                gather(parts, member_ref, sum_ref)
                copy = pltpu.make_async_copy(sum_ref, out_ref, sem)
                copy.start()
                copy.wait()

        out_shape = (groups, tiles_x, tiles_y, cells)
        (both,) = call(pair_kernel, [((2, tiles, cells), f32)], intersection, beside)
        across = permuted(both, lambda l, r, c: (layers - 1 - l, r, c))
        following = permuted(intersection, lambda l, r, c: (l ^ 1, r, c))
        other = permuted(intersection, lambda l, r, c: (l ^ 2, r, c))
        (gradient,) = call(ends_kernel, [(out_shape, f32)], intersection, beside, across, member)
        hbm = pl.BlockSpec(memory_space=pltpu.HBM)
        gradient = pl.pallas_call(
            middle_layers_kernel,
            out_shape=jax.ShapeDtypeStruct(out_shape, f32),
            in_specs=[hbm] + [VM] * 5,
            out_specs=hbm,
            scratch_shapes=[pltpu.VMEM(out_shape, f32), pltpu.SemaphoreType.DMA],
            input_output_aliases={0: 0},
            compiler_params=pltpu.CompilerParams(vmem_limit_bytes=VMEM_BYTES),
        )(
            pltpu.with_memory_space_constraint(gradient, pltpu.HBM),
            intersection,
            across,
            following,
            other,
            member,
        )
    else:
        selected = lax.dynamic_index_in_dim(member, lax.axis_index("layer"), 1, keepdims=False)
        gradient = lax.psum(selected * intersection[None], "layer").reshape(groups, tiles_x, tiles_y, cells)
    shape = (1, ports, tiles_x, tiles_y, cells)
    return (forward.reshape(shape), adjoint.reshape(shape), gradient)


def solution(mesh):
    placed = (
        P("layer", None, "row", "col", None),
        P("layer", None, "row", "col", None),
        P("layer", "row", "col", None, None, None),
        P("layer", "row", "col", None),
        P(),
        P(),
        P(),
    )
    return jax.shard_map(
        local,
        mesh=mesh,
        in_specs=placed,
        out_specs=(
            P("layer", None, "row", "col", None),
            P("layer", None, "row", "col", None),
            P(None, "row", "col", None),
        ),
        check_vma=False,
    )
```

```python
import functools

import jax
import jax.numpy as jnp
from jax import lax
from jax.experimental import pallas as pl
from jax.experimental.pallas import tpu as pltpu
from jax.sharding import PartitionSpec as P

port_strength = 4.0
intersection_scale = 0.125
AXES = ("layer", "row", "col")
OFFSETS = 9
VMEM_BYTES = 24 * 1024 * 1024
BESIDE = 16
SPARE = 2

VM = pl.BlockSpec(memory_space=pltpu.VMEM)


def call(kernel, outs, *args, far_args=0, scratch=(), aliases=None):
    args = [pltpu.with_memory_space_constraint(a, pltpu.HBM) for a in args[:far_args]] + list(args[far_args:])
    return pl.pallas_call(
        kernel,
        out_shape=[jax.ShapeDtypeStruct(shape, dtype) for shape, dtype in outs],
        in_specs=[pl.BlockSpec(memory_space=pltpu.HBM)] * far_args + [VM] * (len(args) - far_args),
        out_specs=[VM] * len(outs),
        scratch_shapes=list(scratch),
        input_output_aliases=aliases or {},
        compiler_params=pltpu.CompilerParams(vmem_limit_bytes=VMEM_BYTES),
    )(*args)


def near(i, n):
    return i ^ 1


def far(i, n):
    return (((i + 1) ^ 1) - 1) % n


def pairings(n):
    return [near] if n == 2 else [near, far]


class Side:
    def __init__(self, pairing, axis, tiles):
        pos, count = lax.axis_index(axis), lax.axis_size(axis)
        even = lax.rem(pos, 2) == 0
        after = even if pairing is near else jnp.logical_not(even)
        self.step = jnp.where(after, 1, -1)
        self.edge = jnp.where(after, tiles - 1, 0)
        self.real = None
        if pairing is far:
            self.real = jnp.logical_not(
                jnp.logical_or(jnp.logical_and(after, pos == count - 1), jnp.logical_and(jnp.logical_not(after), pos == 0))
            )

    def when(self, body):
        if self.real is None:
            body()
        else:
            pl.when(self.real)(body)


def local(sources, adjoint_sources, blocks, pattern, coupling, layer_group, port_cells):
    ports, tiles_x, tiles_y, cells = sources.shape[1:]
    tiles = tiles_x * tiles_y
    groups = coupling.shape[0]
    layers, rows, cols = (lax.axis_size(axis) for axis in AXES)
    if cols != 4 or layers % 2 or layers < 4 or rows % 2:
        raise ValueError("unsupported mesh")
    row_pairs = pairings(rows)
    halos = len(row_pairs)
    ext = tiles_x + halos
    bf16, f32 = jnp.bfloat16, jnp.float32
    tile = (ports, cells)

    def permuted(array, target):
        pairs = []
        for l in range(layers):
            for r in range(rows):
                for c in range(cols):
                    a, b, d = target(l, r, c)
                    pairs.append(((l * rows + r) * cols + c, (a * rows + b) * cols + d))
        return lax.ppermute(array, AXES, pairs)

    def to_core(array):
        return permuted(array, lambda l, r, c: (l, r, near(c, cols)))

    def to_layer(step, beside):
        def target(l, r, c):
            if step is None:
                return l, *beside(r, c)
            a = (near if step % 2 == 0 else far)(l, layers)
            return (a, *beside(r, c)) if abs(a - l) == 1 else (l, r, near(c, cols))

        return lambda array: permuted(array, target)

    def same(r, c):
        return r, c

    def other_row(pairing):
        return lambda r, c: (pairing(r, rows), c)

    def other_chip(pairing):
        def beside(r, c):
            d = far(c, cols)
            return (r if abs(d - c) == 1 else pairing(r, rows)), d

        return beside

    def is_active(step):
        pos = lax.axis_index("layer")
        return jnp.logical_or(pos == step, pos == layers - 1 - step)

    def taker(refs):
        refs = list(refs)

        def take(count=None):
            taken = refs[: 1 if count is None else count]
            del refs[: len(taken)]
            return taken[0] if count is None else taken

        return take

    def first_sweep():
        return jnp.where(lax.axis_index("layer") < layers // 2, 0, 1)

    def port_map(cells_ref, x, y):
        x_pos = lax.axis_index("row") * tiles_x + x
        y_pos = lax.axis_index("col") * tiles_y + y
        first = (x_pos * (tiles_y * cols) + y_pos) * cells
        row = jnp.broadcast_to(cells_ref[...], (ports, ports))
        diagonal = lax.broadcasted_iota(jnp.int32, (ports, ports), 0) == lax.broadcasted_iota(
            jnp.int32, (ports, ports), 1
        )
        column = jnp.sum(jnp.where(diagonal, row, 0), axis=1, keepdims=True)
        lane = lax.broadcasted_iota(jnp.int32, tile, 1)
        return jnp.where(column - first == lane, port_strength, 0.0).astype(f32)

    def source_tile(flat_ref, cells_ref, phase, x, y):
        value = flat_ref[phase, pl.ds(x * tiles_y + y, ports, stride=tiles), :]
        if phase == 0:
            pos = lax.axis_index("layer")
            end = jnp.logical_or(pos == 0, pos == layers - 1)
            value = value + jnp.where(end, port_map(cells_ref, x, y), 0.0)
        return value.astype(bf16)

    def corner_kernel(forward_hbm, adjoint_hbm, cells_hbm, flat_ref, cells_ref, corner_ref, raw_ref, sems):
        copies = [
            pltpu.make_async_copy(src, dst, sems.at[i])
            for i, (src, dst) in enumerate(
                ((forward_hbm, raw_ref.at[0]), (adjoint_hbm, raw_ref.at[1]), (cells_hbm, cells_ref))
            )
        ]
        for copy in copies:
            copy.start()
        for copy in copies:
            copy.wait()
        edge = Side(far, "col", tiles_y).edge
        for phase in range(2):
            flat_ref[phase] = raw_ref[first_sweep() ^ phase].astype(f32).reshape(ports * tiles, cells)
            for h, pairing in enumerate(row_pairs):
                row = Side(pairing, "row", tiles_x).edge
                if phase == 0:
                    corner_ref[h] = source_tile(flat_ref, cells_ref, phase, row, edge)

    def rims_kernel(flat_ref, cells_ref, *refs):
        take = taker(refs)
        rim_refs, column_ref = take(halos), take()
        edge = Side(far, "col", tiles_y).edge
        for x in range(tiles_x):
            column_ref[x] = source_tile(flat_ref, cells_ref, 0, x, edge)
        for h, pairing in enumerate(row_pairs):
            row = Side(pairing, "row", tiles_x).edge
            for y in range(tiles_y):
                rim_refs[h][y] = source_tile(flat_ref, cells_ref, 0, row, y)

    raw_shape = (ports, tiles, cells)
    flat, port_row, corner = call(
        corner_kernel,
        [((2, ports * tiles, cells), f32), ((1, ports), jnp.int32), ((SPARE * halos, *tile), bf16)],
        sources.reshape(raw_shape),
        adjoint_sources.reshape(raw_shape),
        port_cells.reshape(1, ports),
        far_args=3,
        scratch=[pltpu.VMEM((2, *raw_shape), bf16), pltpu.SemaphoreType.DMA((3,))],
    )
    corner = to_core(corner)
    outward = call(rims_kernel, [((tiles_y, *tile), bf16)] * halos + [((tiles_x, *tile), bf16)], flat, port_row)

    def relay_kernel(phase, *refs):
        take = taker(refs)
        column_ref, corner_ref, out_refs = take(), take(), take(halos)
        inner = Side(far, "col", tiles_y).real

        @pl.when(inner)
        def _():
            for out_ref in out_refs:
                out_ref[:tiles_x] = column_ref[...]

        @pl.when(jnp.logical_not(inner))
        def _():
            for h, out_ref in enumerate(out_refs):
                out_ref[0] = corner_ref[h]

    def exchange(step, corner, outward, field=None):
        rims, column = outward[:halos], outward[halos]
        arrived = [] if field is None else [to_layer(step, same)(field)]
        arrived += [to_layer(step, other_row(pairing))(rim) for rim, pairing in zip(rims, row_pairs)]
        kernel = functools.partial(relay_kernel, 0 if step is None else None)
        carried = call(kernel, [(column.shape, bf16)] * halos, column, corner)
        return arrived + [to_layer(step, other_chip(pairing))(part) for part, pairing in zip(carried, row_pairs)]

    source_beside = exchange(None, corner, outward)

    def setup_kernel(pattern_hbm, coupling_hbm, group_hbm, blocks_hbm, *refs):
        take = taker(refs)
        flat_ref, cells_ref, source_ref, front_ref, kappa_ref, member_ref = (take() for _ in range(6))
        late_refs, late_column_ref, late_corner_refs = take(halos), take(), take(halos)
        pattern_ref, coupling_ref, group_ref, blocks_ref, sems, block_sems = (take() for _ in range(6))
        scalars = [
            pltpu.make_async_copy(src, dst, sems.at[i])
            for i, (src, dst) in enumerate(
                ((pattern_hbm, pattern_ref), (coupling_hbm, coupling_ref), (group_hbm, group_ref))
            )
        ]
        loads = [
            pltpu.make_async_copy(blocks_hbm.at[t], blocks_ref.at[t], block_sems.at[t]) for t in range(tiles)
        ]
        for copy in scalars + loads:
            copy.start()
        for phase in range(2):
            for x in range(tiles_x):
                for y in range(tiles_y):
                    source_ref[phase, x * tiles_y + y] = source_tile(flat_ref, cells_ref, phase, x, y)
        for pairing, rim_ref in zip(row_pairs, late_refs):
            row = Side(pairing, "row", tiles_x).edge
            rim_ref[...] = source_ref[1, pl.ds(row * tiles_y, tiles_y)]
        edge = Side(far, "col", tiles_y).edge
        for x in range(tiles_x):
            late_column_ref[x] = source_ref[1, x * tiles_y + edge]
        for pairing, corner_ref in zip(row_pairs, late_corner_refs):
            corner_ref[0] = source_ref[1, Side(pairing, "row", tiles_x).edge * tiles_y + edge]
        for copy in scalars:
            copy.wait()
        for t in range(tiles):
            loads[t].wait()
            for offset in range(OFFSETS):
                present = pattern_ref[t // tiles_y, t % tiles_y, offset] > 0
                front_ref[t, offset] = jnp.where(present, blocks_ref[t, offset], jnp.zeros((cells, cells), bf16))
        pos = lax.axis_index("layer")
        own = coupling_ref[group_ref[pos]]
        following = coupling_ref[group_ref[jnp.minimum(pos + 1, layers - 1)]]
        early = first_sweep() == 0
        kappa_ref[0] = jnp.full((8, cells), jnp.where(early, own, following), f32)
        kappa_ref[1] = jnp.full((8, cells), jnp.where(early, following, own), f32)
        for g in range(groups):
            for l in range(layers):
                member_ref[g, l] = jnp.full((tiles, cells), jnp.where(group_ref[l] == g, 1.0, 0.0), f32)

    source, front, kappa, member, *late = call(
        setup_kernel,
        [
            ((2, tiles, *tile), bf16),
            ((tiles, OFFSETS, cells, cells), bf16),
            ((2, 8, cells), f32),
            ((groups, layers, tiles, cells), f32),
        ]
        + [((tiles_y, *tile), bf16)] * halos
        + [((max(tiles_x, tiles_y), *tile), bf16)] * (halos + 1),
        pattern[0],
        coupling,
        layer_group,
        blocks.reshape(tiles, OFFSETS, cells, cells),
        flat,
        port_row,
        far_args=4,
        scratch=[
            pltpu.SMEM(pattern.shape[1:], jnp.int32),
            pltpu.SMEM(coupling.shape, f32),
            pltpu.SMEM(layer_group.shape, jnp.int32),
            pltpu.VMEM((tiles, OFFSETS, cells, cells), bf16),
            pltpu.SemaphoreType.DMA((3,)),
            pltpu.SemaphoreType.DMA((tiles,)),
        ],
    )

    late_rims, late_sides = late[:halos], late[halos:]
    late_rims = [to_layer(None, other_row(pairing))(part) for part, pairing in zip(late_rims, row_pairs)]

    def inner_only(beside, pairing):
        def target(l, r, c):
            return (l, *beside(r, c)) if abs(far(c, cols) - c) == 1 else (l, pairing(r, rows), c)

        return target

    late_corners = [
        permuted(part, inner_only(lambda r, c, pairing=pairing: (pairing(r, rows), far(c, cols)), pairing))
        for part, pairing in zip(late_sides[1:], row_pairs)
    ]
    late_sides = [permuted(late_sides[0], inner_only(lambda r, c: (r, far(c, cols)), near))] + late_corners
    turn = layers // 2

    def waves(phase, kappa_ref):
        def wave(base, field=None, real=None):
            if field is not None:
                factor = kappa_ref[phase, 0:1, :]
                base = (base.astype(f32) + factor * field.astype(f32)).astype(bf16)
            return base if real is None else jnp.where(real, base, jnp.zeros_like(base))

        return wave

    def row_real():
        return [Side(pairing, "row", tiles_x).real for pairing in row_pairs]

    def step_inputs(step, take):
        source_ref, kappa_ref, rim_refs = take(), take(), take(halos)
        column_refs = take(halos if step < turn else 0 if step == turn else 1)
        if step == 0:
            return source_ref, kappa_ref, rim_refs, column_refs, None, [None] * halos, column_refs
        return source_ref, kappa_ref, rim_refs, column_refs, take(), take(halos), take(halos)

    def core_kernel(step, *refs):
        take = taker(refs)
        phase = int(step >= layers // 2)
        source_ref, kappa_ref, rim_refs, column_refs, field_ref, field_rims, carried = step_inputs(step, take)
        core_ref = take()
        for h in range(halos):
            core_ref[ext + h] = carried[h][0]

        @pl.when(is_active(step))
        def _():
            wave = waves(phase, kappa_ref)
            real = row_real()
            edge = Side(near, "col", tiles_y).edge
            for x in range(tiles_x):
                t = x * tiles_y + edge
                core_ref[x] = wave(source_ref[phase, t], None if step == 0 else field_ref[t])
            for h in range(halos):
                core_ref[tiles_x + h] = wave(
                    rim_refs[h][edge], None if step == 0 else field_rims[h][edge], real[h]
                )

    def product(lhs, rhs):
        return jnp.dot(lhs, rhs, preferred_element_type=f32)

    def column_products(across, front_ref, halo_ref):
        totals = []
        for x in range(tiles_x):
            t = x * tiles_y + across.edge
            reach = [a for a in (-1, 0, 1) if 0 <= x + a < tiles_x]
            lhs = jnp.concatenate([halo_ref[x + a] for a in reach], axis=1)
            rhs = jnp.concatenate([front_ref[t, 3 * (a + 1) + 1 + across.step] for a in reach], axis=0)
            totals.append(product(lhs, rhs))
        return totals

    def corner_product(across, pairing, front_ref, corner):
        side = Side(pairing, "row", tiles_x)
        t = side.edge * tiles_y + across.edge
        return t, product(corner, front_ref[t, 3 * (side.step + 1) + 1 + across.step])

    def early_tiles(step):
        edge = Side(far, "col", tiles_y).edge
        inside = [(x, y) for x in range(tiles_x) for y in range(1, tiles_y - 1)]
        if step == turn:
            return inside
        if halos > 1:
            return inside + [(x, edge) for x in range(1, tiles_x - 1)]
        low = jnp.where(Side(near, "row", tiles_x).edge == 0, 1, 0)
        return inside + [(low + i, edge) for i in range(tiles_x - 1)]

    def late_tiles(step):
        beside, beyond = (Side(pairing, "col", tiles_y).edge for pairing in (near, far))
        corners = [(Side(pairing, "row", tiles_x).edge, beyond) for pairing in row_pairs]
        if step == turn:
            corners = [(x, beyond) for x in range(tiles_x)]
        return [(x, beside) for x in range(tiles_x)] + corners

    def add_parts(some, one_ref, other_ref, part_ref):
        for x, y in some:
            t = x * tiles_y + y
            both = one_ref[t].astype(f32) * other_ref[t].astype(f32)
            part_ref[pl.ds(t, 1), :] = jnp.sum(both, axis=0, keepdims=True) * intersection_scale

    def inner_kernel(step, *refs):
        take = taker(refs)
        phase, last = int(step >= layers // 2), step == layers - 1
        source_ref, kappa_ref, rim_refs, column_refs, field_ref, field_rims, carried = step_inputs(step, take)
        take()
        front_ref, earlier = take(), take(layers - 1 if last else 0)
        sum_ref, out_ref, rest, wave_ref, side_ref = take(), take(), take(1 if last else halos + 1), take(), take()

        @pl.when(is_active(step))
        def _():
            wave = waves(phase, kappa_ref)
            real = row_real()
            for x in range(tiles_x):
                for y in range(tiles_y):
                    t = x * tiles_y + y
                    wave_ref[x, y] = wave(source_ref[phase, t], None if step == 0 else field_ref[t])
                if step != turn:
                    side_ref[x] = wave(column_refs[0][x], None if step == 0 else carried[0][x])
            for h in range(halos):
                for y in range(tiles_y):
                    wave_ref[tiles_x + h, y] = wave(
                        rim_refs[h][y], None if step == 0 else field_rims[h][y], real[h]
                    )
            for y in range(tiles_y):
                low, high = max(y - 1, 0), min(y + 1, tiles_y - 1)
                width = high - low + 1
                first = low - y + 1
                beside = [
                    jnp.concatenate([wave_ref[x, j] for j in range(low, high + 1)], axis=1) for x in range(ext)
                ]
                for x in range(tiles_x):
                    reach = [a for a in (-1, 0, 1) if 0 <= x + a < tiles_x]
                    lhs = jnp.concatenate([beside[x + a] for a in reach], axis=1)
                    rhs = jnp.concatenate(
                        [
                            front_ref[x * tiles_y + y, 3 * (a + 1) + first : 3 * (a + 1) + first + width].reshape(
                                width * cells, cells
                            )
                            for a in reach
                        ],
                        axis=0,
                    )
                    sum_ref[x * tiles_y + y] = product(lhs, rhs)
                for h, pairing in enumerate(row_pairs):
                    side = Side(pairing, "row", tiles_x)
                    t = side.edge * tiles_y + y
                    rhs = front_ref[t, pl.ds(3 * (side.step + 1) + first, width)].reshape(width * cells, cells)
                    sum_ref[t] += product(beside[tiles_x + h], rhs)
            across = Side(far, "col", tiles_y)

            def beyond():
                for x, total in enumerate(column_products(across, front_ref, side_ref)):
                    sum_ref[x * tiles_y + across.edge] += total

            if step != turn:
                across.when(beyond)
            some = early_tiles(step)
            for x, y in some:
                out_ref[x * tiles_y + y] = sum_ref[x * tiles_y + y].astype(bf16)
            if last:
                add_parts(some, earlier[0], out_ref, rest[0])
            else:
                for x in range(tiles_x):
                    rest[halos][x] = out_ref[x * tiles_y + across.edge]
                for h, pairing in enumerate(row_pairs):
                    row = Side(pairing, "row", tiles_x).edge
                    rest[h][1 : tiles_y - 1] = out_ref[pl.ds(row * tiles_y + 1, tiles_y - 2)]

        if last:
            pos = lax.axis_index("layer")
            first = jnp.minimum(pos, layers - 1 - pos)
            whole = [(x, y) for x in range(tiles_x) for y in range(tiles_y)]
            for k in range(1, layers // 2):

                @pl.when(first == k)
                def _(k=k):
                    add_parts(whole, earlier[k], earlier[layers - 1 - k], rest[0])

    def add_far_corners(step, sum_ref, front_ref, kappa_ref, core_ref, bases, column_ref=None, carried_ref=None):
        wave = waves(int(step >= turn), kappa_ref)
        real = row_real()
        beyond = Side(far, "col", tiles_y)

        def corners():
            if step == turn:
                side = [wave(column_ref[x], carried_ref[x]) for x in range(tiles_x)]
                for x, total in enumerate(column_products(beyond, front_ref, side)):
                    sum_ref[x * tiles_y + beyond.edge] += total
            for h, pairing in enumerate(row_pairs):
                corner = wave(bases[h], None if step == 0 else core_ref[ext + h], real[h])
                t, total = corner_product(beyond, pairing, front_ref, corner)
                sum_ref[t] += total

        beyond.when(corners)

    def corner_bases(step, refs):
        return [refs[0][ext + h] for h in range(halos)] if step < turn else [ref[0] for ref in refs]

    def corner_front_kernel(step, *refs):
        take = taker(refs)
        take()
        front_ref, kappa_ref, core_ref = take(), take(), take()
        bases = corner_bases(step, take(1 if step < turn else halos))
        extra = take(2 if step == turn else 0)
        if step == 1:
            take(halos)
        sum_ref, corner_ref = take(), take()

        @pl.when(is_active(step))
        def _():
            add_far_corners(step, sum_ref, front_ref, kappa_ref, core_ref, bases, *extra)
            edge = Side(far, "col", tiles_y).edge
            for h, pairing in enumerate(row_pairs):
                row = Side(pairing, "row", tiles_x).edge
                corner_ref[h] = sum_ref[row * tiles_y + edge].astype(bf16)

    def outer_kernel(step, *refs):
        take = taker(refs)
        last = step == layers - 1
        take(2 + (1 if last else halos + 1))
        front_ref, core_ref = take(), take()
        if last and layers == 4:
            take()
        kappa_ref, bases = (take(), corner_bases(step, take(halos))) if last else (None, None)
        first_ref = take() if last else None
        sum_ref, field_ref, rest = take(), take(), take(1 if last else halos + 1)

        @pl.when(is_active(step))
        def _():
            if last:
                add_far_corners(step, sum_ref, front_ref, kappa_ref, core_ref, bases)
            across, beyond = Side(near, "col", tiles_y), Side(far, "col", tiles_y)
            totals = column_products(across, front_ref, core_ref)
            corners = [
                corner_product(across, pairing, front_ref, core_ref[tiles_x + h])[1]
                for h, pairing in enumerate(row_pairs)
            ]
            edges = [Side(pairing, "row", tiles_x).edge for pairing in row_pairs]
            for x, total in enumerate(totals):
                t = x * tiles_y + across.edge
                total = sum_ref[t] + total
                for edge, corner in zip(edges, corners):
                    total = total + jnp.where(edge == x, corner, 0.0)
                field_ref[t] = total.astype(bf16)
            some = late_tiles(step)
            for x, y in some[tiles_x:]:
                field_ref[x * tiles_y + y] = sum_ref[x * tiles_y + y].astype(bf16)
            if last:
                add_parts(some, first_ref, field_ref, rest[0])
            else:
                for x, y in some[tiles_x:]:
                    rest[halos][x] = field_ref[x * tiles_y + y]
                for h, pairing in enumerate(row_pairs):
                    row = Side(pairing, "row", tiles_x).edge
                    for edge in (across.edge, beyond.edge):
                        rest[h][edge] = field_ref[row * tiles_y + edge]

    def middle_kernel(one_ref, other_ref, part_ref):
        pos = lax.axis_index("layer")

        @pl.when(jnp.logical_and(pos > 0, pos < layers - 1))
        def _():
            whole = [(x, y) for x in range(tiles_x) for y in range(tiles_y)]
            add_parts(whole, one_ref, other_ref, part_ref)

    fields, field_arrived = [], []
    for step in range(layers):
        last = step == layers - 1
        halo = source_beside if step < turn else [*late_rims, *(late_sides[:1] if step > turn else [])]
        inputs = [source, kappa, *halo, *field_arrived]
        (core_out,) = call(
            functools.partial(core_kernel, step),
            [((ext + halos, *tile), bf16)],
            *inputs,
        )
        core = to_core(core_out)
        summed, *partial_out = call(
            functools.partial(inner_kernel, step),
            [((tiles, *tile), f32), ((tiles, *tile), bf16)]
            + ([((tiles, cells), f32)] if last else [((tiles_y, *tile), bf16)] * halos + [((tiles_x, *tile), bf16)]),
            *inputs,
            core_out,
            front,
            *(fields if last else []),
            scratch=[pltpu.VMEM((ext, tiles_y, *tile), bf16), pltpu.VMEM((tiles_x, *tile), bf16)],
        )
        if step == 0:
            base = [core]
        elif step == turn:
            base = late_sides[1:]
        if not last:
            summed, corner = call(
                functools.partial(corner_front_kernel, step),
                [((tiles, *tile), f32), ((SPARE * halos, *tile), bf16)],
                summed,
                front,
                kappa,
                core,
                *base,
                *([late_sides[0], field_arrived[1 + halos]] if step == turn else []),
                *(late_rims if step == 1 else []),
                aliases={0: 0},
            )
            corner = to_core(corner)
        _, field, *extra = call(
            functools.partial(outer_kernel, step),
            [(part.shape, part.dtype) for part in (summed, *partial_out)],
            summed,
            *partial_out,
            front,
            core,
            *([beside] if last and layers == 4 else []),
            *([kappa, *base, fields[0]] if last else []),
            aliases={i: i for i in range(1 + len(partial_out))},
        )
        fields.append(field)
        if not last:
            field_arrived = exchange(step, corner, extra, field)
        if layers == 4 and step == 2:
            (beside,) = call(middle_kernel, [((BESIDE * tiles, cells), f32)], fields[1], fields[2])
            beside = permuted(beside, lambda l, r, c: (l ^ 1, r, c))
    intersection = extra[0]

    def fields_kernel(*refs):
        field_refs, (forward_ref, adjoint_ref, flat_ref) = refs[:layers], refs[layers:]
        pos = lax.axis_index("layer")
        for out_ref, active in ((forward_ref, lambda s: s), (adjoint_ref, lambda s: layers - 1 - s)):
            for step in range(layers):

                @pl.when(pos == active(step))
                def _(step=step):
                    for t in range(tiles):
                        flat_ref[pl.ds(t, ports, stride=tiles), :] = field_refs[step][t].astype(f32)

            out_ref[...] = flat_ref[...].reshape(ports, tiles, cells).astype(bf16)

    forward, adjoint = call(
        fields_kernel,
        [((ports, tiles, cells), bf16)] * 2,
        *fields,
        scratch=[pltpu.VMEM((ports * tiles, cells), f32)],
    )

    if layers == 4:

        def pair_kernel(own_ref, beside_ref, out_ref):
            out_ref[0] = own_ref[...]
            out_ref[1] = beside_ref[:tiles]

        def gather(parts, member_ref, out_ref):
            for g in range(groups):
                total = jnp.zeros((tiles, cells), f32)
                for layer, part in parts:
                    total = total + member_ref[g, layer] * part
                for x in range(tiles_x):
                    out_ref[g, x] = total[x * tiles_y : (x + 1) * tiles_y]

        def ends_kernel(own_ref, beside_ref, across_ref, member_ref, out_ref):
            pos = lax.axis_index("layer")
            end = layers - 1 - pos
            parts = [(pos, own_ref[...]), (pos ^ 1, beside_ref[:tiles]), (end, across_ref[0]), (end ^ 1, across_ref[1])]
            gather(parts, member_ref, out_ref)

        def middle_layers_kernel(ends_ref, own_ref, across_ref, next_ref, other_ref, member_ref, out_ref, sum_ref, sem):
            pos = lax.axis_index("layer")

            @pl.when(jnp.logical_and(pos > 0, pos < layers - 1))
            def _():
                parts = [
                    (pos, own_ref[...]),
                    (layers - 1 - pos, across_ref[0]),
                    (pos ^ 1, next_ref[...]),
                    (pos ^ 2, other_ref[...]),
                ]
                gather(parts, member_ref, sum_ref)
                copy = pltpu.make_async_copy(sum_ref, out_ref, sem)
                copy.start()
                copy.wait()

        out_shape = (groups, tiles_x, tiles_y, cells)
        (both,) = call(pair_kernel, [((2, tiles, cells), f32)], intersection, beside)
        across = permuted(both, lambda l, r, c: (layers - 1 - l, r, c))
        following = permuted(intersection, lambda l, r, c: (l ^ 1, r, c))
        other = permuted(intersection, lambda l, r, c: (l ^ 2, r, c))
        (gradient,) = call(ends_kernel, [(out_shape, f32)], intersection, beside, across, member)
        hbm = pl.BlockSpec(memory_space=pltpu.HBM)
        gradient = pl.pallas_call(
            middle_layers_kernel,
            out_shape=jax.ShapeDtypeStruct(out_shape, f32),
            in_specs=[hbm] + [VM] * 5,
            out_specs=hbm,
            scratch_shapes=[pltpu.VMEM(out_shape, f32), pltpu.SemaphoreType.DMA],
            input_output_aliases={0: 0},
            compiler_params=pltpu.CompilerParams(vmem_limit_bytes=VMEM_BYTES),
        )(
            pltpu.with_memory_space_constraint(gradient, pltpu.HBM),
            intersection,
            across,
            following,
            other,
            member,
        )
    else:
        selected = lax.dynamic_index_in_dim(member, lax.axis_index("layer"), 1, keepdims=False)
        gradient = lax.psum(selected * intersection[None], "layer").reshape(groups, tiles_x, tiles_y, cells)
    shape = (1, ports, tiles_x, tiles_y, cells)
    return (forward.reshape(shape), adjoint.reshape(shape), gradient)


def solution(mesh):
    placed = (
        P("layer", None, "row", "col", None),
        P("layer", None, "row", "col", None),
        P("layer", "row", "col", None, None, None),
        P("layer", "row", "col", None),
        P(),
        P(),
        P(),
    )
    return jax.shard_map(
        local,
        mesh=mesh,
        in_specs=placed,
        out_specs=(
            P("layer", None, "row", "col", None),
            P("layer", None, "row", "col", None),
            P(None, "row", "col", None),
        ),
        check_vma=False,
    )
```

```python
import functools

import jax
import jax.numpy as jnp
from jax import lax
from jax.experimental import pallas as pl
from jax.experimental.pallas import tpu as pltpu
from jax.sharding import PartitionSpec as P

port_strength = 4.0
intersection_scale = 0.125
AXES = ("layer", "row", "col")
OFFSETS = 9
VMEM_BYTES = 24 * 1024 * 1024
BESIDE = 16
SPARE = 2

VM = pl.BlockSpec(memory_space=pltpu.VMEM)


def call(kernel, outs, *args, far_args=0, scratch=(), aliases=None):
    args = [pltpu.with_memory_space_constraint(a, pltpu.HBM) for a in args[:far_args]] + list(args[far_args:])
    return pl.pallas_call(
        kernel,
        out_shape=[jax.ShapeDtypeStruct(shape, dtype) for shape, dtype in outs],
        in_specs=[pl.BlockSpec(memory_space=pltpu.HBM)] * far_args + [VM] * (len(args) - far_args),
        out_specs=[VM] * len(outs),
        scratch_shapes=list(scratch),
        input_output_aliases=aliases or {},
        compiler_params=pltpu.CompilerParams(vmem_limit_bytes=VMEM_BYTES),
    )(*args)


def near(i, n):
    return i ^ 1


def far(i, n):
    return (((i + 1) ^ 1) - 1) % n


def pairings(n):
    return [near] if n == 2 else [near, far]


class Side:
    def __init__(self, pairing, axis, tiles):
        pos, count = lax.axis_index(axis), lax.axis_size(axis)
        even = lax.rem(pos, 2) == 0
        after = even if pairing is near else jnp.logical_not(even)
        self.step = jnp.where(after, 1, -1)
        self.edge = jnp.where(after, tiles - 1, 0)
        self.real = None
        if pairing is far:
            self.real = jnp.logical_not(
                jnp.logical_or(jnp.logical_and(after, pos == count - 1), jnp.logical_and(jnp.logical_not(after), pos == 0))
            )

    def when(self, body):
        if self.real is None:
            body()
        else:
            pl.when(self.real)(body)


def local(sources, adjoint_sources, blocks, pattern, coupling, layer_group, port_cells):
    ports, tiles_x, tiles_y, cells = sources.shape[1:]
    tiles = tiles_x * tiles_y
    groups = coupling.shape[0]
    layers, rows, cols = (lax.axis_size(axis) for axis in AXES)
    if cols != 4 or layers % 2 or layers < 4 or rows % 2:
        raise ValueError("unsupported mesh")
    row_pairs = pairings(rows)
    halos = len(row_pairs)
    ext = tiles_x + halos
    bf16, f32 = jnp.bfloat16, jnp.float32
    tile = (ports, cells)

    def permuted(array, target):
        pairs = []
        for l in range(layers):
            for r in range(rows):
                for c in range(cols):
                    a, b, d = target(l, r, c)
                    pairs.append(((l * rows + r) * cols + c, (a * rows + b) * cols + d))
        return lax.ppermute(array, AXES, pairs)

    def to_core(array):
        return permuted(array, lambda l, r, c: (l, r, near(c, cols)))

    def to_layer(step, beside):
        def target(l, r, c):
            if step is None:
                return l, *beside(r, c)
            a = (near if step % 2 == 0 else far)(l, layers)
            return (a, *beside(r, c)) if abs(a - l) == 1 else (l, r, near(c, cols))

        return lambda array: permuted(array, target)

    def same(r, c):
        return r, c

    def other_row(pairing):
        return lambda r, c: (pairing(r, rows), c)

    def other_chip(pairing):
        def beside(r, c):
            d = far(c, cols)
            return (r if abs(d - c) == 1 else pairing(r, rows)), d

        return beside

    def is_active(step):
        pos = lax.axis_index("layer")
        return jnp.logical_or(pos == step, pos == layers - 1 - step)

    def taker(refs):
        refs = list(refs)

        def take(count=None):
            taken = refs[: 1 if count is None else count]
            del refs[: len(taken)]
            return taken[0] if count is None else taken

        return take

    def first_sweep():
        return jnp.where(lax.axis_index("layer") < layers // 2, 0, 1)

    def port_map(cells_ref, x, y):
        x_pos = lax.axis_index("row") * tiles_x + x
        y_pos = lax.axis_index("col") * tiles_y + y
        first = (x_pos * (tiles_y * cols) + y_pos) * cells
        row = jnp.broadcast_to(cells_ref[...], (ports, ports))
        diagonal = lax.broadcasted_iota(jnp.int32, (ports, ports), 0) == lax.broadcasted_iota(
            jnp.int32, (ports, ports), 1
        )
        column = jnp.sum(jnp.where(diagonal, row, 0), axis=1, keepdims=True)
        lane = lax.broadcasted_iota(jnp.int32, tile, 1)
        return jnp.where(column - first == lane, port_strength, 0.0).astype(f32)

    def source_tile(flat_ref, cells_ref, phase, x, y):
        value = flat_ref[phase, pl.ds(x * tiles_y + y, ports, stride=tiles), :]
        if phase == 0:
            pos = lax.axis_index("layer")
            end = jnp.logical_or(pos == 0, pos == layers - 1)
            value = value + jnp.where(end, port_map(cells_ref, x, y), 0.0)
        return value.astype(bf16)

    def corner_kernel(forward_hbm, adjoint_hbm, cells_hbm, flat_ref, cells_ref, corner_ref, raw_ref, sems):
        copies = [
            pltpu.make_async_copy(src, dst, sems.at[i])
            for i, (src, dst) in enumerate(
                ((forward_hbm, raw_ref.at[0]), (adjoint_hbm, raw_ref.at[1]), (cells_hbm, cells_ref))
            )
        ]
        for copy in copies:
            copy.start()
        for copy in copies:
            copy.wait()
        edge = Side(far, "col", tiles_y).edge
        for phase in range(2):
            flat_ref[phase] = raw_ref[first_sweep() ^ phase].astype(f32).reshape(ports * tiles, cells)
            for h, pairing in enumerate(row_pairs):
                row = Side(pairing, "row", tiles_x).edge
                if phase == 0:
                    corner_ref[h] = source_tile(flat_ref, cells_ref, phase, row, edge)

    def rims_kernel(flat_ref, cells_ref, *refs):
        take = taker(refs)
        rim_refs, column_ref = take(halos), take()
        edge = Side(far, "col", tiles_y).edge
        for x in range(tiles_x):
            column_ref[x] = source_tile(flat_ref, cells_ref, 0, x, edge)
        for h, pairing in enumerate(row_pairs):
            row = Side(pairing, "row", tiles_x).edge
            for y in range(tiles_y):
                rim_refs[h][y] = source_tile(flat_ref, cells_ref, 0, row, y)

    raw_shape = (ports, tiles, cells)
    flat, port_row, corner = call(
        corner_kernel,
        [((2, ports * tiles, cells), f32), ((1, ports), jnp.int32), ((SPARE * halos, *tile), bf16)],
        sources.reshape(raw_shape),
        adjoint_sources.reshape(raw_shape),
        port_cells.reshape(1, ports),
        far_args=3,
        scratch=[pltpu.VMEM((2, *raw_shape), bf16), pltpu.SemaphoreType.DMA((3,))],
    )
    corner = to_core(corner)
    outward = call(rims_kernel, [((tiles_y, *tile), bf16)] * halos + [((tiles_x, *tile), bf16)], flat, port_row)

    def relay_kernel(phase, *refs):
        take = taker(refs)
        column_ref, corner_ref, out_refs = take(), take(), take(halos)
        inner = Side(far, "col", tiles_y).real

        @pl.when(inner)
        def _():
            for out_ref in out_refs:
                out_ref[:tiles_x] = column_ref[...]

        @pl.when(jnp.logical_not(inner))
        def _():
            for h, out_ref in enumerate(out_refs):
                out_ref[0] = corner_ref[h]

    def exchange(step, corner, outward, field=None):
        rims, column = outward[:halos], outward[halos]
        arrived = [] if field is None else [to_layer(step, same)(field)]
        arrived += [to_layer(step, other_row(pairing))(rim) for rim, pairing in zip(rims, row_pairs)]
        kernel = functools.partial(relay_kernel, 0 if step is None else None)
        carried = call(kernel, [(column.shape, bf16)] * halos, column, corner)
        return arrived + [to_layer(step, other_chip(pairing))(part) for part, pairing in zip(carried, row_pairs)]

    source_beside = exchange(None, corner, outward)

    def setup_kernel(pattern_hbm, coupling_hbm, group_hbm, blocks_hbm, *refs):
        take = taker(refs)
        flat_ref, cells_ref, source_ref, front_ref, kappa_ref, member_ref = (take() for _ in range(6))
        late_refs, late_column_ref, late_corner_refs = take(halos), take(), take(halos)
        pattern_ref, coupling_ref, group_ref, blocks_ref, sems, block_sems = (take() for _ in range(6))
        scalars = [
            pltpu.make_async_copy(src, dst, sems.at[i])
            for i, (src, dst) in enumerate(
                ((pattern_hbm, pattern_ref), (coupling_hbm, coupling_ref), (group_hbm, group_ref))
            )
        ]
        loads = [
            pltpu.make_async_copy(blocks_hbm.at[t], blocks_ref.at[t], block_sems.at[t]) for t in range(tiles)
        ]
        for copy in scalars + loads:
            copy.start()
        for phase in range(2):
            for x in range(tiles_x):
                for y in range(tiles_y):
                    source_ref[phase, x * tiles_y + y] = source_tile(flat_ref, cells_ref, phase, x, y)
        for pairing, rim_ref in zip(row_pairs, late_refs):
            row = Side(pairing, "row", tiles_x).edge
            rim_ref[...] = source_ref[1, pl.ds(row * tiles_y, tiles_y)]
        edge = Side(far, "col", tiles_y).edge
        for x in range(tiles_x):
            late_column_ref[x] = source_ref[1, x * tiles_y + edge]
        for pairing, corner_ref in zip(row_pairs, late_corner_refs):
            corner_ref[0] = source_ref[1, Side(pairing, "row", tiles_x).edge * tiles_y + edge]
        for copy in scalars:
            copy.wait()
        for t in range(tiles):
            loads[t].wait()
            for offset in range(OFFSETS):
                present = pattern_ref[t // tiles_y, t % tiles_y, offset] > 0
                front_ref[t, offset] = jnp.where(present, blocks_ref[t, offset], jnp.zeros((cells, cells), bf16))
        pos = lax.axis_index("layer")
        own = coupling_ref[group_ref[pos]]
        following = coupling_ref[group_ref[jnp.minimum(pos + 1, layers - 1)]]
        early = first_sweep() == 0
        kappa_ref[0] = jnp.full((8, cells), jnp.where(early, own, following), f32)
        kappa_ref[1] = jnp.full((8, cells), jnp.where(early, following, own), f32)
        for g in range(groups):
            for l in range(layers):
                member_ref[g, l] = jnp.full((tiles, cells), jnp.where(group_ref[l] == g, 1.0, 0.0), f32)

    source, front, kappa, member, *late = call(
        setup_kernel,
        [
            ((2, tiles, *tile), bf16),
            ((tiles, OFFSETS, cells, cells), bf16),
            ((2, 8, cells), f32),
            ((groups, layers, tiles, cells), f32),
        ]
        + [((tiles_y, *tile), bf16)] * halos
        + [((max(tiles_x, tiles_y), *tile), bf16)] * (halos + 1),
        pattern[0],
        coupling,
        layer_group,
        blocks.reshape(tiles, OFFSETS, cells, cells),
        flat,
        port_row,
        far_args=4,
        scratch=[
            pltpu.SMEM(pattern.shape[1:], jnp.int32),
            pltpu.SMEM(coupling.shape, f32),
            pltpu.SMEM(layer_group.shape, jnp.int32),
            pltpu.VMEM((tiles, OFFSETS, cells, cells), bf16),
            pltpu.SemaphoreType.DMA((3,)),
            pltpu.SemaphoreType.DMA((tiles,)),
        ],
    )

    late_rims, late_sides = late[:halos], late[halos:]

    def inner_only(beside, pairing):
        def target(l, r, c):
            return (l, *beside(r, c)) if abs(far(c, cols) - c) == 1 else (l, pairing(r, rows), c)

        return target

    late_corners = [
        permuted(part, inner_only(lambda r, c, pairing=pairing: (pairing(r, rows), far(c, cols)), pairing))
        for part, pairing in zip(late_sides[1:], row_pairs)
    ]
    late_sides = [permuted(late_sides[0], inner_only(lambda r, c: (r, far(c, cols)), near))] + late_corners
    late_rims = [to_layer(None, other_row(pairing))(part) for part, pairing in zip(late_rims, row_pairs)]
    turn = layers // 2

    def waves(phase, kappa_ref):
        def wave(base, field=None, real=None):
            if field is not None:
                factor = kappa_ref[phase, 0:1, :]
                base = (base.astype(f32) + factor * field.astype(f32)).astype(bf16)
            return base if real is None else jnp.where(real, base, jnp.zeros_like(base))

        return wave

    def row_real():
        return [Side(pairing, "row", tiles_x).real for pairing in row_pairs]

    def step_inputs(step, take):
        source_ref, kappa_ref, rim_refs = take(), take(), take(halos)
        column_refs = take(halos if step < turn else 0 if step == turn else 1)
        if step == 0:
            return source_ref, kappa_ref, rim_refs, column_refs, None, [None] * halos, column_refs
        return source_ref, kappa_ref, rim_refs, column_refs, take(), take(halos), take(halos)

    def core_kernel(step, *refs):
        take = taker(refs)
        phase = int(step >= layers // 2)
        source_ref, kappa_ref, rim_refs, column_refs, field_ref, field_rims, carried = step_inputs(step, take)
        core_ref = take()
        for h in range(halos):
            core_ref[ext + h] = carried[h][0]

        @pl.when(is_active(step))
        def _():
            wave = waves(phase, kappa_ref)
            real = row_real()
            edge = Side(near, "col", tiles_y).edge
            for x in range(tiles_x):
                t = x * tiles_y + edge
                core_ref[x] = wave(source_ref[phase, t], None if step == 0 else field_ref[t])
            for h in range(halos):
                core_ref[tiles_x + h] = wave(
                    rim_refs[h][edge], None if step == 0 else field_rims[h][edge], real[h]
                )

    def product(lhs, rhs):
        return jnp.dot(lhs, rhs, preferred_element_type=f32)

    def column_products(across, front_ref, halo_ref):
        totals = []
        for x in range(tiles_x):
            t = x * tiles_y + across.edge
            reach = [a for a in (-1, 0, 1) if 0 <= x + a < tiles_x]
            lhs = jnp.concatenate([halo_ref[x + a] for a in reach], axis=1)
            rhs = jnp.concatenate([front_ref[t, 3 * (a + 1) + 1 + across.step] for a in reach], axis=0)
            totals.append(product(lhs, rhs))
        return totals

    def corner_product(across, pairing, front_ref, corner):
        side = Side(pairing, "row", tiles_x)
        t = side.edge * tiles_y + across.edge
        return t, product(corner, front_ref[t, 3 * (side.step + 1) + 1 + across.step])

    def early_tiles(step):
        edge = Side(far, "col", tiles_y).edge
        inside = [(x, y) for x in range(tiles_x) for y in range(1, tiles_y - 1)]
        if step == turn:
            return inside
        if halos > 1:
            return inside + [(x, edge) for x in range(1, tiles_x - 1)]
        low = jnp.where(Side(near, "row", tiles_x).edge == 0, 1, 0)
        return inside + [(low + i, edge) for i in range(tiles_x - 1)]

    def late_tiles(step):
        beside, beyond = (Side(pairing, "col", tiles_y).edge for pairing in (near, far))
        corners = [(Side(pairing, "row", tiles_x).edge, beyond) for pairing in row_pairs]
        if step == turn:
            corners = [(x, beyond) for x in range(tiles_x)]
        return [(x, beside) for x in range(tiles_x)] + corners

    def add_parts(some, one_ref, other_ref, part_ref):
        for x, y in some:
            t = x * tiles_y + y
            both = one_ref[t].astype(f32) * other_ref[t].astype(f32)
            part_ref[pl.ds(t, 1), :] = jnp.sum(both, axis=0, keepdims=True) * intersection_scale

    def inner_kernel(step, *refs):
        take = taker(refs)
        phase, last = int(step >= layers // 2), step == layers - 1
        source_ref, kappa_ref, rim_refs, column_refs, field_ref, field_rims, carried = step_inputs(step, take)
        take()
        front_ref, earlier = take(), take(layers - 1 if last else 0)
        sum_ref, out_ref, rest, wave_ref, side_ref = take(), take(), take(1 if last else halos + 1), take(), take()

        @pl.when(is_active(step))
        def _():
            wave = waves(phase, kappa_ref)
            real = row_real()
            for x in range(tiles_x):
                for y in range(tiles_y):
                    t = x * tiles_y + y
                    wave_ref[x, y] = wave(source_ref[phase, t], None if step == 0 else field_ref[t])
                if step != turn:
                    side_ref[x] = wave(column_refs[0][x], None if step == 0 else carried[0][x])
            for h in range(halos):
                for y in range(tiles_y):
                    wave_ref[tiles_x + h, y] = wave(
                        rim_refs[h][y], None if step == 0 else field_rims[h][y], real[h]
                    )
            for y in range(tiles_y):
                low, high = max(y - 1, 0), min(y + 1, tiles_y - 1)
                width = high - low + 1
                first = low - y + 1
                beside = [
                    jnp.concatenate([wave_ref[x, j] for j in range(low, high + 1)], axis=1) for x in range(ext)
                ]
                for x in range(tiles_x):
                    reach = [a for a in (-1, 0, 1) if 0 <= x + a < tiles_x]
                    lhs = jnp.concatenate([beside[x + a] for a in reach], axis=1)
                    rhs = jnp.concatenate(
                        [
                            front_ref[x * tiles_y + y, 3 * (a + 1) + first : 3 * (a + 1) + first + width].reshape(
                                width * cells, cells
                            )
                            for a in reach
                        ],
                        axis=0,
                    )
                    sum_ref[x * tiles_y + y] = product(lhs, rhs)
                for h, pairing in enumerate(row_pairs):
                    side = Side(pairing, "row", tiles_x)
                    t = side.edge * tiles_y + y
                    rhs = front_ref[t, pl.ds(3 * (side.step + 1) + first, width)].reshape(width * cells, cells)
                    sum_ref[t] += product(beside[tiles_x + h], rhs)
            across = Side(far, "col", tiles_y)

            def beyond():
                for x, total in enumerate(column_products(across, front_ref, side_ref)):
                    sum_ref[x * tiles_y + across.edge] += total

            if step != turn:
                across.when(beyond)
            some = early_tiles(step)
            for x, y in some:
                out_ref[x * tiles_y + y] = sum_ref[x * tiles_y + y].astype(bf16)
            if last:
                add_parts(some, earlier[0], out_ref, rest[0])
            else:
                for x in range(tiles_x):
                    rest[halos][x] = out_ref[x * tiles_y + across.edge]
                for h, pairing in enumerate(row_pairs):
                    row = Side(pairing, "row", tiles_x).edge
                    rest[h][1 : tiles_y - 1] = out_ref[pl.ds(row * tiles_y + 1, tiles_y - 2)]

        if last:
            pos = lax.axis_index("layer")
            first = jnp.minimum(pos, layers - 1 - pos)
            whole = [(x, y) for x in range(tiles_x) for y in range(tiles_y)]
            for k in range(1, layers // 2):

                @pl.when(first == k)
                def _(k=k):
                    add_parts(whole, earlier[k], earlier[layers - 1 - k], rest[0])

    def add_far_corners(step, sum_ref, front_ref, kappa_ref, core_ref, bases, column_ref=None, carried_ref=None):
        wave = waves(int(step >= turn), kappa_ref)
        real = row_real()
        beyond = Side(far, "col", tiles_y)

        def corners():
            totals = []
            for h, pairing in enumerate(row_pairs):
                corner = wave(bases[h], None if step == 0 else core_ref[ext + h], real[h])
                totals.append(corner_product(beyond, pairing, front_ref, corner))
            if step == turn:
                side = [wave(column_ref[x], carried_ref[x]) for x in range(tiles_x)]
                products = column_products(beyond, front_ref, side)
                totals += [(x * tiles_y + beyond.edge, total) for x, total in enumerate(products)]
            for t, total in totals:
                sum_ref[t] += total

        beyond.when(corners)

    def corner_bases(step, refs):
        return [refs[0][ext + h] for h in range(halos)] if step < turn else [ref[0] for ref in refs]

    def corner_front_kernel(step, *refs):
        take = taker(refs)
        take()
        front_ref, kappa_ref, core_ref = take(), take(), take()
        bases = corner_bases(step, take(1 if step < turn else halos))
        extra = take(2 if step == turn else 0)
        if step == 1:
            take(halos + 1)
        sum_ref, corner_ref = take(), take()

        @pl.when(is_active(step))
        def _():
            add_far_corners(step, sum_ref, front_ref, kappa_ref, core_ref, bases, *extra)
            edge = Side(far, "col", tiles_y).edge
            for h, pairing in enumerate(row_pairs):
                row = Side(pairing, "row", tiles_x).edge
                corner_ref[h] = sum_ref[row * tiles_y + edge].astype(bf16)

    def outer_kernel(step, *refs):
        take = taker(refs)
        last = step == layers - 1
        take(2 + (1 if last else halos + 1))
        front_ref, core_ref = take(), take()
        if last and layers == 4:
            take()
        kappa_ref, bases = (take(), corner_bases(step, take(halos))) if last else (None, None)
        first_ref = take() if last else None
        sum_ref, field_ref, rest = take(), take(), take(1 if last else halos + 1)

        @pl.when(is_active(step))
        def _():
            if last:
                add_far_corners(step, sum_ref, front_ref, kappa_ref, core_ref, bases)
            across, beyond = Side(near, "col", tiles_y), Side(far, "col", tiles_y)
            totals = column_products(across, front_ref, core_ref)
            corners = [
                corner_product(across, pairing, front_ref, core_ref[tiles_x + h])[1]
                for h, pairing in enumerate(row_pairs)
            ]
            edges = [Side(pairing, "row", tiles_x).edge for pairing in row_pairs]
            for x, total in enumerate(totals):
                t = x * tiles_y + across.edge
                total = sum_ref[t] + total
                for edge, corner in zip(edges, corners):
                    total = total + jnp.where(edge == x, corner, 0.0)
                field_ref[t] = total.astype(bf16)
            some = late_tiles(step)
            for x, y in some[tiles_x:]:
                field_ref[x * tiles_y + y] = sum_ref[x * tiles_y + y].astype(bf16)
            if last:
                add_parts(some, first_ref, field_ref, rest[0])
            else:
                for x, y in some[tiles_x:]:
                    rest[halos][x] = field_ref[x * tiles_y + y]
                for h, pairing in enumerate(row_pairs):
                    row = Side(pairing, "row", tiles_x).edge
                    for edge in (across.edge, beyond.edge):
                        rest[h][edge] = field_ref[row * tiles_y + edge]

    def middle_kernel(one_ref, other_ref, part_ref):
        pos = lax.axis_index("layer")

        @pl.when(jnp.logical_and(pos > 0, pos < layers - 1))
        def _():
            whole = [(x, y) for x in range(tiles_x) for y in range(tiles_y)]
            add_parts(whole, one_ref, other_ref, part_ref)

    fields, field_arrived = [], []
    for step in range(layers):
        last = step == layers - 1
        halo = source_beside if step < turn else [*late_rims, *(late_sides[:1] if step > turn else [])]
        inputs = [source, kappa, *halo, *field_arrived]
        (core_out,) = call(
            functools.partial(core_kernel, step),
            [((ext + halos, *tile), bf16)],
            *inputs,
        )
        core = to_core(core_out)
        summed, *partial_out = call(
            functools.partial(inner_kernel, step),
            [((tiles, *tile), f32), ((tiles, *tile), bf16)]
            + ([((tiles, cells), f32)] if last else [((tiles_y, *tile), bf16)] * halos + [((tiles_x, *tile), bf16)]),
            *inputs,
            core_out,
            front,
            *(fields if last else []),
            scratch=[pltpu.VMEM((ext, tiles_y, *tile), bf16), pltpu.VMEM((tiles_x, *tile), bf16)],
        )
        if step == 0:
            base = [core]
        elif step == turn:
            base = late_sides[1:]
        if not last:
            summed, corner = call(
                functools.partial(corner_front_kernel, step),
                [((tiles, *tile), f32), ((SPARE * halos, *tile), bf16)],
                summed,
                front,
                kappa,
                core,
                *base,
                *([late_sides[0], field_arrived[1 + halos]] if step == turn else []),
                *([*late_rims, late_sides[0]] if step == 1 else []),
                aliases={0: 0},
            )
            corner = to_core(corner)
        _, field, *extra = call(
            functools.partial(outer_kernel, step),
            [(part.shape, part.dtype) for part in (summed, *partial_out)],
            summed,
            *partial_out,
            front,
            core,
            *([beside] if last and layers == 4 else []),
            *([kappa, *base, fields[0]] if last else []),
            aliases={i: i for i in range(1 + len(partial_out))},
        )
        fields.append(field)
        if not last:
            field_arrived = exchange(step, corner, extra, field)
        if layers == 4 and step == 2:
            (beside,) = call(middle_kernel, [((BESIDE * tiles, cells), f32)], fields[1], fields[2])
            beside = permuted(beside, lambda l, r, c: (l ^ 1, r, c))
    intersection = extra[0]

    def fields_kernel(*refs):
        field_refs, (forward_ref, adjoint_ref, flat_ref) = refs[:layers], refs[layers:]
        pos = lax.axis_index("layer")
        for out_ref, active in ((forward_ref, lambda s: s), (adjoint_ref, lambda s: layers - 1 - s)):
            for step in range(layers):

                @pl.when(pos == active(step))
                def _(step=step):
                    for t in range(tiles):
                        flat_ref[pl.ds(t, ports, stride=tiles), :] = field_refs[step][t].astype(f32)

            out_ref[...] = flat_ref[...].reshape(ports, tiles, cells).astype(bf16)

    forward, adjoint = call(
        fields_kernel,
        [((ports, tiles, cells), bf16)] * 2,
        *fields,
        scratch=[pltpu.VMEM((ports * tiles, cells), f32)],
    )

    if layers == 4:

        def pair_kernel(own_ref, beside_ref, out_ref):
            out_ref[0] = own_ref[...]
            out_ref[1] = beside_ref[:tiles]

        def gather(parts, member_ref, out_ref):
            for g in range(groups):
                total = jnp.zeros((tiles, cells), f32)
                for layer, part in parts:
                    total = total + member_ref[g, layer] * part
                for x in range(tiles_x):
                    out_ref[g, x] = total[x * tiles_y : (x + 1) * tiles_y]

        def ends_kernel(own_ref, beside_ref, across_ref, member_ref, out_ref):
            pos = lax.axis_index("layer")
            end = layers - 1 - pos
            parts = [(pos, own_ref[...]), (pos ^ 1, beside_ref[:tiles]), (end, across_ref[0]), (end ^ 1, across_ref[1])]
            gather(parts, member_ref, out_ref)

        def middle_layers_kernel(ends_ref, own_ref, across_ref, next_ref, other_ref, member_ref, out_ref, sum_ref, sem):
            pos = lax.axis_index("layer")

            @pl.when(jnp.logical_and(pos > 0, pos < layers - 1))
            def _():
                parts = [
                    (pos, own_ref[...]),
                    (layers - 1 - pos, across_ref[0]),
                    (pos ^ 1, next_ref[...]),
                    (pos ^ 2, other_ref[...]),
                ]
                gather(parts, member_ref, sum_ref)
                copy = pltpu.make_async_copy(sum_ref, out_ref, sem)
                copy.start()
                copy.wait()

        out_shape = (groups, tiles_x, tiles_y, cells)
        (both,) = call(pair_kernel, [((2, tiles, cells), f32)], intersection, beside)
        across = permuted(both, lambda l, r, c: (layers - 1 - l, r, c))
        following = permuted(intersection, lambda l, r, c: (l ^ 1, r, c))
        other = permuted(intersection, lambda l, r, c: (l ^ 2, r, c))
        (gradient,) = call(ends_kernel, [(out_shape, f32)], intersection, beside, across, member)
        hbm = pl.BlockSpec(memory_space=pltpu.HBM)
        gradient = pl.pallas_call(
            middle_layers_kernel,
            out_shape=jax.ShapeDtypeStruct(out_shape, f32),
            in_specs=[hbm] + [VM] * 5,
            out_specs=hbm,
            scratch_shapes=[pltpu.VMEM(out_shape, f32), pltpu.SemaphoreType.DMA],
            input_output_aliases={0: 0},
            compiler_params=pltpu.CompilerParams(vmem_limit_bytes=VMEM_BYTES),
        )(
            pltpu.with_memory_space_constraint(gradient, pltpu.HBM),
            intersection,
            across,
            following,
            other,
            member,
        )
    else:
        selected = lax.dynamic_index_in_dim(member, lax.axis_index("layer"), 1, keepdims=False)
        gradient = lax.psum(selected * intersection[None], "layer").reshape(groups, tiles_x, tiles_y, cells)
    shape = (1, ports, tiles_x, tiles_y, cells)
    return (forward.reshape(shape), adjoint.reshape(shape), gradient)


def solution(mesh):
    placed = (
        P("layer", None, "row", "col", None),
        P("layer", None, "row", "col", None),
        P("layer", "row", "col", None, None, None),
        P("layer", "row", "col", None),
        P(),
        P(),
        P(),
    )
    return jax.shard_map(
        local,
        mesh=mesh,
        in_specs=placed,
        out_specs=(
            P("layer", None, "row", "col", None),
            P("layer", None, "row", "col", None),
            P(None, "row", "col", None),
        ),
        check_vma=False,
    )
```

```python
import functools

import jax
import jax.numpy as jnp
from jax import lax
from jax.experimental import pallas as pl
from jax.experimental.pallas import tpu as pltpu
from jax.sharding import PartitionSpec as P

port_strength = 4.0
intersection_scale = 0.125
AXES = ("layer", "row", "col")
OFFSETS = 9
VMEM_BYTES = 24 * 1024 * 1024
BESIDE = 16
SPARE = 2

VM = pl.BlockSpec(memory_space=pltpu.VMEM)


def call(kernel, outs, *args, far_args=0, scratch=(), aliases=None):
    args = [pltpu.with_memory_space_constraint(a, pltpu.HBM) for a in args[:far_args]] + list(args[far_args:])
    return pl.pallas_call(
        kernel,
        out_shape=[jax.ShapeDtypeStruct(shape, dtype) for shape, dtype in outs],
        in_specs=[pl.BlockSpec(memory_space=pltpu.HBM)] * far_args + [VM] * (len(args) - far_args),
        out_specs=[VM] * len(outs),
        scratch_shapes=list(scratch),
        input_output_aliases=aliases or {},
        compiler_params=pltpu.CompilerParams(vmem_limit_bytes=VMEM_BYTES),
    )(*args)


def near(i, n):
    return i ^ 1


def far(i, n):
    return (((i + 1) ^ 1) - 1) % n


def pairings(n):
    return [near] if n == 2 else [near, far]


class Side:
    def __init__(self, pairing, axis, tiles):
        pos, count = lax.axis_index(axis), lax.axis_size(axis)
        even = lax.rem(pos, 2) == 0
        after = even if pairing is near else jnp.logical_not(even)
        self.step = jnp.where(after, 1, -1)
        self.edge = jnp.where(after, tiles - 1, 0)
        self.real = None
        if pairing is far:
            self.real = jnp.logical_not(
                jnp.logical_or(jnp.logical_and(after, pos == count - 1), jnp.logical_and(jnp.logical_not(after), pos == 0))
            )

    def when(self, body):
        if self.real is None:
            body()
        else:
            pl.when(self.real)(body)


def local(sources, adjoint_sources, blocks, pattern, coupling, layer_group, port_cells):
    ports, tiles_x, tiles_y, cells = sources.shape[1:]
    tiles = tiles_x * tiles_y
    groups = coupling.shape[0]
    layers, rows, cols = (lax.axis_size(axis) for axis in AXES)
    if cols != 4 or layers % 2 or layers < 4 or rows % 2:
        raise ValueError("unsupported mesh")
    row_pairs = pairings(rows)
    halos = len(row_pairs)
    ext = tiles_x + halos
    bf16, f32 = jnp.bfloat16, jnp.float32
    tile = (ports, cells)

    def permuted(array, target):
        pairs = []
        for l in range(layers):
            for r in range(rows):
                for c in range(cols):
                    a, b, d = target(l, r, c)
                    pairs.append(((l * rows + r) * cols + c, (a * rows + b) * cols + d))
        return lax.ppermute(array, AXES, pairs)

    def to_core(array):
        return permuted(array, lambda l, r, c: (l, r, near(c, cols)))

    def to_layer(step, beside):
        def target(l, r, c):
            if step is None:
                return l, *beside(r, c)
            a = (near if step % 2 == 0 else far)(l, layers)
            return (a, *beside(r, c)) if abs(a - l) == 1 else (l, r, near(c, cols))

        return lambda array: permuted(array, target)

    def same(r, c):
        return r, c

    def other_row(pairing):
        return lambda r, c: (pairing(r, rows), c)

    def other_chip(pairing):
        def beside(r, c):
            d = far(c, cols)
            return (r if abs(d - c) == 1 else pairing(r, rows)), d

        return beside

    def is_active(step):
        pos = lax.axis_index("layer")
        return jnp.logical_or(pos == step, pos == layers - 1 - step)

    def taker(refs):
        refs = list(refs)

        def take(count=None):
            taken = refs[: 1 if count is None else count]
            del refs[: len(taken)]
            return taken[0] if count is None else taken

        return take

    def first_sweep():
        return jnp.where(lax.axis_index("layer") < layers // 2, 0, 1)

    def port_map(cells_ref, x, y):
        x_pos = lax.axis_index("row") * tiles_x + x
        y_pos = lax.axis_index("col") * tiles_y + y
        first = (x_pos * (tiles_y * cols) + y_pos) * cells
        row = jnp.broadcast_to(cells_ref[...], (ports, ports))
        diagonal = lax.broadcasted_iota(jnp.int32, (ports, ports), 0) == lax.broadcasted_iota(
            jnp.int32, (ports, ports), 1
        )
        column = jnp.sum(jnp.where(diagonal, row, 0), axis=1, keepdims=True)
        lane = lax.broadcasted_iota(jnp.int32, tile, 1)
        return jnp.where(column - first == lane, port_strength, 0.0).astype(f32)

    def source_tile(flat_ref, cells_ref, phase, x, y):
        value = flat_ref[phase, pl.ds(x * tiles_y + y, ports, stride=tiles), :]
        if phase == 0:
            pos = lax.axis_index("layer")
            end = jnp.logical_or(pos == 0, pos == layers - 1)
            value = value + jnp.where(end, port_map(cells_ref, x, y), 0.0)
        return value.astype(bf16)

    def corner_kernel(forward_hbm, adjoint_hbm, cells_hbm, flat_ref, cells_ref, corner_ref, raw_ref, sems):
        copies = [
            pltpu.make_async_copy(src, dst, sems.at[i])
            for i, (src, dst) in enumerate(
                ((forward_hbm, raw_ref.at[0]), (adjoint_hbm, raw_ref.at[1]), (cells_hbm, cells_ref))
            )
        ]
        for copy in copies:
            copy.start()
        for copy in copies:
            copy.wait()
        edge = Side(far, "col", tiles_y).edge
        for phase in range(2):
            flat_ref[phase] = raw_ref[first_sweep() ^ phase].astype(f32).reshape(ports * tiles, cells)
            for h, pairing in enumerate(row_pairs):
                row = Side(pairing, "row", tiles_x).edge
                if phase == 0:
                    corner_ref[h] = source_tile(flat_ref, cells_ref, phase, row, edge)

    def rims_kernel(flat_ref, cells_ref, *refs):
        take = taker(refs)
        rim_refs, column_ref = take(halos), take()
        edge = Side(far, "col", tiles_y).edge
        for x in range(tiles_x):
            column_ref[x] = source_tile(flat_ref, cells_ref, 0, x, edge)
        for h, pairing in enumerate(row_pairs):
            row = Side(pairing, "row", tiles_x).edge
            for y in range(tiles_y):
                rim_refs[h][y] = source_tile(flat_ref, cells_ref, 0, row, y)

    raw_shape = (ports, tiles, cells)
    flat, port_row, corner = call(
        corner_kernel,
        [((2, ports * tiles, cells), f32), ((1, ports), jnp.int32), ((SPARE * halos, *tile), bf16)],
        sources.reshape(raw_shape),
        adjoint_sources.reshape(raw_shape),
        port_cells.reshape(1, ports),
        far_args=3,
        scratch=[pltpu.VMEM((2, *raw_shape), bf16), pltpu.SemaphoreType.DMA((3,))],
    )
    corner = to_core(corner)
    outward = call(rims_kernel, [((tiles_y, *tile), bf16)] * halos + [((tiles_x, *tile), bf16)], flat, port_row)

    def relay_kernel(phase, *refs):
        take = taker(refs)
        column_ref, corner_ref, out_refs = take(), take(), take(halos)
        inner = Side(far, "col", tiles_y).real

        @pl.when(inner)
        def _():
            for out_ref in out_refs:
                out_ref[:tiles_x] = column_ref[...]

        @pl.when(jnp.logical_not(inner))
        def _():
            for h, out_ref in enumerate(out_refs):
                out_ref[0] = corner_ref[h]

    def exchange(step, corner, outward, field=None):
        rims, column = outward[:halos], outward[halos]
        arrived = [] if field is None else [to_layer(step, same)(field)]
        arrived += [to_layer(step, other_row(pairing))(rim) for rim, pairing in zip(rims, row_pairs)]
        kernel = functools.partial(relay_kernel, 0 if step is None else None)
        carried = call(kernel, [(column.shape, bf16)] * halos, column, corner)
        return arrived + [to_layer(step, other_chip(pairing))(part) for part, pairing in zip(carried, row_pairs)]

    source_beside = exchange(None, corner, outward)

    def setup_kernel(pattern_hbm, coupling_hbm, group_hbm, blocks_hbm, *refs):
        take = taker(refs)
        flat_ref, cells_ref, source_ref, front_ref, kappa_ref, member_ref = (take() for _ in range(6))
        late_refs, late_column_ref, late_corner_refs = take(halos), take(), take(halos)
        pattern_ref, coupling_ref, group_ref, blocks_ref, sems, block_sems = (take() for _ in range(6))
        scalars = [
            pltpu.make_async_copy(src, dst, sems.at[i])
            for i, (src, dst) in enumerate(
                ((pattern_hbm, pattern_ref), (coupling_hbm, coupling_ref), (group_hbm, group_ref))
            )
        ]
        loads = [
            pltpu.make_async_copy(blocks_hbm.at[t], blocks_ref.at[t], block_sems.at[t]) for t in range(tiles)
        ]
        for copy in scalars + loads:
            copy.start()
        for phase in range(2):
            for x in range(tiles_x):
                for y in range(tiles_y):
                    source_ref[phase, x * tiles_y + y] = source_tile(flat_ref, cells_ref, phase, x, y)
        for pairing, rim_ref in zip(row_pairs, late_refs):
            row = Side(pairing, "row", tiles_x).edge
            rim_ref[...] = source_ref[1, pl.ds(row * tiles_y, tiles_y)]
        edge = Side(far, "col", tiles_y).edge
        for x in range(tiles_x):
            late_column_ref[x] = source_ref[1, x * tiles_y + edge]
        for pairing, corner_ref in zip(row_pairs, late_corner_refs):
            corner_ref[0] = source_ref[1, Side(pairing, "row", tiles_x).edge * tiles_y + edge]
        for copy in scalars:
            copy.wait()
        for t in range(tiles):
            loads[t].wait()
            for offset in range(OFFSETS):
                present = pattern_ref[t // tiles_y, t % tiles_y, offset] > 0
                front_ref[t, offset] = jnp.where(present, blocks_ref[t, offset], jnp.zeros((cells, cells), bf16))
        pos = lax.axis_index("layer")
        own = coupling_ref[group_ref[pos]]
        following = coupling_ref[group_ref[jnp.minimum(pos + 1, layers - 1)]]
        early = first_sweep() == 0
        kappa_ref[0] = jnp.full((8, cells), jnp.where(early, own, following), f32)
        kappa_ref[1] = jnp.full((8, cells), jnp.where(early, following, own), f32)
        for g in range(groups):
            for l in range(layers):
                member_ref[g, l] = jnp.full((tiles, cells), jnp.where(group_ref[l] == g, 1.0, 0.0), f32)

    source, front, kappa, member, *late = call(
        setup_kernel,
        [
            ((2, tiles, *tile), bf16),
            ((tiles, OFFSETS, cells, cells), bf16),
            ((2, 8, cells), f32),
            ((groups, layers, tiles, cells), f32),
        ]
        + [((tiles_y, *tile), bf16)] * halos
        + [((max(tiles_x, tiles_y), *tile), bf16)] * (halos + 1),
        pattern[0],
        coupling,
        layer_group,
        blocks.reshape(tiles, OFFSETS, cells, cells),
        flat,
        port_row,
        far_args=4,
        scratch=[
            pltpu.SMEM(pattern.shape[1:], jnp.int32),
            pltpu.SMEM(coupling.shape, f32),
            pltpu.SMEM(layer_group.shape, jnp.int32),
            pltpu.VMEM((tiles, OFFSETS, cells, cells), bf16),
            pltpu.SemaphoreType.DMA((3,)),
            pltpu.SemaphoreType.DMA((tiles,)),
        ],
    )

    late_rims, late_sides = late[:halos], late[halos:]

    def inner_only(beside, pairing):
        def target(l, r, c):
            return (l, *beside(r, c)) if abs(far(c, cols) - c) == 1 else (l, pairing(r, rows), c)

        return target

    late_corners = [
        permuted(part, inner_only(lambda r, c, pairing=pairing: (pairing(r, rows), far(c, cols)), pairing))
        for part, pairing in zip(late_sides[1:], row_pairs)
    ]
    late_sides = [permuted(late_sides[0], inner_only(lambda r, c: (r, far(c, cols)), near))] + late_corners
    late_rims = [to_layer(None, other_row(pairing))(part) for part, pairing in zip(late_rims, row_pairs)]
    turn = layers // 2

    def waves(phase, kappa_ref):
        def wave(base, field=None, real=None):
            if field is not None:
                factor = kappa_ref[phase, 0:1, :]
                base = (base.astype(f32) + factor * field.astype(f32)).astype(bf16)
            return base if real is None else jnp.where(real, base, jnp.zeros_like(base))

        return wave

    def row_real():
        return [Side(pairing, "row", tiles_x).real for pairing in row_pairs]

    def step_inputs(step, take):
        source_ref, kappa_ref, rim_refs = take(), take(), take(halos)
        column_refs = take(halos if step < turn else 0 if step == turn else 1)
        if step == 0:
            return source_ref, kappa_ref, rim_refs, column_refs, None, [None] * halos, column_refs
        return source_ref, kappa_ref, rim_refs, column_refs, take(), take(halos), take(halos)

    def core_kernel(step, *refs):
        take = taker(refs)
        phase = int(step >= layers // 2)
        source_ref, kappa_ref, rim_refs, column_refs, field_ref, field_rims, carried = step_inputs(step, take)
        core_ref = take()
        for h in range(halos):
            core_ref[ext + h] = carried[h][0]

        @pl.when(is_active(step))
        def _():
            wave = waves(phase, kappa_ref)
            real = row_real()
            edge = Side(near, "col", tiles_y).edge
            for x in range(tiles_x):
                t = x * tiles_y + edge
                core_ref[x] = wave(source_ref[phase, t], None if step == 0 else field_ref[t])
            for h in range(halos):
                core_ref[tiles_x + h] = wave(
                    rim_refs[h][edge], None if step == 0 else field_rims[h][edge], real[h]
                )

    def product(lhs, rhs):
        return jnp.dot(lhs, rhs, preferred_element_type=f32)

    def column_products(across, front_ref, halo_ref):
        totals = []
        for x in range(tiles_x):
            t = x * tiles_y + across.edge
            reach = [a for a in (-1, 0, 1) if 0 <= x + a < tiles_x]
            lhs = jnp.concatenate([halo_ref[x + a] for a in reach], axis=1)
            rhs = jnp.concatenate([front_ref[t, 3 * (a + 1) + 1 + across.step] for a in reach], axis=0)
            totals.append(product(lhs, rhs))
        return totals

    def corner_product(across, pairing, front_ref, corner):
        side = Side(pairing, "row", tiles_x)
        t = side.edge * tiles_y + across.edge
        return t, product(corner, front_ref[t, 3 * (side.step + 1) + 1 + across.step])

    def early_tiles(step):
        edge = Side(far, "col", tiles_y).edge
        inside = [(x, y) for x in range(tiles_x) for y in range(1, tiles_y - 1)]
        if step == turn:
            return inside
        if halos > 1:
            return inside + [(x, edge) for x in range(1, tiles_x - 1)]
        low = jnp.where(Side(near, "row", tiles_x).edge == 0, 1, 0)
        return inside + [(low + i, edge) for i in range(tiles_x - 1)]

    def late_tiles(step):
        beside, beyond = (Side(pairing, "col", tiles_y).edge for pairing in (near, far))
        corners = [(Side(pairing, "row", tiles_x).edge, beyond) for pairing in row_pairs]
        if step == turn:
            corners = [(x, beyond) for x in range(tiles_x)]
        return [(x, beside) for x in range(tiles_x)] + corners

    def add_parts(some, one_ref, other_ref, part_ref):
        for x, y in some:
            t = x * tiles_y + y
            both = one_ref[t].astype(f32) * other_ref[t].astype(f32)
            part_ref[pl.ds(t, 1), :] = jnp.sum(both, axis=0, keepdims=True) * intersection_scale

    def inner_kernel(step, *refs):
        take = taker(refs)
        phase, last = int(step >= layers // 2), step == layers - 1
        source_ref, kappa_ref, rim_refs, column_refs, field_ref, field_rims, carried = step_inputs(step, take)
        take()
        front_ref, earlier = take(), take(layers - 1 if last else 0)
        sum_ref, out_ref, rest, wave_ref, side_ref = take(), take(), take(1 if last else halos + 1), take(), take()

        @pl.when(is_active(step))
        def _():
            wave = waves(phase, kappa_ref)
            real = row_real()
            for x in range(tiles_x):
                for y in range(tiles_y):
                    t = x * tiles_y + y
                    wave_ref[x, y] = wave(source_ref[phase, t], None if step == 0 else field_ref[t])
                if step != turn:
                    side_ref[x] = wave(column_refs[0][x], None if step == 0 else carried[0][x])
            for h in range(halos):
                for y in range(tiles_y):
                    wave_ref[tiles_x + h, y] = wave(
                        rim_refs[h][y], None if step == 0 else field_rims[h][y], real[h]
                    )
            for y in range(tiles_y):
                low, high = max(y - 1, 0), min(y + 1, tiles_y - 1)
                width = high - low + 1
                first = low - y + 1
                beside = [
                    jnp.concatenate([wave_ref[x, j] for j in range(low, high + 1)], axis=1) for x in range(ext)
                ]
                for x in range(tiles_x):
                    reach = [a for a in (-1, 0, 1) if 0 <= x + a < tiles_x]
                    lhs = jnp.concatenate([beside[x + a] for a in reach], axis=1)
                    rhs = jnp.concatenate(
                        [
                            front_ref[x * tiles_y + y, 3 * (a + 1) + first : 3 * (a + 1) + first + width].reshape(
                                width * cells, cells
                            )
                            for a in reach
                        ],
                        axis=0,
                    )
                    sum_ref[x * tiles_y + y] = product(lhs, rhs)
                for h, pairing in enumerate(row_pairs):
                    side = Side(pairing, "row", tiles_x)
                    t = side.edge * tiles_y + y
                    rhs = front_ref[t, pl.ds(3 * (side.step + 1) + first, width)].reshape(width * cells, cells)
                    sum_ref[t] += product(beside[tiles_x + h], rhs)
            across = Side(far, "col", tiles_y)

            def beyond():
                for x, total in enumerate(column_products(across, front_ref, side_ref)):
                    sum_ref[x * tiles_y + across.edge] += total

            if step != turn:
                across.when(beyond)
            some = early_tiles(step)
            for x, y in some:
                out_ref[x * tiles_y + y] = sum_ref[x * tiles_y + y].astype(bf16)
            if last:
                add_parts(some, earlier[0], out_ref, rest[0])
            else:
                for x in range(tiles_x):
                    rest[halos][x] = out_ref[x * tiles_y + across.edge]
                for h, pairing in enumerate(row_pairs):
                    row = Side(pairing, "row", tiles_x).edge
                    rest[h][1 : tiles_y - 1] = out_ref[pl.ds(row * tiles_y + 1, tiles_y - 2)]

        if last:
            pos = lax.axis_index("layer")
            first = jnp.minimum(pos, layers - 1 - pos)
            whole = [(x, y) for x in range(tiles_x) for y in range(tiles_y)]
            for k in range(1, layers // 2):

                @pl.when(first == k)
                def _(k=k):
                    add_parts(whole, earlier[k], earlier[layers - 1 - k], rest[0])

    def add_far_corners(step, sum_ref, front_ref, kappa_ref, core_ref, bases, column_ref=None, carried_ref=None):
        wave = waves(int(step >= turn), kappa_ref)
        real = row_real()
        beyond = Side(far, "col", tiles_y)

        def corners():
            totals = []
            for h, pairing in enumerate(row_pairs):
                corner = wave(bases[h], None if step == 0 else core_ref[ext + h], real[h])
                totals.append(corner_product(beyond, pairing, front_ref, corner))
            if step == turn:
                side = [wave(column_ref[x], carried_ref[x]) for x in range(tiles_x)]
                products = column_products(beyond, front_ref, side)
                totals += [(x * tiles_y + beyond.edge, total) for x, total in enumerate(products)]
            for t, total in totals:
                sum_ref[t] += total

        beyond.when(corners)

    def corner_bases(step, refs):
        return [refs[0][ext + h] for h in range(halos)] if step < turn else [ref[0] for ref in refs]

    def corner_front_kernel(step, *refs):
        take = taker(refs)
        take()
        front_ref, kappa_ref, core_ref = take(), take(), take()
        bases = corner_bases(step, take(1 if step < turn else halos))
        extra = take(2 if step == turn else 0)
        if step == 1:
            take(halos + 1)
        sum_ref, corner_ref = take(), take()

        @pl.when(is_active(step))
        def _():
            add_far_corners(step, sum_ref, front_ref, kappa_ref, core_ref, bases, *extra)
            edge = Side(far, "col", tiles_y).edge
            for h, pairing in enumerate(row_pairs):
                row = Side(pairing, "row", tiles_x).edge
                corner_ref[h] = sum_ref[row * tiles_y + edge].astype(bf16)

    def outer_kernel(step, *refs):
        take = taker(refs)
        last = step == layers - 1
        take(2 + (1 if last else halos + 1))
        front_ref, core_ref = take(), take()
        if last and layers == 4:
            take()
        kappa_ref, bases = (take(), corner_bases(step, take(halos))) if last else (None, None)
        first_ref = take() if last else None
        sum_ref, field_ref, rest = take(), take(), take(1 if last else halos + 1)

        @pl.when(is_active(step))
        def _():
            if last:
                add_far_corners(step, sum_ref, front_ref, kappa_ref, core_ref, bases)
            across, beyond = Side(near, "col", tiles_y), Side(far, "col", tiles_y)
            corners = [
                corner_product(across, pairing, front_ref, core_ref[tiles_x + h])[1]
                for h, pairing in enumerate(row_pairs)
            ]
            totals = column_products(across, front_ref, core_ref)
            edges = [Side(pairing, "row", tiles_x).edge for pairing in row_pairs]
            for x, total in enumerate(totals):
                t = x * tiles_y + across.edge
                total = sum_ref[t] + total
                for edge, corner in zip(edges, corners):
                    total = total + jnp.where(edge == x, corner, 0.0)
                field_ref[t] = total.astype(bf16)
            some = late_tiles(step)
            for x, y in some[tiles_x:]:
                field_ref[x * tiles_y + y] = sum_ref[x * tiles_y + y].astype(bf16)
            if last:
                add_parts(some, first_ref, field_ref, rest[0])
            else:
                for x, y in some[tiles_x:]:
                    rest[halos][x] = field_ref[x * tiles_y + y]
                for h, pairing in enumerate(row_pairs):
                    row = Side(pairing, "row", tiles_x).edge
                    for edge in (across.edge, beyond.edge):
                        rest[h][edge] = field_ref[row * tiles_y + edge]

    def middle_kernel(one_ref, other_ref, part_ref):
        pos = lax.axis_index("layer")

        @pl.when(jnp.logical_and(pos > 0, pos < layers - 1))
        def _():
            whole = [(x, y) for x in range(tiles_x) for y in range(tiles_y)]
            add_parts(whole, one_ref, other_ref, part_ref)

    fields, field_arrived = [], []
    for step in range(layers):
        last = step == layers - 1
        halo = source_beside if step < turn else [*late_rims, *(late_sides[:1] if step > turn else [])]
        inputs = [source, kappa, *halo, *field_arrived]
        (core_out,) = call(
            functools.partial(core_kernel, step),
            [((ext + halos, *tile), bf16)],
            *inputs,
        )
        core = to_core(core_out)
        summed, *partial_out = call(
            functools.partial(inner_kernel, step),
            [((tiles, *tile), f32), ((tiles, *tile), bf16)]
            + ([((tiles, cells), f32)] if last else [((tiles_y, *tile), bf16)] * halos + [((tiles_x, *tile), bf16)]),
            *inputs,
            core_out,
            front,
            *(fields if last else []),
            scratch=[pltpu.VMEM((ext, tiles_y, *tile), bf16), pltpu.VMEM((tiles_x, *tile), bf16)],
        )
        if step == 0:
            base = [core]
        elif step == turn:
            base = late_sides[1:]
        if not last:
            summed, corner = call(
                functools.partial(corner_front_kernel, step),
                [((tiles, *tile), f32), ((SPARE * halos, *tile), bf16)],
                summed,
                front,
                kappa,
                core,
                *base,
                *([late_sides[0], field_arrived[1 + halos]] if step == turn else []),
                *([*late_rims, late_sides[0]] if step == 1 else []),
                aliases={0: 0},
            )
            corner = to_core(corner)
        _, field, *extra = call(
            functools.partial(outer_kernel, step),
            [(part.shape, part.dtype) for part in (summed, *partial_out)],
            summed,
            *partial_out,
            front,
            core,
            *([beside] if last and layers == 4 else []),
            *([kappa, *base, fields[0]] if last else []),
            aliases={i: i for i in range(1 + len(partial_out))},
        )
        fields.append(field)
        if not last:
            field_arrived = exchange(step, corner, extra, field)
        if layers == 4 and step == 2:
            (beside,) = call(middle_kernel, [((BESIDE * tiles, cells), f32)], fields[1], fields[2])
            beside = permuted(beside, lambda l, r, c: (l ^ 1, r, c))
    intersection = extra[0]

    def fields_kernel(*refs):
        field_refs, (forward_ref, adjoint_ref, flat_ref) = refs[:layers], refs[layers:]
        pos = lax.axis_index("layer")
        for out_ref, active in ((forward_ref, lambda s: s), (adjoint_ref, lambda s: layers - 1 - s)):
            for step in range(layers):

                @pl.when(pos == active(step))
                def _(step=step):
                    for t in range(tiles):
                        flat_ref[pl.ds(t, ports, stride=tiles), :] = field_refs[step][t].astype(f32)

            out_ref[...] = flat_ref[...].reshape(ports, tiles, cells).astype(bf16)

    forward, adjoint = call(
        fields_kernel,
        [((ports, tiles, cells), bf16)] * 2,
        *fields,
        scratch=[pltpu.VMEM((ports * tiles, cells), f32)],
    )

    if layers == 4:

        def pair_kernel(own_ref, beside_ref, out_ref):
            out_ref[0] = own_ref[...]
            out_ref[1] = beside_ref[:tiles]

        def gather(parts, member_ref, out_ref):
            for g in range(groups):
                total = jnp.zeros((tiles, cells), f32)
                for layer, part in parts:
                    total = total + member_ref[g, layer] * part
                for x in range(tiles_x):
                    out_ref[g, x] = total[x * tiles_y : (x + 1) * tiles_y]

        def ends_kernel(own_ref, beside_ref, across_ref, member_ref, out_ref):
            pos = lax.axis_index("layer")
            end = layers - 1 - pos
            parts = [(pos, own_ref[...]), (pos ^ 1, beside_ref[:tiles]), (end, across_ref[0]), (end ^ 1, across_ref[1])]
            gather(parts, member_ref, out_ref)

        def middle_layers_kernel(ends_ref, own_ref, across_ref, next_ref, other_ref, member_ref, out_ref, sum_ref, sem):
            pos = lax.axis_index("layer")

            @pl.when(jnp.logical_and(pos > 0, pos < layers - 1))
            def _():
                parts = [
                    (pos, own_ref[...]),
                    (layers - 1 - pos, across_ref[0]),
                    (pos ^ 1, next_ref[...]),
                    (pos ^ 2, other_ref[...]),
                ]
                gather(parts, member_ref, sum_ref)
                copy = pltpu.make_async_copy(sum_ref, out_ref, sem)
                copy.start()
                copy.wait()

        out_shape = (groups, tiles_x, tiles_y, cells)
        (both,) = call(pair_kernel, [((2, tiles, cells), f32)], intersection, beside)
        across = permuted(both, lambda l, r, c: (layers - 1 - l, r, c))
        following = permuted(intersection, lambda l, r, c: (l ^ 1, r, c))
        other = permuted(intersection, lambda l, r, c: (l ^ 2, r, c))
        (gradient,) = call(ends_kernel, [(out_shape, f32)], intersection, beside, across, member)
        hbm = pl.BlockSpec(memory_space=pltpu.HBM)
        gradient = pl.pallas_call(
            middle_layers_kernel,
            out_shape=jax.ShapeDtypeStruct(out_shape, f32),
            in_specs=[hbm] + [VM] * 5,
            out_specs=hbm,
            scratch_shapes=[pltpu.VMEM(out_shape, f32), pltpu.SemaphoreType.DMA],
            input_output_aliases={0: 0},
            compiler_params=pltpu.CompilerParams(vmem_limit_bytes=VMEM_BYTES),
        )(
            pltpu.with_memory_space_constraint(gradient, pltpu.HBM),
            intersection,
            across,
            following,
            other,
            member,
        )
    else:
        selected = lax.dynamic_index_in_dim(member, lax.axis_index("layer"), 1, keepdims=False)
        gradient = lax.psum(selected * intersection[None], "layer").reshape(groups, tiles_x, tiles_y, cells)
    shape = (1, ports, tiles_x, tiles_y, cells)
    return (forward.reshape(shape), adjoint.reshape(shape), gradient)


def solution(mesh):
    placed = (
        P("layer", None, "row", "col", None),
        P("layer", None, "row", "col", None),
        P("layer", "row", "col", None, None, None),
        P("layer", "row", "col", None),
        P(),
        P(),
        P(),
    )
    return jax.shard_map(
        local,
        mesh=mesh,
        in_specs=placed,
        out_specs=(
            P("layer", None, "row", "col", None),
            P("layer", None, "row", "col", None),
            P(None, "row", "col", None),
        ),
        check_vma=False,
    )
```
